32 devices in a mesh: wide: 8 (over y, x, core), narrow: 4 (over z).
Axes of the slice: x: 2, y: 2, z: 4, core: 2. Of those that a mesh axis runs over, the one named last changes fastest.
Arguments:
- latents: bfloat16 [9728, 768], P(('wide', 'narrow')), may hold values from 0 to 1, as said below
- actions: bfloat16 [9728, 3, 8], P(('wide', 'narrow')), may hold values from -1 to 1
- task_ids: int32 [9728], P(('wide', 'narrow')), may hold values from 0 to 79
- steps_left: int32 [9728], P(('wide', 'narrow')), may hold values from 1 to 3
- target_latents: bfloat16 [9728, 3, 768], P(('wide', 'narrow')), may hold values from 0 to 1, as said below
- reward_bins: int32 [9728, 3], P(('wide', 'narrow')), may hold values from 0 to 99
- reward_frac: float32 [9728, 3], P(('wide', 'narrow')), may hold values from 0 to 1
- value_bins: int32 [9728, 3], P(('wide', 'narrow')), may hold values from 0 to 99
- value_frac: float32 [9728, 3], P(('wide', 'narrow')), may hold values from 0 to 1
- first_weight: float32 [872, 3072], P('narrow'), may hold values from -0.21875 to 0.21875
- first_moment: float32 [872, 3072], P('narrow'), may hold values from -4.5776367e-05 to 4.5776367e-05
- first_second: float32 [872, 3072], P('narrow'), may hold values from 5.0370066e-11 to 2.0148026e-10
- dynamics_weight: float32 [1024, 768], P('narrow'), may hold values from -0.1875 to 0.1875
- dynamics_moment: float32 [1024, 768], P('narrow'), may hold values from -2.2888184e-05 to 2.2888184e-05
- dynamics_second: float32 [1024, 768], P('narrow'), may hold values from 1.25925164e-11 to 5.0370066e-11
- heads_weight: float32 [2, 1024, 101], P(None, 'narrow'), may hold values from -0.5 to 0.5
- heads_moment: float32 [2, 1024, 101], P(None, 'narrow'), may hold values from -7.6293945e-05 to 7.6293945e-05
- heads_second: float32 [2, 1024, 101], P(None, 'narrow'), may hold values from 1.4802631e-10 to 5.9210525e-10
- task_table: float32 [80, 96], P('narrow'), may hold values from -6 to 6
- table_moment: float32 [80, 96], P('narrow'), may hold values from -2.2888184e-05 to 2.2888184e-05
- table_second: float32 [80, 96], P('narrow'), may hold values from 1.6447368e-11 to 6.578947e-11
- vector_params: float32 [11520], P('narrow'), may hold values from -0.5 to 1.4, as said below
- vector_moment: float32 [11520], P('narrow'), may hold values from -6.1035156e-05 to 6.1035156e-05
- vector_second: float32 [11520], P('narrow'), may hold values from 1.0279605e-10 to 4.111842e-10
Outputs:
- latent_grad: float32 [9728, 768], P(('wide', 'narrow'))
- first_next: float32 [872, 3072], P('narrow')
- first_moment_next: float32 [872, 3072], P('narrow')
- first_second_next: float32 [872, 3072], P('narrow')
- dynamics_next: float32 [1024, 768], P('narrow')
- dynamics_moment_next: float32 [1024, 768], P('narrow')
- dynamics_second_next: float32 [1024, 768], P('narrow')
- heads_next: float32 [2, 1024, 101], P(None, 'narrow')
- heads_moment_next: float32 [2, 1024, 101], P(None, 'narrow')
- heads_second_next: float32 [2, 1024, 101], P(None, 'narrow')
- table_next: float32 [80, 96], P('narrow')
- table_moment_next: float32 [80, 96], P('narrow')
- table_second_next: float32 [80, 96], P('narrow')
- vector_next: float32 [11520], P('narrow')
- vector_moment_next: float32 [11520], P('narrow')
- vector_second_next: float32 [11520], P('narrow')
The draws below stay inside these ranges and needn't reach their ends.
Inputs may be any that keep to these rules, and one draw needn't show every extreme that they name: `latents`: within each group of 8 consecutive latent entries the values are positive and sum to one. `target_latents`: within each group of 8 consecutive latent entries the values are positive and sum to one. `vector_params`: gains lie in 0.6 to 1.4, biases and shifts in -0.5 to 0.5.
All inputs are finite; a program needn't handle non-finite values.
Results may differ from the reference program's by a relative error of at most 0.0015.
The reference program's roundings to bfloat16 on the way count: a program that leaves them out, or rounds other values in their place, can miss the bound.
Values may be sent and summed in bfloat16 or wider, within the bound.
A program may use at most 256 MiB of HBM per device.

```python
import math
import jax
import jax.numpy as jnp
import numpy as np
from jax import lax

LAT = 768
HID = 1024
BINS = 101
TEMB = 96
NTASK = 80
ACT = 8
HORIZON = 3
NQ = 1
STEP = 5
TOK_DEV = 304
TOKENS = 9728
IN_DIM = 872
BRANCHES = 3
HEADS = 2
VEC_LEN = 11520
N_NARROW = 4


def simplex_draw(key, shape, spread):
    logits = spread * jax.random.normal(key, shape + (8,), jnp.float32)
    return jax.nn.softmax(logits, -1).reshape(shape[:-1] + (shape[-1] * 8,))


def draw_latents(key, part):
    key = jax.random.fold_in(key, 3)
    return simplex_draw(key, (TOKENS, LAT // 8), 1.5).astype(jnp.bfloat16)


def draw_target_latents(key, part):
    key = jax.random.fold_in(key, 5)
    return simplex_draw(key, (TOKENS, HORIZON, LAT // 8), 1.5).astype(jnp.bfloat16)


def draw_vector_params(key, part):
    key = jax.random.fold_in(key, 7)
    first_key, second_key, third_key, fourth_key = jax.random.split(key, 4)
    hidden_base = jax.random.uniform(first_key, (BRANCHES, 3, HID), jnp.float32, -0.5, 0.5)
    hidden_gain = jax.random.uniform(second_key, (BRANCHES, 1, HID), jnp.float32, 0.6, 1.4)
    tail_base = jax.random.uniform(third_key, (3, LAT), jnp.float32, -0.5, 0.5)
    tail_gain = jax.random.uniform(fourth_key, (1, LAT), jnp.float32, 0.6, 1.4)
    hidden_all = jnp.concatenate([hidden_base[:, :1], hidden_gain, hidden_base[:, 2:]], 1)
    tail_all = jnp.concatenate([tail_base[:1], tail_gain, tail_base[2:]], 0)
    return jnp.concatenate([hidden_all.reshape(-1), tail_all.reshape(-1)])


def plant(drawn, rng, least, top_value):
    extent = drawn.shape
    spot = [jax.random.randint(jax.random.fold_in(rng, axis), (), 0, extent[axis]) for axis in range(len(extent))]
    drawn = drawn.at[tuple(spot)].set(least)
    longest = extent.index(max(extent))
    spot[longest] = (spot[longest] + 1) % extent[longest]
    return drawn.at[tuple(spot)].set(top_value)


def block_levels(key, dims, pieces, low, largest):
    def one(dim, shards_of):
        steps = jax.random.uniform(jax.random.fold_in(jax.random.fold_in(key, 6), dim), (shards_of,), jnp.float32, low / len(pieces), largest / len(pieces))
        return jnp.repeat(jnp.exp(steps), dims[dim] // shards_of).reshape((-1,) + (1,) * (len(dims) - dim - 1))

    factor_of = one(*pieces[0])
    for cut in pieces[1:]:
        factor_of = factor_of * one(*cut)
    return factor_of


def cumulative_ranks(number_of, slope):
    weights = [(1 << 20) // math.isqrt(grade ** slope) + 1 for grade in range(1, number_of + 1)]
    width = 1 + sum(weights) // (1 << 30)
    return np.cumsum(np.array([max(1, weight // width) for weight in weights]))


def ranked_ids(own_key, extent, number_of, lean):
    grid = cumulative_ranks(number_of, lean)
    ticket = jax.random.randint(jax.random.fold_in(own_key, 1), extent, 0, int(grid[number_of - 1]))
    standing = jnp.searchsorted(jnp.asarray(grid, jnp.int32), ticket, side="right")
    return jax.random.permutation(jax.random.fold_in(own_key, 2), number_of)[standing].astype(jnp.int32)


def noise(own_key, shape, scale, bound, cuts=(), held_as=jnp.bfloat16):
    entries = scale * jax.random.normal(own_key, shape, jnp.float32)
    if cuts:
        entries = entries * block_levels(own_key, shape, cuts, -0.22, 0.18)
    return jnp.clip(entries, -bound, bound).astype(held_as)


def setup_inputs(seed: int = 0) -> dict:
    seeds = jax.random.split(jax.random.key(seed), 25)
    latents = draw_latents(jax.random.fold_in(seeds[24], 71), 0)
    actions = jnp.clip(jax.random.uniform(seeds[1], (TOKENS, HORIZON, ACT), jnp.float32, -1.0, 1.0) * block_levels(seeds[1], (TOKENS, HORIZON, ACT), ((0, 32),), -0.4, 0.0), -1.0, 1.0).astype(jnp.bfloat16)
    task_ids = plant(ranked_ids(seeds[2], (TOKENS,), NTASK, 2), jax.random.fold_in(seeds[2], 3), 0, NTASK - 1).astype(jnp.int32)
    steps_left = plant(jax.random.randint(seeds[3], (TOKENS,), 1, HORIZON + 1), jax.random.fold_in(seeds[3], 1), 1, HORIZON).astype(jnp.int32)
    target_latents = draw_target_latents(jax.random.fold_in(seeds[24], 71), 0)
    reward_bins = plant(jax.random.randint(seeds[5], (TOKENS, HORIZON), 0, BINS - 1), jax.random.fold_in(seeds[5], 1), 0, (BINS - 1) - 1).astype(jnp.int32)
    reward_frac = jnp.clip(1.0 * jax.random.uniform(seeds[6], (TOKENS, HORIZON), jnp.float32) ** block_levels(seeds[6], (TOKENS, HORIZON), ((0, 32),), -0.2, 0.2), 0.0, 1.0)
    value_bins = plant(jax.random.randint(seeds[7], (TOKENS, HORIZON), 0, BINS - 1), jax.random.fold_in(seeds[7], 1), 0, (BINS - 1) - 1).astype(jnp.int32)
    value_frac = jnp.clip(1.0 * jax.random.uniform(seeds[8], (TOKENS, HORIZON), jnp.float32) ** block_levels(seeds[8], (TOKENS, HORIZON), ((0, 32),), -0.2, 0.2), 0.0, 1.0)
    first_weight = noise(seeds[9], (IN_DIM, BRANCHES * HID), IN_DIM ** -0.5, 0.21875, ((0, 4),), jnp.float32)
    first_moment = noise(seeds[10], (IN_DIM, BRANCHES * HID), (0.0007 / TOKENS ** 0.5), 4.57763671875e-05, ((0, 4),), jnp.float32)
    first_second = jnp.clip(jnp.exp(math.log(2.0148026302901911e-10) - 1.3862944 * jax.random.uniform(seeds[11], (IN_DIM, BRANCHES * HID), jnp.float32) ** block_levels(seeds[11], (IN_DIM, BRANCHES * HID), ((0, 4),), -0.2, 0.2)), 5.037006575725478e-11, 2.0148026302901911e-10)
    dynamics_weight = noise(seeds[12], (HID, LAT), HID ** -0.5, 0.1875, ((0, 4),), jnp.float32)
    dynamics_moment = noise(seeds[13], (HID, LAT), (0.00035 / TOKENS ** 0.5), 2.288818359375e-05, ((0, 4),), jnp.float32)
    dynamics_second = jnp.clip(jnp.exp(math.log(5.037006575725478e-11) - 1.3862944 * jax.random.uniform(seeds[14], (HID, LAT), jnp.float32) ** block_levels(seeds[14], (HID, LAT), ((0, 4),), -0.2, 0.2)), 1.2592516439313695e-11, 5.037006575725478e-11)
    heads_weight = noise(seeds[15], (HEADS, HID, BINS), (2.5 / HID ** 0.5), 0.5, ((1, 4),), jnp.float32)
    heads_moment = noise(seeds[16], (HEADS, HID, BINS), (0.0012 / TOKENS ** 0.5), 7.62939453125e-05, ((1, 4),), jnp.float32)
    heads_second = jnp.clip(jnp.exp(math.log(5.921052537161131e-10) - 1.3862944 * jax.random.uniform(seeds[17], (HEADS, HID, BINS), jnp.float32) ** block_levels(seeds[17], (HEADS, HID, BINS), ((1, 4),), -0.2, 0.2)), 1.4802631342902828e-10, 5.921052537161131e-10)
    task_table = noise(seeds[18], (NTASK, TEMB), 1.0, 6.0, ((0, 4),), jnp.float32)
    table_moment = noise(seeds[19], (NTASK, TEMB), (0.0004 / TOKENS ** 0.5), 2.288818359375e-05, ((0, 4),), jnp.float32)
    table_second = jnp.clip(jnp.exp(math.log(6.578947109314726e-11) - 1.3862944 * jax.random.uniform(seeds[20], (NTASK, TEMB), jnp.float32) ** block_levels(seeds[20], (NTASK, TEMB), ((0, 4),), -0.2, 0.2)), 1.6447367773286814e-11, 6.578947109314726e-11)
    vector_params = draw_vector_params(jax.random.fold_in(seeds[24], 71), 0)
    vector_moment = noise(seeds[22], (VEC_LEN,), (0.001 / TOKENS ** 0.5), 6.103515625e-05, ((0, 4),), jnp.float32)
    vector_second = jnp.clip(jnp.exp(math.log(4.111841978016173e-10) - 1.3862944 * jax.random.uniform(seeds[23], (VEC_LEN,), jnp.float32) ** block_levels(seeds[23], (VEC_LEN,), ((0, 4),), -0.2, 0.2)), 1.0279604945040433e-10, 4.111841978016173e-10)
    return dict(latents=latents, actions=actions, task_ids=task_ids, steps_left=steps_left, target_latents=target_latents, reward_bins=reward_bins, reward_frac=reward_frac, value_bins=value_bins, value_frac=value_frac, first_weight=first_weight, first_moment=first_moment, first_second=first_second, dynamics_weight=dynamics_weight, dynamics_moment=dynamics_moment, dynamics_second=dynamics_second, heads_weight=heads_weight, heads_moment=heads_moment, heads_second=heads_second, task_table=task_table, table_moment=table_moment, table_second=table_second, vector_params=vector_params, vector_moment=vector_moment, vector_second=vector_second)


@jax.custom_vjp
def low(v):
    return lax.optimization_barrier(v.astype(jnp.bfloat16)).astype(jnp.float32)

@jax.custom_vjp
def low_back(v):
    return v

def low_keep(v):
    return (low(v), None)

def low_pass(kept, grad):
    return (grad,)

def back_keep(v):
    return (v, None)

def back_low(kept, grad):
    return (low(grad),)
low.defvjp(low_keep, low_pass)
low_back.defvjp(back_keep, back_low)
norm_eps = 1e-05
adam_eps = 1e-08
moment_decay = 0.5
horizon_decay = 0.5
weight_decay = 0.01
matrix_rate = 0.03
vector_rate = 0.3
consistency_coef = 20.0
reward_coef = 0.1
value_coef = 0.1

def mish_value(values):
    return values * jnp.tanh(jax.nn.softplus(values))

def layer_norm(values, norm_gain, norm_shift):
    centre = values - lax.optimization_barrier(jnp.mean(values, -1, keepdims=True))
    return centre * lax.rsqrt(lax.optimization_barrier(jnp.mean(centre * centre, -1, keepdims=True)) + norm_eps) * norm_gain + norm_shift

def two_hot(bin_index, bin_frac):
    levels = jnp.arange(BINS, dtype=jnp.int32)
    lower_hot = (levels == bin_index[..., None]).astype(jnp.float32)
    upper_hot = (levels == bin_index[..., None] + 1).astype(jnp.float32)
    return (1.0 - bin_frac[..., None]) * lower_hot + bin_frac[..., None] * upper_hot

def block_loss(weights, first_latent, block_data):
    first_copy, dyn_copy, heads_copy, table_copy, vector_copy = tuple((low(member) for member in weights))
    actions, task_ids, steps_left, target_latents, reward_bins, reward_frac, value_bins, value_frac = block_data
    hidden = vector_copy[:3 * BRANCHES * HID].reshape(BRANCHES, 3, HID)
    tail_vec = vector_copy[3 * BRANCHES * HID:].reshape(3, LAT)
    task_rows = table_copy[task_ids]
    row_count = first_latent.shape[0]
    head_scale = jnp.array([reward_coef] + [value_coef / NQ] * NQ, dtype=jnp.float32)
    highest = lax.Precision.HIGHEST
    current = first_latent
    loss_sum = jnp.zeros((), jnp.float32)
    for unroll in range(HORIZON):
        inputs = jnp.concatenate([low(current), actions[:, unroll], task_rows], 1)
        pre_act = low_back(jnp.dot(inputs, first_copy, precision=highest)).reshape(row_count, BRANCHES, HID) + hidden[:, 0]
        active = low(mish_value(layer_norm(pre_act, hidden[:, 1], hidden[:, 2])))
        dyn_pre = low_back(jnp.dot(active[:, 0], dyn_copy, precision=highest)) + tail_vec[0]
        dyn_normed = layer_norm(dyn_pre, tail_vec[1], tail_vec[2])
        simplex = jax.nn.softmax(dyn_normed.reshape(row_count, LAT // 8, 8), -1).reshape(row_count, LAT)
        logits = low_back(jnp.einsum('bkh,khc->bkc', active[:, 1:], heads_copy, precision=highest))
        reward_hot = two_hot(reward_bins[:, unroll], reward_frac[:, unroll])[:, None]
        value_hot = jnp.broadcast_to(two_hot(value_bins[:, unroll], value_frac[:, unroll])[:, None], (row_count, NQ, BINS))
        targets = jnp.concatenate([reward_hot, value_hot], 1)
        cross_entropy = jax.nn.logsumexp(logits, -1) - lax.optimization_barrier(jnp.sum(targets * logits, -1))
        latent_gap = simplex - target_latents[:, unroll]
        row_weight = jnp.where(steps_left > unroll, horizon_decay ** unroll, 0.0) / (HORIZON * TOKENS)
        loss_sum = loss_sum + jnp.sum(row_weight * (consistency_coef * lax.optimization_barrier(jnp.mean(latent_gap * latent_gap, -1)) + lax.optimization_barrier(jnp.sum(head_scale * cross_entropy, -1))))
        current = simplex
    return loss_sum

def adam_update(master, moment, second, gradient, step_rate):
    moment_new = moment_decay * moment + (1.0 - moment_decay) * gradient
    second_new = moment_decay * second + (1.0 - moment_decay) * gradient * gradient
    correct = 1.0 - moment_decay ** STEP
    normed_step = moment_new / correct / (jnp.sqrt(second_new / correct) + adam_eps)
    return (master - step_rate * (normed_step + weight_decay * master), moment_new, second_new)

def reference(latents, actions, task_ids, steps_left, target_latents, reward_bins, reward_frac, value_bins, value_frac, first_weight, first_moment, first_second, dynamics_weight, dynamics_moment, dynamics_second, heads_weight, heads_moment, heads_second, task_table, table_moment, table_second, vector_params, vector_moment, vector_second):
    block_rows = 2 * N_NARROW * TOK_DEV
    block_count = TOKENS // block_rows
    params = (first_weight, dynamics_weight, heads_weight, task_table, vector_params)

    def to_blocks(values):
        return values.reshape((block_count, block_rows) + values.shape[1:])
    rest = tuple((to_blocks(member) for member in (actions.astype(jnp.float32), task_ids, steps_left, target_latents.astype(jnp.float32), reward_bins, reward_frac, value_bins, value_frac)))
    inputs_all = (to_blocks(latents.astype(jnp.float32)), rest)

    def visit_block(grad_sum, block_data):
        start_latent, others = block_data
        block_value, pull_back = jax.vjp(lambda weights, latent: block_loss(weights, latent, others), params, start_latent)
        grad_params, grad_latent = pull_back(jnp.ones_like(block_value))
        return (jax.tree.map(jnp.add, grad_sum, grad_params), grad_latent)
    start_carry = jax.tree.map(jnp.zeros_like, params)
    grad_sum, grad_blocks = lax.scan(visit_block, start_carry, inputs_all)
    latent_grad = grad_blocks.reshape(TOKENS, LAT)
    grad_first, grad_dynamics, grad_heads, grad_table, grad_vectors = grad_sum
    first_new = adam_update(first_weight, first_moment, first_second, grad_first, matrix_rate)
    dynamics_new = adam_update(dynamics_weight, dynamics_moment, dynamics_second, grad_dynamics, matrix_rate)
    heads_new = adam_update(heads_weight, heads_moment, heads_second, grad_heads, matrix_rate)
    table_new = adam_update(task_table, table_moment, table_second, grad_table, vector_rate)
    vector_new = adam_update(vector_params, vector_moment, vector_second, grad_vectors, vector_rate)
    return (latent_grad, first_new[0], first_new[1], first_new[2], dynamics_new[0], dynamics_new[1], dynamics_new[2], heads_new[0], heads_new[1], heads_new[2], table_new[0], table_new[1], table_new[2], vector_new[0], vector_new[1], vector_new[2])
```

```python
import functools

import jax
import jax.numpy as jnp
from jax import lax
from jax.experimental import pallas as pl
from jax.experimental.pallas import tpu as pltpu
from jax.sharding import PartitionSpec as P

f32, bf16, i16, i32 = jnp.float32, jnp.bfloat16, jnp.int16, jnp.int32
MESH = pl.DeviceIdType.MESH

LAT = 768
HID = 1024
BINS = 101
TEMB = 96
ACTN = 8
HORIZON = 3
STEP = 5
NZ = 4
SHARD = 218
SENT = 224
BLK = 256
ROWS = 320
RB = 64
NB = ROWS // RB
ALL = HORIZON * ROWS
HALF = HID // 2
YHALF = LAT // 2
BOTT = 112
TASK_LANE = LAT + ACTN - 3 * SHARD
ACT_LANE = LAT - 3 * SHARD

norm_eps = 1e-05
adam_eps = 1e-08
moment_decay = 0.5
horizon_decay = 0.5
weight_decay = 0.01
matrix_rate = 0.03
vector_rate = 0.3
consistency_coef = 20.0
head_coef = 0.1

NN = (((1,), (0,)), ((), ()))
NT = (((1,), (1,)), ((), ()))
TN = (((0,), (0,)), ((), ()))


def dot(a, b, dims=NN):
    return lax.dot_general(a, b, dims, preferred_element_type=f32)


def lanes(n):
    return lax.broadcasted_iota(i32, (1, n), 1)


def block_rows(i, base=0):
    return pl.ds(pl.multiple_of(base + i * RB, RB), RB)


def encode(v, ref):
    rows = v.shape[0]
    top = jnp.max(jnp.abs(v), 0, keepdims=True)
    e = jnp.clip(jnp.ceil(jnp.log2(jnp.maximum(top, 1e-37))), -100.0, 120.0)
    ref[0:rows, :] = jnp.round(v * jnp.exp2(14.9 - e)).astype(i32).astype(i16)
    ref[rows : rows + 16, :] = jnp.broadcast_to(e, (16, v.shape[1])).astype(i32).astype(i16)


def decode(ref):
    rows = ref.shape[0] - 16
    e = ref[rows : rows + 16, :].astype(i32).astype(f32)[0:1, :]
    return ref[0:rows, :].astype(i32).astype(f32) * jnp.exp2(e - 14.9)


def pack_tiles(x):
    inside = lanes(BLK) < SHARD
    b0 = jnp.where(inside, x[:, 0:256], 0.0)
    b1 = jnp.where(inside, pltpu.roll(x[:, 128:512], 384 - 90, 1)[:, 0:256], 0.0)
    b2 = jnp.where(inside, pltpu.roll(x[:, 384:768], 384 - 52, 1)[:, 0:256], 0.0)
    b3 = jnp.where(lanes(128) < ACT_LANE, pltpu.roll(x[:, 640:768], 128 - 14, 1), 0.0)
    return b0, b1, b2, b3


def unpack_tiles(g):
    inside = lanes(BLK) < SHARD
    empty = jnp.zeros((g.shape[0], 128), f32)
    b0 = jnp.where(inside, g[:, 0:256], 0.0)
    b1 = pltpu.roll(jnp.concatenate([jnp.where(inside, g[:, 256:512], 0.0), empty], 1), 90, 1)
    b2 = pltpu.roll(jnp.concatenate([jnp.where(inside, g[:, 512:768], 0.0), empty], 1), 52, 1)
    b3 = pltpu.roll(jnp.where(lanes(128) < ACT_LANE, g[:, 768:896], 0.0), 14, 1)
    return jnp.concatenate(
        [
            b0[:, 0:128],
            b0[:, 128:256] + b1[:, 0:128],
            b1[:, 128:256],
            b1[:, 256:384] + b2[:, 0:128],
            b2[:, 128:256],
            b2[:, 256:384] + b3,
        ],
        1,
    )


def group_sums(x, ones):
    parts = []
    for j in range(0, x.shape[1], 256):
        v = x[:, j : j + 256]
        high = v.astype(bf16)
        low = (v - high.astype(f32)).astype(bf16)
        parts.append(dot(high, ones) + dot(low, ones))
    return jnp.concatenate(parts, 1)


def mish_parts(n):
    u = jnp.exp(jnp.minimum(n, 40.0))
    q = u * (u + 2.0)
    r = 1.0 / (q + 2.0)
    bent = q * r
    return bent, bent + (4.0 * n) * (u * (u + 1.0)) * (r * r)


def add_columns(acc, values):
    for k, v in enumerate(values):
        total = acc[8 * k : 8 * k + 8, :]
        for j in range(v.shape[0] // 8):
            total = total + v[8 * j : 8 * j + 8, :]
        acc[8 * k : 8 * k + 8, :] = total


def rcopy(src, dst, send_sem, recv_sem, device):
    return pltpu.make_async_remote_copy(
        src_ref=src, dst_ref=dst, send_sem=send_sem, recv_sem=recv_sem, device_id=device, device_id_type=MESH
    )


def step_kernel(wide, token_count, n_tok, n_task, lat, actT, ids, steps, tgt, rb, rf, vb, vf, fw, dw, hw, tab, vec,
                lg, qf, qy, qh, misc, **s):
    ups_n = wide.bit_length() - 4
    w, z = lax.axis_index("wide"), lax.axis_index("narrow")
    b0, b1, b2 = lax.rem(w, 2), lax.rem(lax.div(w, 2), 2), lax.rem(lax.div(w, 4), 2)
    pc, p1, p2 = (w + 1 - 2 * b0, z), (w + 2 - 4 * b1, z), (w + 4 - 8 * b2, z)
    zs = [(w, lax.rem(z + d, NZ)) for d in range(NZ)]
    from_z = [lax.rem(z + NZ - d, NZ) for d in range(NZ)]
    ups = []
    for u in range(ups_n):
        bit = 8 << u
        ups.append((w + bit - 2 * bit * lax.rem(lax.div(w, bit), 2), z))
    me = b0 * 4 + b1 * 2 + b2
    own = b1 * 2 + b2
    sends = []

    def launch(copy):
        copy.start()
        sends.append(copy)

    X, XT, XTp, U, AT, ATp, DU = s["X"], s["XT"], s["XTp"], s["U"], s["AT"], s["ATp"], s["DU"]
    WF, WD, HT, SM, VEC = s["WF"], s["WD"], s["HT"], s["SM"], s["VEC"]
    PRE, TU, TS, ACT = s["PRE"], s["TU"], s["TS"], s["ACT"]
    GP, GPp, GDL, GDLp = s["GP"], s["GPp"], s["GDL"], s["GDLp"]
    INV, DINV, SIDE, SD, ONES, VA, VT, GEMB = (
        s["INV"], s["DINV"], s["SIDE"], s["SD"], s["ONES"], s["VA"], s["VT"], s["GEMB"])

    STG = s["STG"]
    loads = []

    def load_first(part):
        return pltpu.make_async_copy(
            fw.at[:, pl.ds(HALF * part, HALF)], STG.at[part % 2], s["ls"].at[part % 2])

    loads.append(pltpu.make_async_copy(dw, DU.at[pl.ds(0, BLK)], s["ls"].at[3]))
    loads.append(pltpu.make_async_copy(lat, GDL.at[pl.ds(0, n_tok)], s["ls"].at[4]))
    for t in range(3):
        loads.append(pltpu.make_async_copy(tgt.at[t], s["TG"].at[t, pl.ds(0, n_tok)], s["ls"].at[5 + t]))
    load_first(0).start()
    load_first(1).start()
    for c in loads:
        c.start()
    for t in range(3):
        s["TG"][t, n_tok:ROWS, :] = jnp.zeros((ROWS - n_tok, LAT), bf16)
    GDL[n_tok:ROWS, :] = jnp.zeros((ROWS - n_tok, LAT), bf16)
    for q in range(NZ):
        WF[BLK * q + SENT : BLK * q + BLK, :] = jnp.zeros((BLK - SENT, 3 * HID), bf16)
    for ref in (HT, VA, VT, GEMB, s["DWH"], s["MS"]):
        ref[...] = jnp.zeros_like(ref)

    barrier = pltpu.get_barrier_semaphore()
    peers = [pc, p1, p2] + zs[1:] + ups
    for p in peers:
        pl.semaphore_signal(barrier, inc=1, device_id=p, device_id_type=MESH)

    def cast_first(br):
        for part in (2 * br, 2 * br + 1):
            load_first(part).wait()
            rows = jnp.concatenate([STG[part % 2].astype(bf16), jnp.zeros((SENT - SHARD, HALF), bf16)], 0)
            WF[pl.ds(pl.multiple_of(BLK * z, BLK), SENT), HALF * part : HALF * part + HALF] = rows
            if part < 4:
                load_first(part + 2).start()

    cast_first(0)
    loads[0].wait()
    WD[pl.ds(pl.multiple_of(BLK * z, BLK), BLK), :] = DU[0:BLK, :].astype(bf16)
    SM[z, 0:24, :] = vec[...].astype(bf16).astype(f32)
    SM[z, 24:56, :] = jnp.zeros((32, 128), f32)
    SM[z, 24 : 24 + n_task, 0:TEMB] = tab[...].astype(bf16).astype(f32)
    pl.semaphore_wait(barrier, len(peers))

    gs, gr = s["gs"], s["gr"]

    class Item:
        def __init__(self, index, view):
            self.i, self.view = index, view

        def _recv(self, d, kind, view):
            rcopy(view, view, gs.at[self.i, d - 1, kind], gr.at[self.i, d - 1, kind], pc).wait_recv()

        def _send(self, d, kind, view, device):
            launch(rcopy(view, view, gs.at[self.i, d - 1, kind], gr.at[self.i, d - 1, kind], device))

        def start(self):
            for d in (1, 3, 2):
                self._send(d, 0, self.view(z, me, 1, None), zs[d])

        def spread(self):
            for d in (1, 3, 2):
                mine = self.view(from_z[d], me, 1, None)
                self._recv(d, 0, mine)
                self._send(d, 1, mine, p1)
                self._send(d, 2, mine, p2)

        def forward(self):
            s1, s2 = me + 2 - 4 * b1, me + 1 - 2 * b2
            for d in (1, 3, 2):
                q = from_z[d]
                self._recv(d, 1, self.view(q, s1, 1, None))
                self._send(d, 3, self.view(q, s1, 1, 0), p2)
                self._recv(d, 2, self.view(q, s2, 1, None))
                self._send(d, 4, self.view(q, s2, 1, 1), p1)

        def cross(self):
            s12 = 4 * b0 + 3 - own
            for d in (1, 3, 2):
                q = from_z[d]
                self._recv(d, 3, self.view(q, s12, 1, 0))
                self._recv(d, 4, self.view(q, s12, 1, 1))
                self._send(d, 5, self.view(q, 4 * b0, 4, None), pc)

        def finish(self):
            for d in (1, 3, 2):
                self._recv(d, 5, self.view(from_z[d], 4 - 4 * b0, 4, None))

    def first_view(br):
        def view(q, at, n, half):
            lo, size = (0, SENT) if half is None else (BOTT * half, BOTT)
            return WF.at[pl.ds(pl.multiple_of(BLK * q + lo, 16), size), pl.ds(pl.multiple_of(HID * br + 128 * at, 128), 128 * n)]
        return view

    def dyn_view(q, at, n, half):
        lo, size = (0, 32 * n) if half is None else (16 * half, 16)
        return WD.at[pl.ds(pl.multiple_of(BLK * q + 32 * at + lo, 16), size)]

    def heads_view(q, at, n, half):
        cols = pl.ds(pl.multiple_of(BLK * q, BLK), BLK)
        rows = pl.ds(pl.multiple_of(16 * at, 16), 16 * n)
        if half is None:
            return HT.at[:, rows, cols]
        return HT.at[pl.ds(half, 1), rows, cols]

    gD, gY, gR, gV, gH = (
        Item(0, first_view(0)), Item(1, dyn_view), Item(2, first_view(1)), Item(3, first_view(2)), Item(4, heads_view))

    gD.start()
    for d in (1, 3, 2):
        launch(rcopy(SM.at[z], SM.at[z], s["ms"].at[d], s["mr"].at[d], zs[d]))
    gY.start()

    cast_first(1)
    cast_first(2)
    own_cols = pl.ds(pl.multiple_of(BLK * z, BLK), BLK)
    gD.spread()
    for k in range(2):
        PRE[0:128, 0:BLK] = jnp.zeros((128, BLK), f32)
        PRE[0:BINS, 0:BLK] = hw[:, k, :]
        HT[k, :, own_cols] = PRE[0:128, 0:BLK].astype(bf16)
    gY.spread()

    tile = lax.broadcasted_iota(i32, (256, 256), 0) // 8 == lax.broadcasted_iota(i32, (256, 256), 1) // 8
    ONES[...] = jnp.where(tile, 1.0, 0.0).astype(bf16)
    for t in range(3):
        st = s["ST"]
        st[...] = jnp.zeros_like(st)
        st[0:1, 0:n_tok] = steps[...].astype(f32)
        for k, ref in enumerate((rb, rf, vb, vf)):
            st[k + 1 : k + 2, 0:n_tok] = ref[t : t + 1, :].astype(f32)
        SIDE[t] = st[...].T[0:ROWS, :]
    idr = s["IDR"]
    idr[...] = jnp.full_like(idr, -1)
    idr[0:1, 0:n_tok] = ids[...]
    slot = lax.broadcasted_iota(i32, (128, 1), 0)
    task = jnp.where(slot % 32 < n_task, n_task * (slot // 32) + slot % 32, -2)
    PKT = s["PKT"]
    PKT[...] = jnp.where(idr[0:1, 0:ROWS] == task, 1.0, 0.0).astype(bf16)

    loads[1].wait()

    def pack_latents(i, c):
        rows = block_rows(i)
        b = pack_tiles(GDL[rows, :].astype(f32))
        X[rows, 0:896] = jnp.concatenate(b, 1).astype(bf16)
        return c

    lax.fori_loop(0, NB, pack_latents, 0)
    gD.forward()

    for d in (1, 3, 2):
        q = from_z[d]
        rcopy(SM.at[q], SM.at[q], s["ms"].at[d], s["mr"].at[d], pc).wait_recv()
    full = s["VFULL"]
    full[...] = jnp.zeros_like(full)
    for q, at in enumerate((0, 22, 45, 67)):
        full[at : at + 24, :] = full[at : at + 24, :] + SM[q, 0:24, :]
    for r in range(12):
        n, first = (8, 8 * r) if r < 9 else (6, 72 + 6 * (r - 9))
        for j in range(n):
            VEC[r : r + 1, 128 * j : 128 * j + 128] = full[first + j : first + j + 1, :]
    place = jnp.concatenate([SM[q, 24:56, :] for q in range(NZ)], 0)
    table = pltpu.roll(jnp.concatenate([place, jnp.zeros_like(place)], 1), TASK_LANE, 1).astype(bf16)
    AC = s["AC"]
    AC[...] = jnp.zeros_like(AC)
    act_to = jnp.where(
        lax.broadcasted_iota(i32, (16, BLK), 0) + ACT_LANE == lax.broadcasted_iota(i32, (16, BLK), 1), 1.0, 0.0
    ).astype(bf16)
    rows_of_task = dot(PKT[...], table, TN)
    for t in range(3):
        AC[0:ACTN, 0:n_tok] = actT[t].astype(f32)
        SD[t] = (rows_of_task + dot(AC[:, 0:ROWS].astype(bf16), act_to, TN)).astype(bf16)

    def side_block(t, dest):
        X[dest : dest + ROWS, 768:896] = (X[dest : dest + ROWS, 768:896].astype(f32) + SD[t, :, 0:128].astype(f32)).astype(bf16)
        X[dest : dest + ROWS, 896:1024] = SD[t, :, 128:256]

    gD.cross()
    gR.start()
    gY.forward()
    side_block(0, 0)
    gD.finish()

    def matmul(out, orows, n, width, left, right, dims=NN):
        def tile_step(j, c):
            cols = pl.ds(pl.multiple_of(j * width, width), width)
            out[orows, cols] = dot(left, right(cols), dims)
            return c
        lax.fori_loop(0, n // width, tile_step, 0)

    def first_forward(br, base):
        def tile_step(j, c):
            cols = pl.ds(pl.multiple_of(j * 512, 512), 512)
            from_cols = pl.ds(pl.multiple_of(HID * br + j * 512, 512), 512)
            PRE[:, cols] = dot(X[pl.ds(base, ROWS), :], WF[:, from_cols])
            return c
        lax.fori_loop(0, 2, tile_step, 0)

    def norm_mish(br, unit, inv, unit_base, slope):
        bias, gain, shift = (VEC[3 * br + k : 3 * br + k + 1, :] for k in range(3))

        def step(i, c):
            rows = block_rows(i)
            p = PRE[rows, :] + bias
            ce = p - jnp.mean(p, -1, keepdims=True)
            iv = lax.rsqrt(jnp.mean(ce * ce, -1, keepdims=True) + norm_eps)
            un = ce * iv
            n = un * gain + shift
            bent, sl = mish_parts(n)
            ACT[rows, :] = (n * bent).astype(bf16)
            if slope is not None:
                slope[rows, :] = sl
            unit[block_rows(i, unit_base), :] = un
            inv[block_rows(i, unit_base), :] = jnp.broadcast_to(iv, (RB, 128))
            return c
        lax.fori_loop(0, NB, step, 0)

    def dyn_forward(t):
        base = ROWS * t
        first_forward(0, base)
        norm_mish(0, U, INV, base, None)
        if t == 0:
            gY.finish()
        matmul(TU, slice(0, ROWS), LAT, 384, ACT[...], lambda cols: WD[:, cols])
        AT[:, base : base + ROWS] = ACT[...].T
        bias, gain, shift = (VEC[9 + k : 10 + k, 0:LAT] for k in range(3))

        def step(i, c):
            rows, at = block_rows(i), block_rows(i, base)
            p = TU[rows, 0:LAT] + bias
            ce = p - jnp.mean(p, -1, keepdims=True)
            iv = lax.rsqrt(jnp.mean(ce * ce, -1, keepdims=True) + norm_eps)
            un = ce * iv
            DU[at, :] = un
            DINV[at, :] = jnp.broadcast_to(iv, (RB, 128))
            if t < 2:
                e = jnp.exp(un * gain + shift)
                b = pack_tiles(e / group_sums(e, ONES[...]))
                X[block_rows(i, base + ROWS), 0:896] = jnp.concatenate(b, 1).astype(bf16)
            return c
        lax.fori_loop(0, NB, step, 0)
        if t < 2:
            side_block(t + 1, base + ROWS)

    gY.cross()
    gR.spread()
    dyn_forward(0)
    gV.start()
    gR.forward()
    gH.start()
    dyn_forward(1)
    gV.spread()
    gR.cross()
    gH.spread()
    dyn_forward(2)
    gV.forward()
    gH.forward()
    XT[...] = X[...].T
    xs, xr = s["xs"], s["xr"]
    launch(rcopy(XT, XTp, xs.at[0], xr.at[0], pc))
    launch(rcopy(AT, ATp, xs.at[1], xr.at[1], pc))
    gR.finish()
    gH.cross()
    gV.cross()
    gH.finish()

    def norm_backward(br, unit, inv, unit_base, slope, out_base):
        gain, shift = VEC[3 * br + 1 : 3 * br + 2, :], VEC[3 * br + 2 : 3 * br + 3, :]
        acc = VA.at[br]

        def step(i, c):
            rows, at = block_rows(i), block_rows(i, unit_base)
            un = unit[at, :]
            sl = mish_parts(un * gain + shift)[1] if slope is None else slope[rows, :]
            gn = PRE[rows, :] * sl
            h = gn * gain
            gp = (h - jnp.mean(h, -1, keepdims=True) - un * jnp.mean(h * un, -1, keepdims=True)) * inv[at, 0:1]
            GP[block_rows(i, out_base), HID * br : HID * br + HID] = gp.astype(bf16)
            add_columns(acc, (gp, gn * un, gn))
            return c
        lax.fori_loop(0, NB, step, 0)

    def head_step(k, t):
        base = ROWS * t
        first_forward(1 + k, base)
        norm_mish(1 + k, TU, s["HINV"], 0, TS)
        logits = dot(ACT[...], HT[k], NT)
        real = lanes(128) < BINS
        logits = jnp.where(real, logits, -1e30)
        e = jnp.exp(logits - jnp.max(logits, -1, keepdims=True))
        soft = e / jnp.sum(e, -1, keepdims=True)
        side = SIDE[t]
        at, frac = side[:, 1 + 2 * k : 2 + 2 * k], side[:, 2 + 2 * k : 3 + 2 * k]
        level = lanes(128).astype(f32)
        hot = jnp.where(level == at, 1.0 - frac, 0.0) + jnp.where(level == at + 1.0, frac, 0.0)
        weight = jnp.where(side[:, 0:1] > t, f32(horizon_decay**t), 0.0) / token_count
        gl = jnp.where(real, weight * head_coef * (soft - hot), 0.0).astype(bf16)
        s["DWH"][k] = s["DWH"][k] + dot(gl.astype(f32).T.astype(bf16), ACT[...])
        PRE[...] = dot(gl, HT[k])
        norm_backward(1 + k, TU, s["HINV"], 0, TS, base)

    def dyn_backward(t):
        base = ROWS * t
        gain, shift = VEC[10:11, 0:LAT], VEC[11:12, 0:LAT]
        scale = 2.0 * consistency_coef / LAT

        def step(i, c):
            rows, at = block_rows(i), block_rows(i, base)
            un = DU[at, :]
            e = jnp.exp(un * gain + shift)
            sx = e / group_sums(e, ONES[...])
            weight = jnp.where(SIDE[t, rows, 0:1] > t, f32(horizon_decay**t), 0.0) / token_count
            g = weight * scale * (sx - s["TG"][t, rows, :].astype(f32))
            if t < 2:
                g = g + unpack_tiles(PRE[rows, 0:896])
            gn = sx * (g - group_sums(g * sx, ONES[...]))
            h = gn * gain
            gp = (h - jnp.mean(h, -1, keepdims=True) - un * jnp.mean(h * un, -1, keepdims=True)) * DINV[at, 0:1]
            GDL[at, :] = gp.astype(bf16)
            add_columns(VT, (gp, gn * un, gn))
            return c
        lax.fori_loop(0, NB, step, 0)
        yc = pl.ds(pl.multiple_of(YHALF * (1 - b0), 128), YHALF)
        launch(rcopy(GDL.at[pl.ds(base, ROWS), yc], GDLp.at[pl.ds(base, ROWS)], xs.at[4 + t], xr.at[4 + t], pc))

        def tile_step(j, c):
            cols = pl.ds(pl.multiple_of(j * 512, 512), 512)
            PRE[:, cols] = dot(GDL[pl.ds(base, ROWS), :], WD[cols, :], NT)
            return c
        lax.fori_loop(0, 2, tile_step, 0)
        norm_backward(0, U, INV, base, None, base)
        gc = pl.ds(pl.multiple_of(HALF * (1 - b0), HALF), HALF)
        launch(rcopy(GP.at[pl.ds(base, ROWS), gc], GPp.at[0, pl.ds(base, ROWS)], xs.at[7 + t], xr.at[7 + t], pc))

    def inputs_backward(t):
        base = ROWS * t

        def tile_step(j, c):
            cols = pl.ds(pl.multiple_of(j * 512, 512), 512)
            PRE[:, cols] = dot(GP[pl.ds(base, ROWS), :], WF[cols, :], NT)
            return c
        lax.fori_loop(0, 2, tile_step, 0)
        GEMB[...] = GEMB[...] + PRE[:, 768:1024]

    rs_s, rs_r = s["ss"], s["sr"]

    class Stream:
        def __init__(self, index, grad, view, E, R, Q, half):
            self.i, self.grad, self.view, self.Q, self.half = index, grad, view, Q, half
            (self.E1, self.E2, self.E3), (self.R1, self.R2, self.R3) = E, R
            self.held = {}

        def _copy(self, at, src, dst, device):
            return rcopy(src, dst, rs_s.at[self.i, at], rs_r.at[self.i, at], device)

        def _send(self, at, src, dst, device):
            c = self._copy(at, src, dst, device)
            c.start()
            self.held[at] = c

        def _recv(self, at, dst):
            self._copy(at, dst, dst, pc).wait_recv()

        def release(self):
            for c in self.held.values():
                c.wait_send()
            self.held = {}

        def stage1(self, qs=(0, 1, 2, 3)):
            for q in qs:
                if q % 2 == 0:
                    pair, device = (2 - 2 * b1, 3 - 2 * b1), p1
                else:
                    pair, device = (1 - b2, 3 - b2), p2
                for j in range(2):
                    encode(self.grad[self.view(q, pair[j])], self.E1.at[q, j])
                self._send(q, self.E1.at[q], self.R1.at[q], device)

        def stage2(self, qs=(0, 1, 2, 3)):
            for q in qs:
                self._recv(q, self.R1.at[q])
                keep, other, device = (b2, own + 1 - 2 * b2, p2) if q % 2 == 0 else (b1, own + 2 - 4 * b1, p1)
                encode(self.grad[self.view(q, other)] + decode(self.R1.at[q, 1 - keep]), self.E2.at[q])
                self._send(4 + q, self.E2.at[q], self.R2.at[q], device)
                mine = self.view(q, own)
                self.grad[mine] = self.grad[mine] + decode(self.R1.at[q, keep])

        def stage3(self):
            for d in (2, 1, 3):
                q = zs[d][1]
                self._recv(4 + q, self.R2.at[q])
                encode(self.grad[self.view(q, own)] + decode(self.R2.at[q]), self.E3.at[d - 1])
                self._send(7 + d, self.E3.at[d - 1], self.R3.at[d - 1], zs[d])

        def stage4(self):
            self._recv(4 + z, self.R2.at[z])
            total = self.grad[self.view(z, own)] + decode(self.R2.at[z])
            for d in (1, 3, 2):
                self._recv(7 + d, self.R3.at[d - 1])
                total = total + decode(self.R3.at[d - 1])
            for u in range(ups_n):
                rows, cols = total.shape
                F, FR = s["F"].at[pl.ds(0, rows), pl.ds(0, cols)], s["FR%d" % self.i]
                F[...] = total
                self._send(16 + u, F, FR.at[u], ups[u])
                self._recv(16 + u, FR.at[u])
                self.held.pop(16 + u).wait_send()
                total = total + FR[u]
            encode(total, self.Q.at[me])
            self._send(11, self.Q.at[me], self.Q.at[me], p1)
            self._send(12, self.Q.at[me], self.Q.at[me], p2)

        def stage5(self):
            s1, s2 = me + 2 - 4 * b1, me + 1 - 2 * b2
            n = self.Q.shape[1]
            low, high = pl.ds(0, self.half), pl.ds(self.half, n - self.half)
            self._recv(11, self.Q.at[s1])
            self._send(13, self.Q.at[s1, low], self.Q.at[s1, low], p2)
            self._recv(12, self.Q.at[s2])
            self._send(14, self.Q.at[s2, high], self.Q.at[s2, high], p1)

        def stage6(self):
            s12 = 4 * b0 + 3 - own
            n = self.Q.shape[1]
            low, high = pl.ds(0, self.half), pl.ds(self.half, n - self.half)
            self._recv(13, self.Q.at[s12, low])
            self._recv(14, self.Q.at[s12, high])
            mine = self.Q.at[pl.ds(4 * b0, 4)]
            self._send(15, mine, mine, pc)

        def stage7(self, out, sem):
            self._recv(15, self.Q.at[pl.ds(4 - 4 * b0, 4)])
            c = pltpu.make_async_copy(self.Q, out, sem)
            c.start()
            return c

    def first_slice(q, at):
        return (pl.ds(pl.multiple_of(BLK * q, BLK), SENT), pl.ds(pl.multiple_of(128 * at, 128), 128))

    def y_slice(q, at):
        return (pl.ds(pl.multiple_of(BLK * q + 64 * at, 64), 64), slice(None))

    def h_slice(q, at):
        return (b0, pl.ds(pl.multiple_of(32 * at, 32), 32), pl.ds(pl.multiple_of(BLK * q, BLK), BLK))

    EF = (s["E1"], s["E2"], s["E3"])
    streams = []
    for i, name in enumerate("DRV"):
        streams.append(Stream(
            i, s["DWB"] if name == "V" else s["DWA"], first_slice, EF,
            tuple(s["R%d%s" % (k, name)] for k in (1, 2, 3)), s["QF"].at[i], 128))
    sD, sR, sV = streams
    sY = Stream(3, s["DWY"], y_slice, tuple(s["E%dY" % k] for k in (1, 2, 3)),
                tuple(s["R%dY" % k] for k in (1, 2, 3)), s["QY"], 48)
    sH = Stream(4, s["DWH"], h_slice, tuple(s["E%dH" % k] for k in (1, 2, 3)),
                tuple(s["R%dH" % k] for k in (1, 2, 3)), s["QH"], 32)

    def send_half(br):
        cols = pl.ds(pl.multiple_of(HID * br + HALF * (1 - b0), HALF), HALF)
        launch(rcopy(GP.at[:, cols], GPp.at[br], xs.at[1 + br], xr.at[1 + br], pc))

    def wait_x(at, dst):
        rcopy(dst, dst, xs.at[at], xr.at[at], pc).wait_recv()

    def weight_grad(out, n, left, right, left2, right2):
        def tile_step(j, c):
            cols = pl.ds(pl.multiple_of(j * n, n), n)
            out[:, cols] = dot(left[...], right(j)) + dot(left2[...], right2(cols))
            return c
        lax.fori_loop(0, out.shape[1] // n, tile_step, 0)

    def first_grad(br, out):
        weight_grad(
            out, 256, XT,
            lambda j: GP[:, pl.ds(pl.multiple_of(HID * br + HALF * b0 + 256 * j, 256), 256)],
            XTp, lambda cols: GPp[br, :, cols])

    for t in range(3):
        head_step(0, t)
    send_half(1)
    gV.finish()
    head_step(1, 0)
    wait_x(0, XTp)
    wait_x(2, GPp.at[1])
    first_grad(1, s["DWA"])
    sR.stage1()
    head_step(1, 1)
    head_step(1, 2)
    sR.stage2()
    send_half(2)
    launch(rcopy(s["DWH"].at[1 - b0], s["DWHp"], xs.at[10], xr.at[10], pc))
    for c in loads[2:]:
        c.wait()
    dyn_backward(2)
    wait_x(3, GPp.at[2])
    first_grad(2, s["DWB"])
    sR.stage3()
    sR.release()
    sV.stage1()
    inputs_backward(2)
    wait_x(10, s["DWHp"])
    s["DWH"][b0] = s["DWH"][b0] + s["DWHp"][...]
    sH.stage1()
    sR.stage4()
    dyn_backward(1)
    sV.stage2()
    sH.stage2()
    sR.stage5()
    inputs_backward(1)
    sV.stage3()
    sH.stage3()
    sR.stage6()
    sV.release()
    dyn_backward(0)
    wait_x(1, ATp)
    for t in range(3):
        wait_x(4 + t, GDLp.at[pl.ds(ROWS * t, ROWS)])

    def y_grad():
        weight_grad(
            s["DWY"], 128, AT,
            lambda j: GDL[:, pl.ds(pl.multiple_of(YHALF * b0 + 128 * j, 128), 128)],
            ATp, lambda cols: GDLp[:, cols])
    y_grad()
    sY.stage1()
    for t in range(3):
        wait_x(7 + t, GPp.at[0, pl.ds(ROWS * t, ROWS)])
    first_grad(0, s["DWA"])
    sD.stage1()
    inputs_backward(0)

    def write_latent(i, c):
        rows = block_rows(i)
        DU[rows, :] = unpack_tiles(PRE[rows, 0:896])
        return c
    lax.fori_loop(0, NB, write_latent, 0)
    lg_copy = pltpu.make_async_copy(DU.at[pl.ds(0, n_tok)], lg, s["ls"].at[8])
    lg_copy.start()
    ge = GEMB[...]
    g1 = ge.astype(bf16)
    g2 = (ge - g1.astype(f32)).astype(bf16)
    g3 = (ge - g1.astype(f32) - g2.astype(f32)).astype(bf16)
    pk = PKT[...]
    by_task = dot(pk, g1) + dot(pk, g2) + dot(pk, g3)
    M = s["MS"]
    M[128:256, :] = pltpu.roll(by_task, BLK - TASK_LANE, 1)[:, 0:128]
    for r in range(12):
        acc, n, first = (VA.at[r // 3], 8, 8 * r) if r < 9 else (VT, 6, 72 + 6 * (r - 9))
        k = r % 3
        row = jnp.sum(acc[8 * k : 8 * k + 8, :], 0, keepdims=True)
        for j in range(n):
            M[first + j : first + j + 1, :] = row[:, 128 * j : 128 * j + 128]

    vs, vr = s["vs"], s["vr"]

    def small(at, src, dst, device):
        return rcopy(src, dst, vs.at[at], vr.at[at], device)

    def rows_of(start, n):
        return pl.ds(pl.multiple_of(start, 32), n)

    halves = ((0, pc, b0, 128), (1, p1, b1, 64), (2, p2, b2, 32))

    def halve(step, start):
        at, device, bit, n = halves[step]
        launch(small(at, M.at[rows_of(start + n * (1 - bit), n)], s["MR%d" % step], device))

    def halved(step, start):
        at, device, bit, n = halves[step]
        small(at, s["MR%d" % step], s["MR%d" % step], device).wait_recv()
        mine = rows_of(start + n * bit, n)
        M[mine, :] = M[mine, :] + s["MR%d" % step][...]
        return start + n * bit

    halve(0, 0)
    sY.stage2()
    at = halved(0, 0)
    halve(1, at)
    sD.stage2((0, 1))
    at = halved(1, at)
    halve(2, at)
    sY.stage3()
    sD.stage2((2, 3))
    at = halved(2, at)
    MZ = s["MZ"]
    MZ[z] = M[rows_of(at, 32), :]
    for d in (2, 1, 3):
        launch(small(2 + d, MZ.at[z], MZ.at[z], zs[d]))
    sD.stage3()
    sH.stage4()
    sV.stage4()
    sY.stage4()
    for d in (1, 3, 2):
        small(2 + d, MZ.at[from_z[d]], MZ.at[from_z[d]], pc).wait_recv()
    total = (MZ[0] + MZ[1]) + (MZ[2] + MZ[3])
    for u in range(ups_n):
        s["MF"][u] = total
        launch(small(9 + u, s["MF"].at[u], s["MFR"].at[u], ups[u]))
        small(9 + u, s["MFR"].at[u], s["MFR"].at[u], ups[u]).wait_recv()
        total = total + s["MFR"][u]
    MO = s["MO"]
    MO[rows_of(at, 32), :] = total
    launch(small(6, MO.at[rows_of(at, 32)], MO.at[rows_of(at, 32)], p2))
    sD.stage4()
    sV.stage5()
    sH.stage5()
    sY.stage5()
    o = at + 32 - 64 * b2
    small(6, MO.at[rows_of(o, 32)], MO.at[rows_of(o, 32)], p2).wait_recv()
    at = at - 32 * b2
    launch(small(7, MO.at[rows_of(at, 64)], MO.at[rows_of(at, 64)], p1))
    sD.stage5()
    sV.stage6()
    sH.stage6()
    sY.stage6()
    o = at + 64 - 128 * b1
    small(7, MO.at[rows_of(o, 64)], MO.at[rows_of(o, 64)], p1).wait_recv()
    at = at - 64 * b1
    launch(small(8, MO.at[rows_of(at, 128)], MO.at[rows_of(at, 128)], pc))
    sD.stage6()
    outs = [lg_copy]
    outs.append(sR.stage7(qf.at[1], s["ls"].at[9]))
    outs.append(sV.stage7(qf.at[2], s["ls"].at[10]))
    outs.append(sH.stage7(qh, s["ls"].at[11]))
    outs.append(sY.stage7(qy, s["ls"].at[12]))
    o = at + 128 - 256 * b0
    small(8, MO.at[rows_of(o, 128)], MO.at[rows_of(o, 128)], pc).wait_recv()
    c = pltpu.make_async_copy(MO, misc, s["ls"].at[13])
    c.start()
    outs.append(c)
    outs.append(sD.stage7(qf.at[0], s["ls"].at[14]))
    for c in outs:
        c.wait()
    for st in (sD, sR, sV, sY, sH):
        st.release()
    for c in sends:
        c.wait_send()


def step_call(wide, token_count, n_task, lat, actT, ids, steps, tgt, rb, rf, vb, vf, fw, dw, hw, tab, vec):
    n_tok = lat.shape[0]
    ups_n = wide.bit_length() - 4
    V = pltpu.VMEM
    D = pltpu.SemaphoreType.DMA
    scratch = dict(
        WF=V((HID, 3 * HID), bf16), WD=V((HID, LAT), bf16), HT=V((2, 128, HID), bf16),
        SM=V((NZ, 56, 128), f32), VEC=V((16, HID), f32), VFULL=V((96, 128), f32),
        X=V((ALL, HID), bf16), XT=V((HID, ALL), bf16), XTp=V((HID, ALL), bf16),
        U=V((ALL, HID), f32), AT=V((HID, ALL), bf16), ATp=V((HID, ALL), bf16),
        DU=V((ALL, LAT), f32), TG=V((3, ROWS, LAT), bf16),
        PRE=V((ROWS, HID), f32), TU=V((ROWS, HID), f32), TS=V((ROWS, HID), f32), ACT=V((ROWS, HID), bf16),
        GP=V((ALL, 3 * HID), bf16), GPp=V((3, ALL, HALF), bf16), GDL=V((ALL, LAT), bf16), GDLp=V((ALL, YHALF), bf16),
        INV=V((ALL, 128), f32), HINV=V((ROWS, 128), f32), DINV=V((ALL, 128), f32),
        SIDE=V((3, ROWS, 16), f32), SD=V((3, ROWS, BLK), bf16), ONES=V((256, 256), bf16),
        VA=V((3, 24, HID), f32), VT=V((24, LAT), f32), GEMB=V((ROWS, BLK), f32),
        ST=V((16, 384), f32), IDR=V((8, 384), i32), PKT=V((128, ROWS), bf16), AC=V((16, 384), f32),
        DWA=V((HID, HALF), f32), DWB=V((HID, HALF), f32), DWY=V((HID, YHALF), f32), STG=V((2, SHARD, HALF), f32),
        DWH=V((2, 128, HID), f32), DWHp=V((128, HID), f32),
        MS=V((256, 128), f32), MO=V((256, 128), f32), MZ=V((NZ, 32, 128), f32),
        MR0=V((128, 128), f32), MR1=V((64, 128), f32), MR2=V((32, 128), f32),
        QF=V((3, 8, SENT + 16, 128), i16), QY=V((8, 80, YHALF), i16), QH=V((8, 48, BLK), i16),
    )
    for name, rows, cols in (("", SENT + 16, 128), ("Y", 80, YHALF), ("H", 48, BLK)):
        scratch["E1" + name] = V((4, 2, rows, cols), i16)
        scratch["E2" + name] = V((4, rows, cols), i16)
        scratch["E3" + name] = V((3, rows, cols), i16)
    for name, rows, cols in (("D", SENT + 16, 128), ("R", SENT + 16, 128), ("V", SENT + 16, 128), ("Y", 80, YHALF), ("H", 48, BLK)):
        scratch["R1" + name] = V((4, 2, rows, cols), i16)
        scratch["R2" + name] = V((4, rows, cols), i16)
        scratch["R3" + name] = V((3, rows, cols), i16)
    if ups_n:
        for i, (rows, cols) in enumerate(((SENT, 128),) * 3 + ((64, YHALF), (32, BLK))):
            scratch["FR%d" % i] = V((ups_n, rows, cols), f32)
        scratch["F"] = V((SENT, YHALF), f32)
        scratch["MF"] = V((ups_n, 32, 128), f32)
        scratch["MFR"] = V((ups_n, 32, 128), f32)
    scratch.update(
        ls=D((16,)), gs=D((5, 3, 6)), gr=D((5, 3, 6)), ms=D((4,)), mr=D((4,)),
        xs=D((11,)), xr=D((11,)), ss=D((5, 16 + ups_n)), sr=D((5, 16 + ups_n)), vs=D((9 + ups_n,)), vr=D((9 + ups_n,)),
    )
    vm, hb = pl.BlockSpec(memory_space=pltpu.VMEM), pl.BlockSpec(memory_space=pl.ANY)
    return pl.pallas_call(
        functools.partial(step_kernel, wide, token_count, n_tok, n_task),
        out_shape=(
            jax.ShapeDtypeStruct((n_tok, LAT), f32),
            jax.ShapeDtypeStruct((3, 8, SENT + 16, 128), i16),
            jax.ShapeDtypeStruct((8, 80, YHALF), i16),
            jax.ShapeDtypeStruct((8, 48, BLK), i16),
            jax.ShapeDtypeStruct((256, 128), f32),
        ),
        in_specs=[hb, vm, vm, vm, hb, vm, vm, vm, vm, hb, hb, vm, vm, vm],
        out_specs=[hb] * 5,
        scratch_shapes=scratch,
        compiler_params=pltpu.CompilerParams(
            collective_id=0, has_side_effects=True, vmem_limit_bytes=64 * 2**20),
    )(lat, actT, ids, steps, tgt, rb, rf, vb, vf, fw, dw, hw, tab, vec)


def adam(master, moment, second, gradient, rate):
    moment_new = moment_decay * moment + (1.0 - moment_decay) * gradient
    second_new = moment_decay * second + (1.0 - moment_decay) * gradient * gradient
    correct = 1.0 - moment_decay**STEP
    normed = moment_new / correct / (jnp.sqrt(second_new / correct) + adam_eps)
    return master - rate * (normed + weight_decay * master), moment_new, second_new


def adam_kernel(qf, qy, qh, fw, fm, fs, dw, dm, ds, hw, hm, hs, ofw, ofm, ofs, odw, odm, ods, ohw, ohm, ohs, gh):
    for j in range(4):
        cols = slice(128 * j, 128 * j + 128)
        g = decode(qf.at[0, j])[0:SHARD, :]
        ofw[:, cols], ofm[:, cols], ofs[:, cols] = adam(fw[:, cols], fm[:, cols], fs[:, cols], g, matrix_rate)
    for j in range(4):
        rows = slice(64 * j, 64 * j + 64)
        odw[rows, :], odm[rows, :], ods[rows, :] = adam(dw[rows, :], dm[rows, :], ds[rows, :], decode(qy.at[j]), matrix_rate)

    @pl.when(pl.program_id(0) == 0)
    def _():
        for k in range(2):
            for j in range(4):
                gh[32 * j : 32 * j + 32, :] = decode(qh.at[4 * k + j])
            new = adam(hw[:, k, :], hm[:, k, :], hs[:, k, :], gh[0:BINS, :], matrix_rate)
            ohw[:, k, :], ohm[:, k, :], ohs[:, k, :] = new


def adam_call(qf, qy, qh, first, dyn, heads):
    fblock = pl.BlockSpec((SHARD, HALF), lambda i: (0, i))
    dblock = pl.BlockSpec((BLK, 128), lambda i: (0, i))
    whole = pl.BlockSpec(heads[0].shape, lambda i: (0, 0, 0))
    out = [jax.ShapeDtypeStruct(a.shape, f32) for a in first + dyn + heads]
    return pl.pallas_call(
        adam_kernel,
        grid=(6,),
        out_shape=out,
        in_specs=[
            pl.BlockSpec((1, 4, SENT + 16, 128), lambda i: (i // 2, i % 2, 0, 0)),
            pl.BlockSpec((4, 80, 128), lambda i: (i // 3, 0, i % 3)),
            pl.BlockSpec(qh.shape, lambda i: (0, 0, 0)),
        ] + [fblock] * 3 + [dblock] * 3 + [whole] * 3,
        out_specs=[fblock] * 3 + [dblock] * 3 + [whole] * 3,
        scratch_shapes=[pltpu.VMEM((128, BLK), f32)],
        compiler_params=pltpu.CompilerParams(vmem_limit_bytes=48 * 2**20),
    )(qf, qy, qh, *first, *dyn, *heads)


def per_device(
    latents, actions, task_ids, steps_left, target_latents, reward_bins, reward_frac, value_bins, value_frac,
    first_weight, first_moment, first_second, dynamics_weight, dynamics_moment, dynamics_second,
    heads_weight, heads_moment, heads_second, task_table, table_moment, table_second,
    vector_params, vector_moment, vector_second,
):
    n_tok = latents.shape[0]
    wide = lax.axis_size("wide")
    token_count = float(HORIZON * n_tok * wide * lax.axis_size("narrow"))
    z = lax.axis_index("narrow")
    n_task = task_table.shape[0]
    n_vec = vector_params.shape[0]
    frame = lax.dynamic_update_slice(jnp.zeros((3072,), f32), vector_params, (64 * (z % 2),)).reshape(24, 128)
    to_class = lambda a: a.transpose(2, 0, 1)
    lg, qf, qy, qh, misc = step_call(
        wide, token_count, n_task, latents, actions.transpose(1, 2, 0), task_ids.reshape(1, n_tok),
        steps_left.reshape(1, n_tok), target_latents.transpose(1, 0, 2),
        reward_bins.T, reward_frac.T, value_bins.T, value_frac.T,
        first_weight, dynamics_weight, to_class(heads_weight), task_table, frame)
    new = adam_call(
        qf, qy, qh, [first_weight, first_moment, first_second], [dynamics_weight, dynamics_moment, dynamics_second],
        [to_class(a) for a in (heads_weight, heads_moment, heads_second)])
    heads_new = [a.transpose(1, 2, 0) for a in new[6:]]
    grad_vec = lax.dynamic_slice(misc[0:90].reshape(-1), (n_vec * z,), (n_vec,))
    grad_tab = lax.dynamic_slice(misc, (128 + 32 * z, 0), (n_task, TEMB))
    table_new = adam(task_table, table_moment, table_second, grad_tab, vector_rate)
    vector_new = adam(vector_params, vector_moment, vector_second, grad_vec, vector_rate)
    return (lg, *new[:6], *heads_new, *table_new, *vector_new)


def solution(mesh):
    tokens = ("wide", "narrow")
    in_specs = (
        P(tokens, None), P(tokens, None, None), P(tokens), P(tokens), P(tokens, None, None),
        P(tokens, None), P(tokens, None), P(tokens, None), P(tokens, None),
        *(P("narrow", None),) * 6, *(P(None, "narrow", None),) * 3, *(P("narrow", None),) * 3, *(P("narrow"),) * 3,
    )
    out_specs = (
        P(tokens, None), *(P("narrow", None),) * 6, *(P(None, "narrow", None),) * 3,
        *(P("narrow", None),) * 3, *(P("narrow"),) * 3,
    )
    return jax.shard_map(per_device, mesh=mesh, in_specs=in_specs, out_specs=out_specs, check_vma=False)
```

```python
import functools

import jax
import jax.numpy as jnp
from jax import lax
from jax.experimental import pallas as pl
from jax.experimental.pallas import tpu as pltpu
from jax.sharding import PartitionSpec as P

f32, bf16, i16, i32 = jnp.float32, jnp.bfloat16, jnp.int16, jnp.int32
MESH = pl.DeviceIdType.MESH

LAT = 768
HID = 1024
BINS = 101
TEMB = 96
ACTN = 8
HORIZON = 3
STEP = 5
NZ = 4
SHARD = 218
SENT = 224
BLK = 256
ROWS = 320
RB = 64
NB = ROWS // RB
ALL = HORIZON * ROWS
HALF = HID // 2
YHALF = LAT // 2
BOTT = 112
TASK_LANE = LAT + ACTN - 3 * SHARD
ACT_LANE = LAT - 3 * SHARD

norm_eps = 1e-05
adam_eps = 1e-08
moment_decay = 0.5
horizon_decay = 0.5
weight_decay = 0.01
matrix_rate = 0.03
vector_rate = 0.3
consistency_coef = 20.0
head_coef = 0.1

NN = (((1,), (0,)), ((), ()))
NT = (((1,), (1,)), ((), ()))
TN = (((0,), (0,)), ((), ()))


def dot(a, b, dims=NN):
    return lax.dot_general(a, b, dims, preferred_element_type=f32)


def lanes(n):
    return lax.broadcasted_iota(i32, (1, n), 1)


def block_rows(i, base=0):
    return pl.ds(pl.multiple_of(base + i * RB, RB), RB)


def encode(v, ref):
    rows = v.shape[0]
    top = jnp.max(jnp.abs(v), 0, keepdims=True)
    e = jnp.clip(jnp.ceil(jnp.log2(jnp.maximum(top, 1e-37))), -100.0, 120.0)
    ref[0:rows, :] = jnp.round(v * jnp.exp2(14.9 - e)).astype(i32).astype(i16)
    ref[rows : rows + 16, :] = jnp.broadcast_to(e, (16, v.shape[1])).astype(i32).astype(i16)


def decode(ref):
    rows = ref.shape[0] - 16
    e = ref[rows : rows + 16, :].astype(i32).astype(f32)[0:1, :]
    return ref[0:rows, :].astype(i32).astype(f32) * jnp.exp2(e - 14.9)


def pack_tiles(x):
    inside = lanes(BLK) < SHARD
    b0 = jnp.where(inside, x[:, 0:256], 0.0)
    b1 = jnp.where(inside, pltpu.roll(x[:, 128:512], 384 - 90, 1)[:, 0:256], 0.0)
    b2 = jnp.where(inside, pltpu.roll(x[:, 384:768], 384 - 52, 1)[:, 0:256], 0.0)
    b3 = jnp.where(lanes(128) < ACT_LANE, pltpu.roll(x[:, 640:768], 128 - 14, 1), 0.0)
    return b0, b1, b2, b3


def unpack_tiles(g):
    inside = lanes(BLK) < SHARD
    empty = jnp.zeros((g.shape[0], 128), f32)
    b0 = jnp.where(inside, g[:, 0:256], 0.0)
    b1 = pltpu.roll(jnp.concatenate([jnp.where(inside, g[:, 256:512], 0.0), empty], 1), 90, 1)
    b2 = pltpu.roll(jnp.concatenate([jnp.where(inside, g[:, 512:768], 0.0), empty], 1), 52, 1)
    b3 = pltpu.roll(jnp.where(lanes(128) < ACT_LANE, g[:, 768:896], 0.0), 14, 1)
    return jnp.concatenate(
        [
            b0[:, 0:128],
            b0[:, 128:256] + b1[:, 0:128],
            b1[:, 128:256],
            b1[:, 256:384] + b2[:, 0:128],
            b2[:, 128:256],
            b2[:, 256:384] + b3,
        ],
        1,
    )


def group_sums(x, ones):
    parts = []
    for j in range(0, x.shape[1], 256):
        v = x[:, j : j + 256]
        high = v.astype(bf16)
        low = (v - high.astype(f32)).astype(bf16)
        parts.append(dot(high, ones) + dot(low, ones))
    return jnp.concatenate(parts, 1)


def mish_parts(n):
    u = jnp.exp(jnp.minimum(n, 40.0))
    q = u * (u + 2.0)
    r = 1.0 / (q + 2.0)
    bent = q * r
    return bent, bent + (4.0 * n) * (u * (u + 1.0)) * (r * r)


def add_columns(acc, values):
    for k, v in enumerate(values):
        total = acc[8 * k : 8 * k + 8, :]
        for j in range(v.shape[0] // 8):
            total = total + v[8 * j : 8 * j + 8, :]
        acc[8 * k : 8 * k + 8, :] = total


def rcopy(src, dst, send_sem, recv_sem, device):
    return pltpu.make_async_remote_copy(
        src_ref=src, dst_ref=dst, send_sem=send_sem, recv_sem=recv_sem, device_id=device, device_id_type=MESH
    )


def step_kernel(wide, token_count, n_tok, n_task, lat, actT, ids, steps, tgt, rb, rf, vb, vf, fw, dw, hw, tab, vec,
                lg, qf, qy, qh, misc, **s):
    ups_n = wide.bit_length() - 4
    w, z = lax.axis_index("wide"), lax.axis_index("narrow")
    b0, b1, b2 = lax.rem(w, 2), lax.rem(lax.div(w, 2), 2), lax.rem(lax.div(w, 4), 2)
    pc, p1, p2 = (w + 1 - 2 * b0, z), (w + 2 - 4 * b1, z), (w + 4 - 8 * b2, z)
    zs = [(w, lax.rem(z + d, NZ)) for d in range(NZ)]
    from_z = [lax.rem(z + NZ - d, NZ) for d in range(NZ)]
    ups = []
    for u in range(ups_n):
        bit = 8 << u
        ups.append((w + bit - 2 * bit * lax.rem(lax.div(w, bit), 2), z))
    me = b0 * 4 + b1 * 2 + b2
    own = b1 * 2 + b2
    sends = []

    def pick(odd, even_value, odd_value):
        return even_value + odd * (odd_value - even_value)

    def launch(copy):
        copy.start()
        sends.append(copy)

    X, XT, XTp, U, AT, ATp, DU = s["X"], s["XT"], s["XTp"], s["U"], s["AT"], s["ATp"], s["DU"]
    WF, WD, HT, SM, VEC = s["WF"], s["WD"], s["HT"], s["SM"], s["VEC"]
    PRE, TU, TS, ACT = s["PRE"], s["TU"], s["TS"], s["ACT"]
    GP, GPp, GDL, GDLp = s["GP"], s["GPp"], s["GDL"], s["GDLp"]
    INV, DINV, SIDE, SD, ONES, VA, VT, GEMB = (
        s["INV"], s["DINV"], s["SIDE"], s["SD"], s["ONES"], s["VA"], s["VT"], s["GEMB"])

    barrier = pltpu.get_barrier_semaphore()
    peers = [pc, p1, p2] + zs[1:] + ups
    for p in peers:
        pl.semaphore_signal(barrier, inc=1, device_id=p, device_id_type=MESH)

    STG = s["STG"]
    loads = []

    def load_first(part):
        return pltpu.make_async_copy(
            fw.at[:, pl.ds(HALF * part, HALF)], STG.at[part % 2], s["ls"].at[part % 2])

    loads.append(pltpu.make_async_copy(dw, DU.at[pl.ds(0, BLK)], s["ls"].at[3]))
    loads.append(pltpu.make_async_copy(lat, GDL.at[pl.ds(0, n_tok)], s["ls"].at[4]))
    for t in range(3):
        loads.append(pltpu.make_async_copy(tgt.at[t], s["TG"].at[t, pl.ds(0, n_tok)], s["ls"].at[5 + t]))
    load_first(0).start()
    load_first(1).start()
    for c in loads:
        c.start()

    def cast_first(br):
        for part in (2 * br, 2 * br + 1):
            load_first(part).wait()
            rows = jnp.concatenate([STG[part % 2].astype(bf16), jnp.zeros((SENT - SHARD, HALF), bf16)], 0)
            WF[pl.ds(pl.multiple_of(BLK * z, BLK), SENT), HALF * part : HALF * part + HALF] = rows
            if part < 4:
                load_first(part + 2).start()

    cast_first(0)
    pl.semaphore_wait(barrier, len(peers))

    gs, gr = s["gs"], s["gr"]

    class Item:
        def __init__(self, index, view):
            self.i, self.view = index, view

        def _recv(self, d, kind, view):
            rcopy(view, view, gs.at[self.i, d - 1, kind], gr.at[self.i, d - 1, kind], pc).wait_recv()

        def _send(self, d, kind, view, device):
            launch(rcopy(view, view, gs.at[self.i, d - 1, kind], gr.at[self.i, d - 1, kind], device))

        def start(self):
            for d in (1, 3, 2):
                self._send(d, 0, self.view(z, me, 1, None), zs[d])

        def spread(self, *ds):
            for d in ds or (1, 3, 2):
                mine = self.view(from_z[d], me, 1, None)
                self._recv(d, 0, mine)
                self._send(d, 1, mine, p1)
                self._send(d, 2, mine, p2)

        def forward(self, *ds):
            s1, s2 = me + 2 - 4 * b1, me + 1 - 2 * b2
            for d in ds or (1, 3, 2):
                q = from_z[d]
                self._recv(d, 1, self.view(q, s1, 1, None))
                self._send(d, 3, self.view(q, s1, 1, 0), p2)
                self._recv(d, 2, self.view(q, s2, 1, None))
                self._send(d, 4, self.view(q, s2, 1, 1), p1)

        def cross(self, *ds):
            s12 = 4 * b0 + 3 - own
            for d in ds or (1, 3, 2):
                q = from_z[d]
                self._recv(d, 3, self.view(q, s12, 1, 0))
                self._recv(d, 4, self.view(q, s12, 1, 1))
                self._send(d, 5, self.view(q, 4 * b0, 4, None), pc)

        def finish(self):
            for d in (1, 3, 2):
                self._recv(d, 5, self.view(from_z[d], 4 - 4 * b0, 4, None))

    def first_view(br):
        def view(q, at, n, half):
            lo, size = (0, SENT) if half is None else (BOTT * half, BOTT)
            return WF.at[pl.ds(pl.multiple_of(BLK * q + lo, 16), size), pl.ds(pl.multiple_of(HID * br + 128 * at, 128), 128 * n)]
        return view

    def dyn_view(q, at, n, half):
        lo, size = (0, 32 * n) if half is None else (16 * half, 16)
        return WD.at[pl.ds(pl.multiple_of(BLK * q + 32 * at + lo, 16), size)]

    def heads_view(q, at, n, half):
        cols = pl.ds(pl.multiple_of(BLK * q, BLK), BLK)
        rows = pl.ds(pl.multiple_of(16 * at, 16), 16 * n)
        if half is None:
            return HT.at[:, rows, cols]
        return HT.at[pl.ds(half, 1), rows, cols]

    gD, gY, gR, gV, gH = (
        Item(0, first_view(0)), Item(1, dyn_view), Item(2, first_view(1)), Item(3, first_view(2)), Item(4, heads_view))

    def vec_rows():
        n_vec = vec.shape[0]
        whole = n_vec // 128
        VR = s["VR"]
        VR[...] = jnp.zeros_like(VR)
        for r in range(whole):
            VR[r + 1 : r + 2, :] = vec[pl.ds(128 * r, 128)].reshape(1, 128)
        left = n_vec - 128 * whole
        VR[whole + 1 : whole + 2, 0:left] = vec[pl.ds(128 * whole, left)].reshape(1, left)
        plain = VR[1:33, :]
        moved = jnp.where(lanes(128) < 64, pltpu.roll(VR[0:32, :], 64, 1), pltpu.roll(plain, 64, 1))
        return jnp.where(lax.rem(z, 2) == 1, moved, plain).astype(bf16)

    gD.start()
    frame = vec_rows()
    SM[z, 0:32, :] = frame
    SM[z, 32:64, :] = jnp.zeros((32, 128), bf16)
    SM[z, 32 : 32 + n_task, 0:TEMB] = tab[...].astype(bf16)
    for d in (1, 3, 2):
        launch(rcopy(SM.at[z], SM.at[z], s["ms"].at[d], s["mr"].at[d], zs[d]))
    loads[0].wait()
    WD[pl.ds(pl.multiple_of(BLK * z, BLK), BLK), :] = DU[0:BLK, :].astype(bf16)
    gY.start()
    cast_first(1)
    gR.start()
    gD.spread(1, 3)
    own_cols = pl.ds(pl.multiple_of(BLK * z, BLK), BLK)
    for k in range(2):
        PRE[0:128, 0:BLK] = jnp.zeros((128, BLK), f32)
        PRE[0:BINS, 0:BLK] = hw[:, k, :]
        HT[k, :, own_cols] = PRE[0:128, 0:BLK].astype(bf16)
    gH.start()
    gD.spread(2)
    cast_first(2)
    gV.start()

    for t in range(3):
        s["TG"][t, n_tok:ROWS, :] = jnp.zeros((ROWS - n_tok, LAT), bf16)
    GDL[n_tok:ROWS, :] = jnp.zeros((ROWS - n_tok, LAT), bf16)
    for q in range(NZ):
        WF[BLK * q + SENT : BLK * q + BLK, :] = jnp.zeros((BLK - SENT, 3 * HID), bf16)
    loads[1].wait()

    def pack_latents(i, c):
        rows = block_rows(i)
        b = pack_tiles(GDL[rows, :].astype(f32))
        X[rows, 0:896] = jnp.concatenate(b, 1).astype(bf16)
        return c

    lax.fori_loop(0, NB, pack_latents, 0)
    gD.forward(1, 3)
    gY.spread(1, 3)
    idr = s["IDR"]
    idr[...] = jnp.full_like(idr, -1)
    idr[0:1, 0:n_tok] = ids[...].reshape(1, n_tok)
    slot = lax.broadcasted_iota(i32, (128, 1), 0)
    task = jnp.where(slot % 32 < n_task, n_task * (slot // 32) + slot % 32, -2)
    PKT = s["PKT"]
    PKT[...] = jnp.where(idr[0:1, 0:ROWS] == task, 1.0, 0.0).astype(bf16)
    gD.forward(2)
    gY.spread(2)
    gD.cross(1, 3)

    for d in (1, 3, 2):
        q = from_z[d]
        rcopy(SM.at[q], SM.at[q], s["ms"].at[d], s["mr"].at[d], pc).wait_recv()
    full = s["VFULL"]
    full[...] = jnp.zeros_like(full)
    for q, at in enumerate((0, 22, 45, 67)):
        full[at : at + 24, :] = full[at : at + 24, :] + SM[q, 0:32, :].astype(f32)[0:24, :]
    for r in range(12):
        n, first = (8, 8 * r) if r < 9 else (6, 72 + 6 * (r - 9))
        for j in range(n):
            VEC[r : r + 1, 128 * j : 128 * j + 128] = full[first + j : first + j + 1, :]
    place = jnp.concatenate([SM[q, 32:64, :] for q in range(NZ)], 0).astype(f32)
    table = pltpu.roll(jnp.concatenate([place, jnp.zeros_like(place)], 1), TASK_LANE, 1).astype(bf16)
    AC = s["AC"]
    AC[...] = jnp.zeros_like(AC)
    act_to = jnp.where(
        lax.broadcasted_iota(i32, (16, BLK), 0) + ACT_LANE == lax.broadcasted_iota(i32, (16, BLK), 1), 1.0, 0.0
    ).astype(bf16)
    rows_of_task = dot(PKT[...], table, TN)
    gD.cross(2)
    for t in range(3):
        AC[0:ACTN, 0:n_tok] = actT[t].astype(f32)
        SD[t] = (rows_of_task + dot(AC[:, 0:ROWS].astype(bf16), act_to, TN)).astype(bf16)

    def side_block(t, dest):
        X[dest : dest + ROWS, 768:896] = (X[dest : dest + ROWS, 768:896].astype(f32) + SD[t, :, 0:128].astype(f32)).astype(bf16)
        X[dest : dest + ROWS, 896:1024] = SD[t, :, 128:256]

    side_block(0, 0)
    gY.forward(1, 3)

    def later_setup():
        tile = lax.broadcasted_iota(i32, (256, 256), 0) // 8 == lax.broadcasted_iota(i32, (256, 256), 1) // 8
        ONES[...] = jnp.where(tile, 1.0, 0.0).astype(bf16)
        for t in range(3):
            st = s["ST"]
            st[...] = jnp.zeros_like(st)
            st[0:1, 0:n_tok] = steps[...].reshape(1, n_tok).astype(f32)
            for k, ref in enumerate((rb, rf, vb, vf)):
                st[k + 1 : k + 2, 0:n_tok] = ref[t : t + 1, :].astype(f32)
            SIDE[t] = st[...].T[0:ROWS, :]
        for ref in (VA, VT, GEMB, s["DWH"], s["MS"]):
            ref[...] = jnp.zeros_like(ref)

    gD.finish()

    def matmul(out, orows, n, width, left, right, dims=NN):
        def tile_step(j, c):
            cols = pl.ds(pl.multiple_of(j * width, width), width)
            out[orows, cols] = dot(left, right(cols), dims)
            return c
        lax.fori_loop(0, n // width, tile_step, 0)

    def first_forward(br, base):
        def tile_step(j, c):
            cols = pl.ds(pl.multiple_of(j * 512, 512), 512)
            from_cols = pl.ds(pl.multiple_of(HID * br + j * 512, 512), 512)
            PRE[:, cols] = dot(X[pl.ds(base, ROWS), :], WF[:, from_cols])
            return c
        lax.fori_loop(0, 2, tile_step, 0)

    def norm_mish(br, unit, inv, unit_base, slope):
        bias, gain, shift = (VEC[3 * br + k : 3 * br + k + 1, :] for k in range(3))

        def step(i, c):
            rows = block_rows(i)
            p = PRE[rows, :] + bias
            ce = p - jnp.mean(p, -1, keepdims=True)
            iv = lax.rsqrt(jnp.mean(ce * ce, -1, keepdims=True) + norm_eps)
            un = ce * iv
            n = un * gain + shift
            bent, sl = mish_parts(n)
            ACT[rows, :] = (n * bent).astype(bf16)
            if slope is not None:
                slope[rows, :] = sl
            unit[block_rows(i, unit_base), :] = un
            inv[block_rows(i, unit_base), :] = jnp.broadcast_to(iv, (RB, 128))
            return c
        lax.fori_loop(0, NB, step, 0)

    def dyn_forward(t, between):
        base = ROWS * t
        first_forward(0, base)
        between(0)
        norm_mish(0, U, INV, base, None)
        between(1)
        matmul(TU, slice(0, ROWS), LAT, 384, ACT[...], lambda cols: WD[:, cols])
        AT[:, base : base + ROWS] = ACT[...].T
        bias, gain, shift = (VEC[9 + k : 10 + k, 0:LAT] for k in range(3))

        def step(i, c):
            rows, at = block_rows(i), block_rows(i, base)
            p = TU[rows, 0:LAT] + bias
            ce = p - jnp.mean(p, -1, keepdims=True)
            iv = lax.rsqrt(jnp.mean(ce * ce, -1, keepdims=True) + norm_eps)
            un = ce * iv
            DU[at, :] = un
            DINV[at, :] = jnp.broadcast_to(iv, (RB, 128))
            if t < 2:
                e = jnp.exp(un * gain + shift)
                b = pack_tiles(e / group_sums(e, ONES[...]))
                X[block_rows(i, base + ROWS), 0:896] = jnp.concatenate(b, 1).astype(bf16)
            return c
        lax.fori_loop(0, NB, step, 0)
        if t < 2:
            side_block(t + 1, base + ROWS)

    def between_0(at):
        if at == 0:
            gY.forward(2)
        else:
            gY.cross()
            gR.spread()
            later_setup()
            gY.finish()

    def between_1(at):
        if at == 1:
            gR.forward()

    def between_2(at):
        if at == 1:
            gH.cross()

    dyn_forward(0, between_0)
    gH.spread()
    dyn_forward(1, between_1)
    gR.cross()
    gH.forward()
    gV.spread()
    dyn_forward(2, between_2)
    XT[...] = X[...].T
    xs, xr = s["xs"], s["xr"]
    launch(rcopy(XT, XTp, xs.at[0], xr.at[0], pc))
    launch(rcopy(AT, ATp, xs.at[1], xr.at[1], pc))
    gR.finish()
    gH.finish()
    gV.forward()

    def norm_backward(br, unit, inv, unit_base, slope, out_base):
        gain, shift = VEC[3 * br + 1 : 3 * br + 2, :], VEC[3 * br + 2 : 3 * br + 3, :]
        acc = VA.at[br]

        def step(i, c):
            rows, at = block_rows(i), block_rows(i, unit_base)
            un = unit[at, :]
            sl = mish_parts(un * gain + shift)[1] if slope is None else slope[rows, :]
            gn = PRE[rows, :] * sl
            h = gn * gain
            gp = (h - jnp.mean(h, -1, keepdims=True) - un * jnp.mean(h * un, -1, keepdims=True)) * inv[at, 0:1]
            GP[block_rows(i, out_base), HID * br : HID * br + HID] = gp.astype(bf16)
            add_columns(acc, (gp, gn * un, gn))
            return c
        lax.fori_loop(0, NB, step, 0)

    def head_step(k, t):
        base = ROWS * t
        first_forward(1 + k, base)
        norm_mish(1 + k, TU, s["HINV"], 0, TS)
        logits = dot(ACT[...], HT[k], NT)
        real = lanes(128) < BINS
        logits = jnp.where(real, logits, -1e30)
        e = jnp.exp(logits - jnp.max(logits, -1, keepdims=True))
        soft = e / jnp.sum(e, -1, keepdims=True)
        side = SIDE[t]
        at, frac = side[:, 1 + 2 * k : 2 + 2 * k], side[:, 2 + 2 * k : 3 + 2 * k]
        level = lanes(128).astype(f32)
        hot = jnp.where(level == at, 1.0 - frac, 0.0) + jnp.where(level == at + 1.0, frac, 0.0)
        weight = jnp.where(side[:, 0:1] > t, f32(horizon_decay**t), 0.0) / token_count
        gl = jnp.where(real, weight * head_coef * (soft - hot), 0.0).astype(bf16)
        s["DWH"][k] = s["DWH"][k] + dot(gl.astype(f32).T.astype(bf16), ACT[...])
        PRE[...] = dot(gl, HT[k])
        norm_backward(1 + k, TU, s["HINV"], 0, TS, base)

    def dyn_backward(t, between=None):
        base = ROWS * t
        gain, shift = VEC[10:11, 0:LAT], VEC[11:12, 0:LAT]
        scale = 2.0 * consistency_coef / LAT

        def step(i, c):
            rows, at = block_rows(i), block_rows(i, base)
            un = DU[at, :]
            e = jnp.exp(un * gain + shift)
            sx = e / group_sums(e, ONES[...])
            weight = jnp.where(SIDE[t, rows, 0:1] > t, f32(horizon_decay**t), 0.0) / token_count
            g = weight * scale * (sx - s["TG"][t, rows, :].astype(f32))
            if t < 2:
                g = g + unpack_tiles(PRE[rows, 0:896])
            gn = sx * (g - group_sums(g * sx, ONES[...]))
            h = gn * gain
            gp = (h - jnp.mean(h, -1, keepdims=True) - un * jnp.mean(h * un, -1, keepdims=True)) * DINV[at, 0:1]
            GDL[at, :] = gp.astype(bf16)
            add_columns(VT, (gp, gn * un, gn))
            return c
        lax.fori_loop(0, NB, step, 0)
        yc = pl.ds(pl.multiple_of(YHALF * (1 - b0), 128), YHALF)
        launch(rcopy(GDL.at[pl.ds(base, ROWS), yc], GDLp.at[pl.ds(base, ROWS)], xs.at[4 + t], xr.at[4 + t], pc))
        if between is not None:
            between()

        def tile_step(j, c):
            cols = pl.ds(pl.multiple_of(j * 512, 512), 512)
            PRE[:, cols] = dot(GDL[pl.ds(base, ROWS), :], WD[cols, :], NT)
            return c
        lax.fori_loop(0, 2, tile_step, 0)
        norm_backward(0, U, INV, base, None, base)
        gc = pl.ds(pl.multiple_of(HALF * (1 - b0), HALF), HALF)
        launch(rcopy(GP.at[pl.ds(base, ROWS), gc], GPp.at[0, pl.ds(base, ROWS)], xs.at[7 + t], xr.at[7 + t], pc))

    def inputs_backward(t):
        base = ROWS * t

        def tile_step(j, c):
            cols = pl.ds(pl.multiple_of(j * 512, 512), 512)
            PRE[:, cols] = dot(GP[pl.ds(base, ROWS), :], WF[cols, :], NT)
            return c
        lax.fori_loop(0, 2, tile_step, 0)
        GEMB[...] = GEMB[...] + PRE[:, 768:1024]

    rs_s, rs_r = s["ss"], s["sr"]

    class Stream:
        def __init__(self, index, grad, view, E, R, Q, half):
            self.i, self.grad, self.view, self.Q, self.half = index, grad, view, Q, half
            (self.E1, self.E2, self.E3), (self.R1, self.R2, self.R3) = E, R
            self.held = {}

        def _copy(self, at, src, dst, device):
            return rcopy(src, dst, rs_s.at[self.i, at], rs_r.at[self.i, at], device)

        def _send(self, at, src, dst, device):
            c = self._copy(at, src, dst, device)
            c.start()
            self.held[at] = c

        def _recv(self, at, dst):
            self._copy(at, dst, dst, pc).wait_recv()

        def release(self):
            for c in self.held.values():
                c.wait_send()
            self.held = {}

        def stage1(self):
            for d in (2, 1, 3, 0):
                q = zs[d][1]
                odd = lax.rem(q, 2)
                base = pick(odd, 2 - 2 * b1, 1 - b2)
                for j in range(2):
                    encode(self.grad[self.view(q, base + j * (1 + odd))], self.E1.at[q, j])
                self._send(d, self.E1.at[q], self.R1.at[q], (pick(odd, p1[0], p2[0]), z))

        def stage2(self, *ds):
            for d in ds or (2, 1, 3, 0):
                q = zs[d][1]
                odd = lax.rem(q, 2)
                self._recv(d, self.R1.at[q])
                keep = pick(odd, b2, b1)
                other = pick(odd, own + 1 - 2 * b2, own + 2 - 4 * b1)
                encode(self.grad[self.view(q, other)] + decode(self.R1.at[q, 1 - keep]), self.E2.at[q])
                self._send(4 + d, self.E2.at[q], self.R2.at[q], (pick(odd, p2[0], p1[0]), z))
                mine = self.view(q, own)
                self.grad[mine] = self.grad[mine] + decode(self.R1.at[q, keep])

        def stage3(self, *ds):
            for d in ds or (2, 1, 3):
                q = zs[d][1]
                self._recv(4 + d, self.R2.at[q])
                encode(self.grad[self.view(q, own)] + decode(self.R2.at[q]), self.E3.at[d - 1])
                self._send(7 + d, self.E3.at[d - 1], self.R3.at[d - 1], zs[d])

        def stage4(self):
            self._recv(4, self.R2.at[z])
            total = self.grad[self.view(z, own)] + decode(self.R2.at[z])
            for d in (1, 3, 2):
                self._recv(7 + d, self.R3.at[d - 1])
                total = total + decode(self.R3.at[d - 1])
            for u in range(ups_n):
                rows, cols = total.shape
                F, FR = s["F"].at[pl.ds(0, rows), pl.ds(0, cols)], s["FR%d" % self.i]
                F[...] = total
                self._send(16 + u, F, FR.at[u], ups[u])
                self._recv(16 + u, FR.at[u])
                self.held.pop(16 + u).wait_send()
                total = total + FR[u]
            encode(total, self.Q.at[me])
            self._send(11, self.Q.at[me], self.Q.at[me], p1)
            self._send(12, self.Q.at[me], self.Q.at[me], p2)

        def stage5(self):
            s1, s2 = me + 2 - 4 * b1, me + 1 - 2 * b2
            n = self.Q.shape[1]
            low, high = pl.ds(0, self.half), pl.ds(self.half, n - self.half)
            self._recv(11, self.Q.at[s1])
            self._send(13, self.Q.at[s1, low], self.Q.at[s1, low], p2)
            self._recv(12, self.Q.at[s2])
            self._send(14, self.Q.at[s2, high], self.Q.at[s2, high], p1)

        def stage6(self):
            s12 = 4 * b0 + 3 - own
            n = self.Q.shape[1]
            low, high = pl.ds(0, self.half), pl.ds(self.half, n - self.half)
            self._recv(13, self.Q.at[s12, low])
            self._recv(14, self.Q.at[s12, high])
            mine = self.Q.at[pl.ds(4 * b0, 4)]
            self._send(15, mine, mine, pc)

        def stage7(self, out, sem):
            self._recv(15, self.Q.at[pl.ds(4 - 4 * b0, 4)])
            c = pltpu.make_async_copy(self.Q, out, sem)
            c.start()
            return c

    def first_slice(q, at):
        return (pl.ds(pl.multiple_of(BLK * q, BLK), SENT), pl.ds(pl.multiple_of(128 * at, 128), 128))

    def y_slice(q, at):
        return (pl.ds(pl.multiple_of(BLK * q + 64 * at, 64), 64), slice(None))

    def h_slice(q, at):
        return (b0, pl.ds(pl.multiple_of(32 * at, 32), 32), pl.ds(pl.multiple_of(BLK * q, BLK), BLK))

    EF = (s["E1"], s["E2"], s["E3"])
    streams = []
    for i, name in enumerate("DRV"):
        streams.append(Stream(
            i, s["DWB"] if name == "V" else s["DWA"], first_slice, EF,
            tuple(s["R%d%s" % (k, name)] for k in (1, 2, 3)), s["QF"].at[i], 128))
    sD, sR, sV = streams
    sY = Stream(3, s["DWY"], y_slice, tuple(s["E%dY" % k] for k in (1, 2, 3)),
                tuple(s["R%dY" % k] for k in (1, 2, 3)), s["QY"], 48)
    sH = Stream(4, s["DWH"], h_slice, tuple(s["E%dH" % k] for k in (1, 2, 3)),
                tuple(s["R%dH" % k] for k in (1, 2, 3)), s["QH"], 32)

    def send_half(br):
        cols = pl.ds(pl.multiple_of(HID * br + HALF * (1 - b0), HALF), HALF)
        launch(rcopy(GP.at[:, cols], GPp.at[br], xs.at[1 + br], xr.at[1 + br], pc))

    def wait_x(at, dst):
        rcopy(dst, dst, xs.at[at], xr.at[at], pc).wait_recv()

    def weight_grad(out, n, left, right, left2, right2):
        def tile_step(j, c):
            cols = pl.ds(pl.multiple_of(j * n, n), n)
            out[:, cols] = dot(left[...], right(j)) + dot(left2[...], right2(cols))
            return c
        lax.fori_loop(0, out.shape[1] // n, tile_step, 0)

    def first_grad(br, out):
        weight_grad(
            out, 256, XT,
            lambda j: GP[:, pl.ds(pl.multiple_of(HID * br + HALF * b0 + 256 * j, 256), 256)],
            XTp, lambda cols: GPp[br, :, cols])

    def y_grad():
        wait_x(1, ATp)
        for t in range(3):
            wait_x(4 + t, GDLp.at[pl.ds(ROWS * t, ROWS)])
        weight_grad(
            s["DWY"], 128, AT,
            lambda j: GDL[:, pl.ds(pl.multiple_of(YHALF * b0 + 128 * j, 128), 128)],
            ATp, lambda cols: GDLp[:, cols])
        sY.stage1()

    head_step(0, 0)
    gV.cross()
    head_step(0, 1)
    head_step(0, 2)
    send_half(1)
    gV.finish()
    head_step(1, 0)
    wait_x(0, XTp)
    wait_x(2, GPp.at[1])
    first_grad(1, s["DWA"])
    sR.stage1()
    head_step(1, 1)
    head_step(1, 2)
    sR.stage2()
    send_half(2)
    launch(rcopy(s["DWH"].at[1 - b0], s["DWHp"], xs.at[10], xr.at[10], pc))
    for c in loads[2:]:
        c.wait()
    dyn_backward(2)
    sR.stage3()
    wait_x(3, GPp.at[2])
    first_grad(2, s["DWB"])
    sR.release()
    sV.stage1()
    inputs_backward(2)
    wait_x(10, s["DWHp"])
    s["DWH"][b0] = s["DWH"][b0] + s["DWHp"][...]
    sH.stage1()
    dyn_backward(1)
    sR.stage4()
    sV.stage2()
    sH.stage2()
    inputs_backward(1)
    sR.stage5()
    dyn_backward(0, y_grad)
    sV.stage3()
    sH.stage3()
    for t in range(3):
        wait_x(7 + t, GPp.at[0, pl.ds(ROWS * t, ROWS)])
    first_grad(0, s["DWA"])
    sV.release()
    sD.stage1()
    sR.stage6()
    inputs_backward(0)

    def write_latent(i, c):
        rows = block_rows(i)
        DU[rows, :] = unpack_tiles(PRE[rows, 0:896])
        return c
    lax.fori_loop(0, NB, write_latent, 0)
    lg_copy = pltpu.make_async_copy(DU.at[pl.ds(0, n_tok)], lg, s["ls"].at[8])
    lg_copy.start()
    ge = GEMB[...]
    g1 = ge.astype(bf16)
    g2 = (ge - g1.astype(f32)).astype(bf16)
    g3 = (ge - g1.astype(f32) - g2.astype(f32)).astype(bf16)
    pk = PKT[...]
    by_task = dot(pk, g1) + dot(pk, g2) + dot(pk, g3)
    M = s["MS"]
    M[128:256, :] = pltpu.roll(by_task, BLK - TASK_LANE, 1)[:, 0:128]
    for r in range(12):
        acc, n, first = (VA.at[r // 3], 8, 8 * r) if r < 9 else (VT, 6, 72 + 6 * (r - 9))
        k = r % 3
        row = jnp.sum(acc[8 * k : 8 * k + 8, :], 0, keepdims=True)
        for j in range(n):
            M[first + j : first + j + 1, :] = row[:, 128 * j : 128 * j + 128]

    vs, vr = s["vs"], s["vr"]

    def small(at, src, dst, device):
        return rcopy(src, dst, vs.at[at], vr.at[at], device)

    def rows_of(start, n):
        return pl.ds(pl.multiple_of(start, 32), n)

    halves = ((0, pc, b0, 128), (1, p1, b1, 64), (2, p2, b2, 32))

    def halve(step, start):
        at, device, bit, n = halves[step]
        launch(small(at, M.at[rows_of(start + n * (1 - bit), n)], s["MR%d" % step], device))

    def halved(step, start):
        at, device, bit, n = halves[step]
        small(at, s["MR%d" % step], s["MR%d" % step], device).wait_recv()
        mine = rows_of(start + n * bit, n)
        M[mine, :] = M[mine, :] + s["MR%d" % step][...]
        return start + n * bit

    halve(0, 0)
    sY.stage2()
    at = halved(0, 0)
    halve(1, at)
    sV.stage4()
    sH.stage4()
    at = halved(1, at)
    halve(2, at)
    sD.stage2(2, 1)
    sY.stage3()
    sD.stage2(3, 0)
    at = halved(2, at)
    MZ = s["MZ"]
    MZ[z] = M[rows_of(at, 32), :]
    for d in (2, 1, 3):
        launch(small(2 + d, MZ.at[z], MZ.at[z], zs[d]))
    sV.stage5()
    sH.stage5()
    sD.stage3()
    sY.stage4()
    for d in (1, 3, 2):
        small(2 + d, MZ.at[from_z[d]], MZ.at[from_z[d]], pc).wait_recv()
    total = (MZ[0] + MZ[1]) + (MZ[2] + MZ[3])
    for u in range(ups_n):
        s["MF"][u] = total
        launch(small(9 + u, s["MF"].at[u], s["MFR"].at[u], ups[u]))
        small(9 + u, s["MFR"].at[u], s["MFR"].at[u], ups[u]).wait_recv()
        total = total + s["MFR"][u]
    MO = s["MO"]
    MO[rows_of(at, 32), :] = total
    launch(small(6, MO.at[rows_of(at, 32)], MO.at[rows_of(at, 32)], p2))
    sV.stage6()
    sH.stage6()
    outs = [lg_copy]
    outs.append(sR.stage7(qf.at[1], s["ls"].at[9]))
    sY.stage5()
    o = at + 32 - 64 * b2
    small(6, MO.at[rows_of(o, 32)], MO.at[rows_of(o, 32)], p2).wait_recv()
    at = at - 32 * b2
    launch(small(7, MO.at[rows_of(at, 64)], MO.at[rows_of(at, 64)], p1))
    sD.stage4()
    sY.stage6()
    o = at + 64 - 128 * b1
    small(7, MO.at[rows_of(o, 64)], MO.at[rows_of(o, 64)], p1).wait_recv()
    at = at - 64 * b1
    launch(small(8, MO.at[rows_of(at, 128)], MO.at[rows_of(at, 128)], pc))
    outs.append(sV.stage7(qf.at[2], s["ls"].at[10]))
    outs.append(sH.stage7(qh, s["ls"].at[11]))
    sD.stage5()
    outs.append(sY.stage7(qy, s["ls"].at[12]))
    o = at + 128 - 256 * b0
    small(8, MO.at[rows_of(o, 128)], MO.at[rows_of(o, 128)], pc).wait_recv()
    c = pltpu.make_async_copy(MO, misc, s["ls"].at[13])
    c.start()
    outs.append(c)
    sD.stage6()
    outs.append(sD.stage7(qf.at[0], s["ls"].at[14]))
    for c in outs:
        c.wait()
    for st in (sD, sR, sV, sY, sH):
        st.release()
    for c in sends:
        c.wait_send()


def step_call(wide, token_count, n_task, lat, actT, ids, steps, tgt, rb, rf, vb, vf, fw, dw, hw, tab, vec):
    n_tok = lat.shape[0]
    ups_n = wide.bit_length() - 4
    V = pltpu.VMEM
    D = pltpu.SemaphoreType.DMA
    scratch = dict(
        WF=V((HID, 3 * HID), bf16), WD=V((HID, LAT), bf16), HT=V((2, 128, HID), bf16),
        SM=V((NZ, 64, 128), bf16), VR=V((40, 128), f32), VEC=V((16, HID), f32), VFULL=V((96, 128), f32),
        X=V((ALL, HID), bf16), XT=V((HID, ALL), bf16), XTp=V((HID, ALL), bf16),
        U=V((ALL, HID), f32), AT=V((HID, ALL), bf16), ATp=V((HID, ALL), bf16),
        DU=V((ALL, LAT), f32), TG=V((3, ROWS, LAT), bf16),
        PRE=V((ROWS, HID), f32), TU=V((ROWS, HID), f32), TS=V((ROWS, HID), f32), ACT=V((ROWS, HID), bf16),
        GP=V((ALL, 3 * HID), bf16), GPp=V((3, ALL, HALF), bf16), GDL=V((ALL, LAT), bf16), GDLp=V((ALL, YHALF), bf16),
        INV=V((ALL, 128), f32), HINV=V((ROWS, 128), f32), DINV=V((ALL, 128), f32),
        SIDE=V((3, ROWS, 16), f32), SD=V((3, ROWS, BLK), bf16), ONES=V((256, 256), bf16),
        VA=V((3, 24, HID), f32), VT=V((24, LAT), f32), GEMB=V((ROWS, BLK), f32),
        ST=V((16, 384), f32), IDR=V((8, 384), i32), PKT=V((128, ROWS), bf16), AC=V((16, 384), f32),
        DWA=V((HID, HALF), f32), DWB=V((HID, HALF), f32), DWY=V((HID, YHALF), f32), STG=V((2, SHARD, HALF), f32),
        DWH=V((2, 128, HID), f32), DWHp=V((128, HID), f32),
        MS=V((256, 128), f32), MO=V((256, 128), f32), MZ=V((NZ, 32, 128), f32),
        MR0=V((128, 128), f32), MR1=V((64, 128), f32), MR2=V((32, 128), f32),
        QF=V((3, 8, SENT + 16, 128), i16), QY=V((8, 80, YHALF), i16), QH=V((8, 48, BLK), i16),
    )
    for name, rows, cols in (("", SENT + 16, 128), ("Y", 80, YHALF), ("H", 48, BLK)):
        scratch["E1" + name] = V((4, 2, rows, cols), i16)
        scratch["E2" + name] = V((4, rows, cols), i16)
        scratch["E3" + name] = V((3, rows, cols), i16)
    for name, rows, cols in (("D", SENT + 16, 128), ("R", SENT + 16, 128), ("V", SENT + 16, 128), ("Y", 80, YHALF), ("H", 48, BLK)):
        scratch["R1" + name] = V((4, 2, rows, cols), i16)
        scratch["R2" + name] = V((4, rows, cols), i16)
        scratch["R3" + name] = V((3, rows, cols), i16)
    if ups_n:
        for i, (rows, cols) in enumerate(((SENT, 128),) * 3 + ((64, YHALF), (32, BLK))):
            scratch["FR%d" % i] = V((ups_n, rows, cols), f32)
        scratch["F"] = V((SENT, YHALF), f32)
        scratch["MF"] = V((ups_n, 32, 128), f32)
        scratch["MFR"] = V((ups_n, 32, 128), f32)
    scratch.update(
        ls=D((16,)), gs=D((5, 3, 6)), gr=D((5, 3, 6)), ms=D((4,)), mr=D((4,)),
        xs=D((11,)), xr=D((11,)), ss=D((5, 16 + ups_n)), sr=D((5, 16 + ups_n)), vs=D((9 + ups_n,)), vr=D((9 + ups_n,)),
    )
    vm, hb = pl.BlockSpec(memory_space=pltpu.VMEM), pl.BlockSpec(memory_space=pl.ANY)
    return pl.pallas_call(
        functools.partial(step_kernel, wide, token_count, n_tok, n_task),
        out_shape=(
            jax.ShapeDtypeStruct((n_tok, LAT), f32),
            jax.ShapeDtypeStruct((3, 8, SENT + 16, 128), i16),
            jax.ShapeDtypeStruct((8, 80, YHALF), i16),
            jax.ShapeDtypeStruct((8, 48, BLK), i16),
            jax.ShapeDtypeStruct((256, 128), f32),
        ),
        in_specs=[hb, vm, vm, vm, hb, vm, vm, vm, vm, hb, hb, vm, vm, vm],
        out_specs=[hb] * 5,
        scratch_shapes=scratch,
        compiler_params=pltpu.CompilerParams(
            collective_id=0, has_side_effects=True, vmem_limit_bytes=64 * 2**20),
    )(lat, actT, ids, steps, tgt, rb, rf, vb, vf, fw, dw, hw, tab, vec)


def adam(master, moment, second, gradient, rate):
    moment_new = moment_decay * moment + (1.0 - moment_decay) * gradient
    second_new = moment_decay * second + (1.0 - moment_decay) * gradient * gradient
    correct = 1.0 - moment_decay**STEP
    normed = moment_new / correct / (jnp.sqrt(second_new / correct) + adam_eps)
    return master - rate * (normed + weight_decay * master), moment_new, second_new


def adam_kernel(qf, qy, qh, fw, fm, fs, dw, dm, ds, hw, hm, hs, ofw, ofm, ofs, odw, odm, ods, ohw, ohm, ohs, gh):
    for j in range(4):
        cols = slice(128 * j, 128 * j + 128)
        g = decode(qf.at[0, j])[0:SHARD, :]
        ofw[:, cols], ofm[:, cols], ofs[:, cols] = adam(fw[:, cols], fm[:, cols], fs[:, cols], g, matrix_rate)
    for j in range(4):
        rows = slice(64 * j, 64 * j + 64)
        odw[rows, :], odm[rows, :], ods[rows, :] = adam(dw[rows, :], dm[rows, :], ds[rows, :], decode(qy.at[j]), matrix_rate)

    @pl.when(pl.program_id(0) == 0)
    def _():
        for k in range(2):
            for j in range(4):
                gh[32 * j : 32 * j + 32, :] = decode(qh.at[4 * k + j])
            new = adam(hw[:, k, :], hm[:, k, :], hs[:, k, :], gh[0:BINS, :], matrix_rate)
            ohw[:, k, :], ohm[:, k, :], ohs[:, k, :] = new


def adam_call(qf, qy, qh, first, dyn, heads):
    fblock = pl.BlockSpec((SHARD, HALF), lambda i: (0, i))
    dblock = pl.BlockSpec((BLK, 128), lambda i: (0, i))
    whole = pl.BlockSpec(heads[0].shape, lambda i: (0, 0, 0))
    out = [jax.ShapeDtypeStruct(a.shape, f32) for a in first + dyn + heads]
    return pl.pallas_call(
        adam_kernel,
        grid=(6,),
        out_shape=out,
        in_specs=[
            pl.BlockSpec((1, 4, SENT + 16, 128), lambda i: (i // 2, i % 2, 0, 0)),
            pl.BlockSpec((4, 80, 128), lambda i: (i // 3, 0, i % 3)),
            pl.BlockSpec(qh.shape, lambda i: (0, 0, 0)),
        ] + [fblock] * 3 + [dblock] * 3 + [whole] * 3,
        out_specs=[fblock] * 3 + [dblock] * 3 + [whole] * 3,
        scratch_shapes=[pltpu.VMEM((128, BLK), f32)],
        compiler_params=pltpu.CompilerParams(vmem_limit_bytes=64 * 2**20),
    )(qf, qy, qh, *first, *dyn, *heads)


def per_device(
    latents, actions, task_ids, steps_left, target_latents, reward_bins, reward_frac, value_bins, value_frac,
    first_weight, first_moment, first_second, dynamics_weight, dynamics_moment, dynamics_second,
    heads_weight, heads_moment, heads_second, task_table, table_moment, table_second,
    vector_params, vector_moment, vector_second,
):
    n_tok = latents.shape[0]
    wide = lax.axis_size("wide")
    token_count = float(HORIZON * n_tok * wide * lax.axis_size("narrow"))
    z = lax.axis_index("narrow")
    n_task = task_table.shape[0]
    n_vec = vector_params.shape[0]
    to_class = lambda a: a.transpose(2, 0, 1)
    lg, qf, qy, qh, misc = step_call(
        wide, token_count, n_task, latents, actions.transpose(1, 2, 0), task_ids,
        steps_left, target_latents.transpose(1, 0, 2),
        reward_bins.T, reward_frac.T, value_bins.T, value_frac.T,
        first_weight, dynamics_weight, to_class(heads_weight), task_table, vector_params)
    new = adam_call(
        qf, qy, qh, [first_weight, first_moment, first_second], [dynamics_weight, dynamics_moment, dynamics_second],
        [to_class(a) for a in (heads_weight, heads_moment, heads_second)])
    heads_new = [a.transpose(1, 2, 0) for a in new[6:]]
    grad_vec = lax.dynamic_slice(misc[0:90].reshape(-1), (n_vec * z,), (n_vec,))
    grad_tab = lax.dynamic_slice(misc, (128 + 32 * z, 0), (n_task, TEMB))
    table_new = adam(task_table, table_moment, table_second, grad_tab, vector_rate)
    vector_new = adam(vector_params, vector_moment, vector_second, grad_vec, vector_rate)
    return (lg, *new[:6], *heads_new, *table_new, *vector_new)


def solution(mesh):
    tokens = ("wide", "narrow")
    in_specs = (
        P(tokens, None), P(tokens, None, None), P(tokens), P(tokens), P(tokens, None, None),
        P(tokens, None), P(tokens, None), P(tokens, None), P(tokens, None),
        *(P("narrow", None),) * 6, *(P(None, "narrow", None),) * 3, *(P("narrow", None),) * 3, *(P("narrow"),) * 3,
    )
    out_specs = (
        P(tokens, None), *(P("narrow", None),) * 6, *(P(None, "narrow", None),) * 3,
        *(P("narrow", None),) * 3, *(P("narrow"),) * 3,
    )
    return jax.shard_map(per_device, mesh=mesh, in_specs=in_specs, out_specs=out_specs, check_vma=False)
```

```python
import functools

import jax
import jax.numpy as jnp
from jax import lax
from jax.experimental import pallas as pl
from jax.experimental.pallas import tpu as pltpu
from jax.sharding import PartitionSpec as P

f32, bf16, i16, i32 = jnp.float32, jnp.bfloat16, jnp.int16, jnp.int32
MESH = pl.DeviceIdType.MESH

LAT = 768
HID = 1024
BINS = 101
TEMB = 96
ACTN = 8
HORIZON = 3
STEP = 5
NZ = 4
SHARD = 218
SENT = 224
BLK = 256
ROWS = 320
RB = 320
NB = ROWS // RB
ALL = HORIZON * ROWS
HALF = HID // 2
YHALF = LAT // 2
BOTT = 112
TASK_LANE = LAT + ACTN - 3 * SHARD
ACT_LANE = LAT - 3 * SHARD

norm_eps = 1e-05
adam_eps = 1e-08
moment_decay = 0.5
horizon_decay = 0.5
weight_decay = 0.01
matrix_rate = 0.03
vector_rate = 0.3
consistency_coef = 20.0
head_coef = 0.1

NN = (((1,), (0,)), ((), ()))
NT = (((1,), (1,)), ((), ()))
TN = (((0,), (0,)), ((), ()))


def dot(a, b, dims=NN):
    return lax.dot_general(a, b, dims, preferred_element_type=f32)


def loop(start, end, body, carry):
    for i in range(start, end):
        carry = body(i, carry)
    return carry


def lanes(n):
    return lax.broadcasted_iota(i32, (1, n), 1)


def block_rows(i, base=0):
    return pl.ds(base + i * RB, RB)


def encode(v, ref):
    rows = v.shape[0]
    top = jnp.max(jnp.abs(v), 0, keepdims=True)
    e = jnp.clip(jnp.ceil(jnp.log2(jnp.maximum(top, 1e-37))), -100.0, 120.0)
    ref[0:rows, :] = jnp.round(v * jnp.exp2(14.9 - e)).astype(i32).astype(i16)
    ref[rows : rows + 16, :] = jnp.broadcast_to(e, (16, v.shape[1])).astype(i32).astype(i16)


def decode(ref):
    rows = ref.shape[0] - 16
    e = ref[rows : rows + 16, :].astype(i32).astype(f32)[0:1, :]
    return ref[0:rows, :].astype(i32).astype(f32) * jnp.exp2(e - 14.9)


def pack_tiles(x):
    inside = lanes(BLK) < SHARD
    b0 = jnp.where(inside, x[:, 0:256], 0.0)
    b1 = jnp.where(inside, pltpu.roll(x[:, 128:512], 384 - 90, 1)[:, 0:256], 0.0)
    b2 = jnp.where(inside, pltpu.roll(x[:, 384:768], 384 - 52, 1)[:, 0:256], 0.0)
    b3 = jnp.where(lanes(128) < ACT_LANE, pltpu.roll(x[:, 640:768], 128 - 14, 1), 0.0)
    return b0, b1, b2, b3


def unpack_tiles(g):
    inside = lanes(BLK) < SHARD
    empty = jnp.zeros((g.shape[0], 128), f32)
    b0 = jnp.where(inside, g[:, 0:256], 0.0)
    b1 = pltpu.roll(jnp.concatenate([jnp.where(inside, g[:, 256:512], 0.0), empty], 1), 90, 1)
    b2 = pltpu.roll(jnp.concatenate([jnp.where(inside, g[:, 512:768], 0.0), empty], 1), 52, 1)
    b3 = pltpu.roll(jnp.where(lanes(128) < ACT_LANE, g[:, 768:896], 0.0), 14, 1)
    return jnp.concatenate(
        [
            b0[:, 0:128],
            b0[:, 128:256] + b1[:, 0:128],
            b1[:, 128:256],
            b1[:, 256:384] + b2[:, 0:128],
            b2[:, 128:256],
            b2[:, 256:384] + b3,
        ],
        1,
    )


def group_sums(x, ones):
    parts = []
    for j in range(0, x.shape[1], 256):
        v = x[:, j : j + 256]
        high = v.astype(bf16)
        low = (v - high.astype(f32)).astype(bf16)
        parts.append(dot(high, ones) + dot(low, ones))
    return jnp.concatenate(parts, 1)


def mish_parts(n):
    u = jnp.exp(jnp.minimum(n, 40.0))
    q = u * (u + 2.0)
    r = 1.0 / (q + 2.0)
    bent = q * r
    return bent, bent + (4.0 * n) * (u * (u + 1.0)) * (r * r)


def add_columns(acc, values):
    for k, v in enumerate(values):
        total = acc[8 * k : 8 * k + 8, :]
        for j in range(v.shape[0] // 8):
            total = total + v[8 * j : 8 * j + 8, :]
        acc[8 * k : 8 * k + 8, :] = total


def rcopy(src, dst, send_sem, recv_sem, device):
    return pltpu.make_async_remote_copy(
        src_ref=src, dst_ref=dst, send_sem=send_sem, recv_sem=recv_sem, device_id=device, device_id_type=MESH
    )


def step_kernel(wide, token_count, n_tok, n_task, lat, actT, ids, steps, tgt, rb, rf, vb, vf, fw, dw, hw, tab, vec,
                lg, qf, qy, qh, misc, **s):
    ups_n = wide.bit_length() - 4
    w, z = lax.axis_index("wide"), lax.axis_index("narrow")
    b0, b1, b2 = lax.rem(w, 2), lax.rem(lax.div(w, 2), 2), lax.rem(lax.div(w, 4), 2)
    pc, p1, p2 = (w + 1 - 2 * b0, z), (w + 2 - 4 * b1, z), (w + 4 - 8 * b2, z)
    zs = [(w, lax.rem(z + d, NZ)) for d in range(NZ)]
    from_z = [lax.rem(z + NZ - d, NZ) for d in range(NZ)]
    ups = []
    for u in range(ups_n):
        bit = 8 << u
        ups.append((w + bit - 2 * bit * lax.rem(lax.div(w, bit), 2), z))
    me = b0 * 4 + b1 * 2 + b2
    own = b1 * 2 + b2
    sends = []

    def pick(odd, even_value, odd_value):
        return even_value + odd * (odd_value - even_value)

    def launch(copy):
        copy.start()
        sends.append(copy)

    X, XT, XTp, U, AT, ATp, DU = s["X"], s["XT"], s["XTp"], s["U"], s["AT"], s["ATp"], s["DU"]
    WF, WD, HT, SM, VEC = s["WF"], s["WD"], s["HT"], s["SM"], s["VEC"]
    PRE, ACT, TT = s["PRE"], s["ACT"], s["TT"]
    TU, TS = TT.at[pl.ds(0, ROWS)], TT.at[pl.ds(ROWS, ROWS)]
    GP, GPp, GDL, GDLp = s["GP"], s["GPp"], s["GDL"], s["GDLp"]
    INV, SIDE, SD, ONES, VA, VT, GEMB = (
        s["INV"], s["SIDE"], s["SD"], s["ONES"], s["VA"], s["VT"], s["GEMB"])

    barrier = pltpu.get_barrier_semaphore()
    peers = [pc, p1, p2] + zs[1:] + ups
    for p in peers:
        pl.semaphore_signal(barrier, inc=1, device_id=p, device_id_type=MESH)

    STG = s["STG"]
    loads = []

    def load_first(part):
        return pltpu.make_async_copy(
            fw.at[:, pl.ds(HALF * part, HALF)], STG.at[part % 2], s["ls"].at[part % 2])

    loads.append(pltpu.make_async_copy(dw, DU.at[pl.ds(0, BLK)], s["ls"].at[3]))
    loads.append(pltpu.make_async_copy(lat, GDL.at[pl.ds(0, n_tok)], s["ls"].at[4]))
    load_first(0).start()
    load_first(1).start()
    for c in loads:
        c.start()

    def cast_first(br):
        for part in (2 * br, 2 * br + 1):
            load_first(part).wait()
            rows = jnp.concatenate([STG[part % 2].astype(bf16), jnp.zeros((SENT - SHARD, HALF), bf16)], 0)
            WF[pl.ds(pl.multiple_of(BLK * z, BLK), SENT), HALF * part : HALF * part + HALF] = rows
            if part < 4:
                load_first(part + 2).start()

    cast_first(0)
    pl.semaphore_wait(barrier, len(peers))

    gs, gr = s["gs"], s["gr"]

    class Item:
        def __init__(self, index, view):
            self.i, self.view = index, view

        def _recv(self, d, kind, view):
            rcopy(view, view, gs.at[self.i, d - 1, kind], gr.at[self.i, d - 1, kind], pc).wait_recv()

        def _send(self, d, kind, view, device):
            launch(rcopy(view, view, gs.at[self.i, d - 1, kind], gr.at[self.i, d - 1, kind], device))

        def start(self):
            for d in (1, 3, 2):
                self._send(d, 0, self.view(z, me, 1, None), zs[d])

        def spread(self, *ds):
            for d in ds or (1, 3, 2):
                mine = self.view(from_z[d], me, 1, None)
                self._recv(d, 0, mine)
                self._send(d, 1, mine, p1)
                self._send(d, 2, mine, p2)

        def forward(self, *ds):
            s1, s2 = me + 2 - 4 * b1, me + 1 - 2 * b2
            for d in ds or (1, 3, 2):
                q = from_z[d]
                self._recv(d, 1, self.view(q, s1, 1, None))
                self._send(d, 3, self.view(q, s1, 1, 0), p2)
                self._recv(d, 2, self.view(q, s2, 1, None))
                self._send(d, 4, self.view(q, s2, 1, 1), p1)

        def cross(self, *ds):
            s12 = 4 * b0 + 3 - own
            for d in ds or (1, 3, 2):
                q = from_z[d]
                self._recv(d, 3, self.view(q, s12, 1, 0))
                self._recv(d, 4, self.view(q, s12, 1, 1))
                self._send(d, 5, self.view(q, 4 * b0, 4, None), pc)

        def finish(self):
            for d in (1, 3, 2):
                self._recv(d, 5, self.view(from_z[d], 4 - 4 * b0, 4, None))

    def first_view(br):
        def view(q, at, n, half):
            lo, size = (0, SENT) if half is None else (BOTT * half, BOTT)
            return WF.at[pl.ds(pl.multiple_of(BLK * q + lo, 16), size), pl.ds(pl.multiple_of(HID * br + 128 * at, 128), 128 * n)]
        return view

    def dyn_view(q, at, n, half):
        lo, size = (0, 32 * n) if half is None else (16 * half, 16)
        return WD.at[pl.ds(pl.multiple_of(BLK * q + 32 * at + lo, 16), size)]

    def heads_view(q, at, n, half):
        cols = pl.ds(pl.multiple_of(BLK * q, BLK), BLK)
        rows = pl.ds(pl.multiple_of(16 * at, 16), 16 * n)
        if half is None:
            return HT.at[:, rows, cols]
        return HT.at[pl.ds(half, 1), rows, cols]

    gD, gY, gR, gV, gH = (
        Item(0, first_view(0)), Item(1, dyn_view), Item(2, first_view(1)), Item(3, first_view(2)), Item(4, heads_view))

    def vec_rows():
        n_vec = vec.shape[0]
        whole = n_vec // 128
        VR = s["VR"]
        VR[...] = jnp.zeros_like(VR)
        for r in range(whole):
            VR[r + 1 : r + 2, :] = vec[pl.ds(128 * r, 128)].reshape(1, 128)
        left = n_vec - 128 * whole
        VR[whole + 1 : whole + 2, 0:left] = vec[pl.ds(128 * whole, left)].reshape(1, left)
        plain = VR[1:33, :]
        moved = jnp.where(lanes(128) < 64, pltpu.roll(VR[0:32, :], 64, 1), pltpu.roll(plain, 64, 1))
        return jnp.where(lax.rem(z, 2) == 1, moved, plain).astype(bf16)

    gD.start()
    frame = vec_rows()
    SM[z, 0:32, :] = frame
    SM[z, 32:64, :] = jnp.zeros((32, 128), bf16)
    SM[z, 32 : 32 + n_task, 0:TEMB] = tab[...].astype(bf16)
    for d in (1, 3, 2):
        launch(rcopy(SM.at[z], SM.at[z], s["ms"].at[d], s["mr"].at[d], zs[d]))
    loads[0].wait()
    WD[pl.ds(pl.multiple_of(BLK * z, BLK), BLK), :] = DU[0:BLK, :].astype(bf16)
    gY.start()
    cast_first(1)
    gR.start()
    gD.spread(1, 3)
    own_cols = pl.ds(pl.multiple_of(BLK * z, BLK), BLK)
    for k in range(2):
        PRE[0:128, 0:BLK] = jnp.zeros((128, BLK), f32)
        PRE[0:BINS, 0:BLK] = hw[:, k, :]
        HT[k, :, own_cols] = PRE[0:128, 0:BLK].astype(bf16)
    gH.start()
    gD.spread(2)
    cast_first(2)
    gV.start()

    GDL[n_tok:ROWS, :] = jnp.zeros((ROWS - n_tok, LAT), bf16)
    for q in range(NZ):
        WF[BLK * q + SENT : BLK * q + BLK, :] = jnp.zeros((BLK - SENT, 3 * HID), bf16)
    loads[1].wait()

    def pack_latents(i, c):
        rows = block_rows(i)
        b = pack_tiles(GDL[rows, :].astype(f32))
        X[rows, 0:896] = jnp.concatenate(b, 1).astype(bf16)
        return c

    loop(0, NB, pack_latents, 0)
    gD.forward(1, 3)
    gY.spread(1, 3)
    idr = s["IDR"]
    idr[...] = jnp.full_like(idr, -1)
    idr[0:1, 0:n_tok] = ids[...].reshape(1, n_tok)
    slot = lax.broadcasted_iota(i32, (128, 1), 0)
    task = jnp.where(slot % 32 < n_task, n_task * (slot // 32) + slot % 32, -2)
    PKT = s["PKT"]
    PKT[...] = jnp.where(idr[0:1, 0:ROWS] == task, 1.0, 0.0).astype(bf16)
    gD.forward(2)
    gY.spread(2)
    gD.cross(1, 3)

    for d in (1, 3, 2):
        q = from_z[d]
        rcopy(SM.at[q], SM.at[q], s["ms"].at[d], s["mr"].at[d], pc).wait_recv()
    full = s["VFULL"]
    full[...] = jnp.zeros_like(full)
    for q, at in enumerate((0, 22, 45, 67)):
        full[at : at + 24, :] = full[at : at + 24, :] + SM[q, 0:32, :].astype(f32)[0:24, :]
    for r in range(12):
        n, first = (8, 8 * r) if r < 9 else (6, 72 + 6 * (r - 9))
        for j in range(n):
            VEC[r : r + 1, 128 * j : 128 * j + 128] = full[first + j : first + j + 1, :]
    place = jnp.concatenate([SM[q, 32:64, :] for q in range(NZ)], 0).astype(f32)
    table = pltpu.roll(jnp.concatenate([place, jnp.zeros_like(place)], 1), TASK_LANE, 1).astype(bf16)
    AC = s["AC"]
    AC[...] = jnp.zeros_like(AC)
    act_to = jnp.where(
        lax.broadcasted_iota(i32, (16, BLK), 0) + ACT_LANE == lax.broadcasted_iota(i32, (16, BLK), 1), 1.0, 0.0
    ).astype(bf16)
    rows_of_task = dot(PKT[...], table, TN)
    gD.cross(2)
    for t in range(3):
        AC[0:ACTN, 0:n_tok] = actT[t].astype(f32)
        SD[t] = (rows_of_task + dot(AC[:, 0:ROWS].astype(bf16), act_to, TN)).astype(bf16)

    def side_block(t, dest):
        X[dest : dest + ROWS, 768:896] = (X[dest : dest + ROWS, 768:896].astype(f32) + SD[t, :, 0:128].astype(f32)).astype(bf16)
        X[dest : dest + ROWS, 896:1024] = SD[t, :, 128:256]

    side_block(0, 0)
    gY.forward(1, 3)

    def later_setup():
        tile = lax.broadcasted_iota(i32, (256, 256), 0) // 8 == lax.broadcasted_iota(i32, (256, 256), 1) // 8
        ONES[...] = jnp.where(tile, 1.0, 0.0).astype(bf16)
        st = s["ST"]
        st[...] = jnp.zeros_like(st)
        st[0:1, 0:n_tok] = steps[...].reshape(1, n_tok).astype(f32)
        for k, ref in enumerate((rb, rf, vb, vf)):
            st[8 * k + 8 : 8 * k + 11, 0:n_tok] = ref[...].astype(f32)
        SIDE[...] = st[...].T[0:ROWS, :]
        for ref in (VA, VT, GEMB, s["DWH"], s["MS"]):
            ref[...] = jnp.zeros_like(ref)

    gD.finish()

    def matmul(out, orows, n, width, left, right, dims=NN):
        def tile_step(j, c):
            cols = pl.ds(j * width, width)
            out[orows, cols] = dot(left, right(cols), dims)
            return c
        loop(0, n // width, tile_step, 0)

    def first_forward(br, base):
        def tile_step(j, c):
            cols = pl.ds(j * 512, 512)
            from_cols = pl.ds(HID * br + j * 512, 512)
            PRE[:, cols] = dot(X[pl.ds(base, ROWS), :], WF[:, from_cols])
            return c
        loop(0, 2, tile_step, 0)

    def norm_mish(br, unit, inv, unit_base, slope):
        bias, gain, shift = (VEC[3 * br + k : 3 * br + k + 1, :] for k in range(3))

        def step(i, c):
            rows = block_rows(i)
            p = PRE[rows, :] + bias
            ce = p - jnp.mean(p, -1, keepdims=True)
            iv = lax.rsqrt(jnp.mean(ce * ce, -1, keepdims=True) + norm_eps)
            un = ce * iv
            n = un * gain + shift
            bent, sl = mish_parts(n)
            ACT[rows, :] = (n * bent).astype(bf16)
            if slope is not None:
                slope[rows, :] = sl
            unit[block_rows(i, unit_base), :] = un
            inv[block_rows(i, unit_base), :] = jnp.broadcast_to(iv, (RB, 128))
            return c
        loop(0, NB, step, 0)

    def dyn_forward(t, between):
        base = ROWS * t
        first_forward(0, base)
        between(0)
        norm_mish(0, U, INV, base, None)
        between(1)
        matmul(TU, pl.ds(0, ROWS), LAT, 384, ACT[...], lambda cols: WD[:, cols])
        AT[:, base : base + ROWS] = ACT[...].T
        bias, gain, shift = (VEC[9 + k : 10 + k, 0:LAT] for k in range(3))

        def step(i, c):
            rows, at = block_rows(i), block_rows(i, base)
            p = TU[rows, 0:LAT] + bias
            ce = p - jnp.mean(p, -1, keepdims=True)
            iv = lax.rsqrt(jnp.mean(ce * ce, -1, keepdims=True) + norm_eps)
            un = ce * iv
            DU[at, :] = un
            INV[at, 64:128] = jnp.broadcast_to(iv, (RB, 64))
            if t < 2:
                e = jnp.exp(un * gain + shift)
                b = pack_tiles(e / group_sums(e, ONES[...]))
                X[block_rows(i, base + ROWS), 0:896] = jnp.concatenate(b, 1).astype(bf16)
            return c
        loop(0, NB, step, 0)
        if t < 2:
            side_block(t + 1, base + ROWS)

    def between_0(at):
        if at == 0:
            gY.forward(2)
        else:
            gY.cross()
            gR.spread()
            later_setup()
            gY.finish()

    def between_1(at):
        if at == 1:
            gR.forward()

    def between_2(at):
        if at == 1:
            gH.cross()

    dyn_forward(0, between_0)
    gH.spread()
    dyn_forward(1, between_1)
    gR.cross()
    gH.forward()
    gV.spread()
    dyn_forward(2, between_2)
    XT[...] = X[...].T
    xs, xr = s["xs"], s["xr"]
    launch(rcopy(XT, XTp, xs.at[0], xr.at[0], pc))
    launch(rcopy(AT, ATp, xs.at[1], xr.at[1], pc))
    gR.finish()
    gH.finish()
    gV.forward()

    def norm_backward(br, unit, inv, unit_base, slope, out_base):
        gain, shift = VEC[3 * br + 1 : 3 * br + 2, :], VEC[3 * br + 2 : 3 * br + 3, :]
        acc = VA.at[br]

        def step(i, c):
            rows, at = block_rows(i), block_rows(i, unit_base)
            un = unit[at, :]
            sl = mish_parts(un * gain + shift)[1] if slope is None else slope[rows, :]
            gn = PRE[rows, :] * sl
            h = gn * gain
            gp = (h - jnp.mean(h, -1, keepdims=True) - un * jnp.mean(h * un, -1, keepdims=True)) * inv[at, 0:1]
            GP[block_rows(i, out_base), HID * br : HID * br + HID] = gp.astype(bf16)
            add_columns(acc, (gp, gn * un, gn))
            return c
        loop(0, NB, step, 0)

    def head_step(k, t):
        base = ROWS * t
        first_forward(1 + k, base)
        norm_mish(1 + k, TU, s["HINV"], 0, TS)
        logits = dot(ACT[...], HT[k], NT)
        real = lanes(128) < BINS
        logits = jnp.where(real, logits, -1e30)
        e = jnp.exp(logits - jnp.max(logits, -1, keepdims=True))
        soft = e / jnp.sum(e, -1, keepdims=True)
        side = SIDE[...]
        c0 = 8 + 16 * k + t
        at, frac = side[:, c0 : c0 + 1], side[:, c0 + 8 : c0 + 9]
        level = lanes(128).astype(f32)
        hot = jnp.where(level == at, 1.0 - frac, 0.0) + jnp.where(level == at + 1.0, frac, 0.0)
        weight = jnp.where(side[:, 0:1] > t, f32(horizon_decay**t), 0.0) / token_count
        gl = jnp.where(real, weight * head_coef * (soft - hot), 0.0).astype(bf16)
        s["DWH"][k] = s["DWH"][k] + dot(gl.astype(f32).T.astype(bf16), ACT[...])
        PRE[...] = dot(gl, HT[k])
        norm_backward(1 + k, TU, s["HINV"], 0, TS, base)

    def dyn_backward(t, between=None):
        base = ROWS * t
        gain, shift = VEC[10:11, 0:LAT], VEC[11:12, 0:LAT]
        scale = 2.0 * consistency_coef / LAT

        def step(i, c):
            rows, at = block_rows(i), block_rows(i, base)
            un = DU[at, :]
            e = jnp.exp(un * gain + shift)
            sx = e / group_sums(e, ONES[...])
            weight = jnp.where(SIDE[rows, 0:1] > t, f32(horizon_decay**t), 0.0) / token_count
            g = weight * scale * (sx - X[at, 0:LAT].astype(f32))
            if t < 2:
                g = g + unpack_tiles(PRE[rows, 0:896])
            gn = sx * (g - group_sums(g * sx, ONES[...]))
            h = gn * gain
            gp = (h - jnp.mean(h, -1, keepdims=True) - un * jnp.mean(h * un, -1, keepdims=True)) * INV[at, 64:65]
            GDL[at, :] = gp.astype(bf16)
            add_columns(VT, (gp, gn * un, gn))
            return c
        loop(0, NB, step, 0)
        yc = pl.ds(pl.multiple_of(YHALF * (1 - b0), 128), YHALF)
        launch(rcopy(GDL.at[pl.ds(base, ROWS), yc], GDLp.at[pl.ds(base, ROWS)], xs.at[4 + t], xr.at[4 + t], pc))
        if between is not None:
            between()

        def tile_step(j, c):
            cols = pl.ds(j * 512, 512)
            PRE[:, cols] = dot(GDL[pl.ds(base, ROWS), :], WD[cols, :], NT)
            return c
        loop(0, 2, tile_step, 0)
        norm_backward(0, U, INV, base, None, base)
        gc = pl.ds(pl.multiple_of(HALF * (1 - b0), HALF), HALF)
        launch(rcopy(GP.at[pl.ds(base, ROWS), gc], GPp.at[0, pl.ds(base, ROWS)], xs.at[7 + t], xr.at[7 + t], pc))

    def inputs_backward(t):
        base = ROWS * t

        def tile_step(j, c):
            cols = pl.ds(j * 512, 512)
            PRE[:, cols] = dot(GP[pl.ds(base, ROWS), :], WF[cols, :], NT)
            return c
        loop(0, 2, tile_step, 0)
        GEMB[...] = GEMB[...] + PRE[:, 768:1024]

    rs_s, rs_r = s["ss"], s["sr"]

    class Stream:
        def __init__(self, index, grad, view, E, R, Q, half):
            self.i, self.grad, self.view, self.Q, self.half = index, grad, view, Q, half
            (self.E1, self.E2, self.E3), (self.R1, self.R2, self.R3) = E, R
            self.held = {}

        def _copy(self, at, src, dst, device):
            return rcopy(src, dst, rs_s.at[self.i, at], rs_r.at[self.i, at], device)

        def _send(self, at, src, dst, device):
            c = self._copy(at, src, dst, device)
            c.start()
            self.held[at] = c

        def _recv(self, at, dst):
            self._copy(at, dst, dst, pc).wait_recv()

        def release(self):
            for c in self.held.values():
                c.wait_send()
            self.held = {}

        def stage1(self):
            for d in (2, 1, 3, 0):
                q = zs[d][1]
                odd = lax.rem(q, 2)
                base = pick(odd, 2 - 2 * b1, 1 - b2)
                for j in range(2):
                    encode(self.grad[self.view(q, base + j * (1 + odd))], self.E1.at[q, j])
                self._send(d, self.E1.at[q], self.R1.at[q], (pick(odd, p1[0], p2[0]), z))

        def stage2(self, *ds):
            for d in ds or (2, 1, 3, 0):
                q = zs[d][1]
                odd = lax.rem(q, 2)
                self._recv(d, self.R1.at[q])
                keep = pick(odd, b2, b1)
                other = pick(odd, own + 1 - 2 * b2, own + 2 - 4 * b1)
                encode(self.grad[self.view(q, other)] + decode(self.R1.at[q, 1 - keep]), self.E2.at[q])
                self._send(4 + d, self.E2.at[q], self.R2.at[q], (pick(odd, p2[0], p1[0]), z))
                mine = self.view(q, own)
                self.grad[mine] = self.grad[mine] + decode(self.R1.at[q, keep])

        def stage3(self, *ds):
            for d in ds or (2, 1, 3):
                q = zs[d][1]
                self._recv(4 + d, self.R2.at[q])
                encode(self.grad[self.view(q, own)] + decode(self.R2.at[q]), self.E3.at[d - 1])
                self._send(7 + d, self.E3.at[d - 1], self.R3.at[d - 1], zs[d])

        def stage4(self):
            self._recv(4, self.R2.at[z])
            total = self.grad[self.view(z, own)] + decode(self.R2.at[z])
            for d in (1, 3, 2):
                self._recv(7 + d, self.R3.at[d - 1])
                total = total + decode(self.R3.at[d - 1])
            for u in range(ups_n):
                rows, cols = total.shape
                F, FR = s["F"].at[pl.ds(0, rows), pl.ds(0, cols)], s["FR%d" % self.i]
                F[...] = total
                self._send(16 + u, F, FR.at[u], ups[u])
                self._recv(16 + u, FR.at[u])
                self.held.pop(16 + u).wait_send()
                total = total + FR[u]
            encode(total, self.Q.at[me])
            self._send(11, self.Q.at[me], self.Q.at[me], p1)
            self._send(12, self.Q.at[me], self.Q.at[me], p2)

        def stage5(self):
            s1, s2 = me + 2 - 4 * b1, me + 1 - 2 * b2
            n = self.Q.shape[1]
            low, high = pl.ds(0, self.half), pl.ds(self.half, n - self.half)
            self._recv(11, self.Q.at[s1])
            self._send(13, self.Q.at[s1, low], self.Q.at[s1, low], p2)
            self._recv(12, self.Q.at[s2])
            self._send(14, self.Q.at[s2, high], self.Q.at[s2, high], p1)

        def stage6(self):
            s12 = 4 * b0 + 3 - own
            n = self.Q.shape[1]
            low, high = pl.ds(0, self.half), pl.ds(self.half, n - self.half)
            self._recv(13, self.Q.at[s12, low])
            self._recv(14, self.Q.at[s12, high])
            mine = self.Q.at[pl.ds(4 * b0, 4)]
            self._send(15, mine, mine, pc)

        def stage7(self, out, sem):
            self._recv(15, self.Q.at[pl.ds(4 - 4 * b0, 4)])
            c = pltpu.make_async_copy(self.Q, out, sem)
            c.start()
            return c

    def first_slice(q, at):
        return (pl.ds(pl.multiple_of(BLK * q, BLK), SENT), pl.ds(pl.multiple_of(128 * at, 128), 128))

    def value_slice(q, at):
        cols = HALF * lax.div(q, 2) + 128 * at
        return (pl.ds(pl.multiple_of(BLK * lax.rem(q, 2), BLK), SENT), pl.ds(pl.multiple_of(cols, 128), 128))

    def y_slice(q, at):
        return (pl.ds(pl.multiple_of(BLK * q + 64 * at, 64), 64), slice(None))

    def h_slice(q, at):
        return (b0, pl.ds(pl.multiple_of(32 * at, 32), 32), pl.ds(pl.multiple_of(BLK * q, BLK), BLK))

    EF = (s["E1"], s["E2"], s["E3"])
    streams = []
    for i, name in enumerate("DRV"):
        streams.append(Stream(
            i, *((TT, value_slice) if name == "V" else (s["DWA"], first_slice)), EF,
            tuple(s["R%d%s" % (k, name)] for k in (1, 2, 3)), s["QF"].at[i], 128))
    sD, sR, sV = streams
    sY = Stream(3, s["DWY"], y_slice, tuple(s["E%dY" % k] for k in (1, 2, 3)),
                tuple(s["R%dY" % k] for k in (1, 2, 3)), s["QY"], 48)
    sH = Stream(4, s["DWH"], h_slice, tuple(s["E%dH" % k] for k in (1, 2, 3)),
                tuple(s["R%dH" % k] for k in (1, 2, 3)), s["QH"], 32)

    def send_half(br):
        cols = pl.ds(pl.multiple_of(HID * br + HALF * (1 - b0), HALF), HALF)
        launch(rcopy(GP.at[:, cols], GPp.at[br], xs.at[1 + br], xr.at[1 + br], pc))

    def wait_x(at, dst):
        rcopy(dst, dst, xs.at[at], xr.at[at], pc).wait_recv()

    def weight_grad(out, n, left, right, left2, right2):
        def tile_step(j, c):
            cols = pl.ds(pl.multiple_of(j * n, n), n)
            out[:, cols] = dot(left[...], right(j)) + dot(left2[...], right2(cols))
            return c
        lax.fori_loop(0, out.shape[1] // n, tile_step, 0)

    def first_grad(br, out):
        weight_grad(
            out, 256, XT,
            lambda j: GP[:, pl.ds(pl.multiple_of(HID * br + HALF * b0 + 256 * j, 256), 256)],
            XTp, lambda cols: GPp[br, :, cols])

    def value_grad():
        def tile_step(j, c):
            cols = pl.ds(pl.multiple_of(j * 256, 256), 256)
            low_cols = pl.ds(pl.multiple_of(HALF + j * 256, 256), 256)
            right = GP[:, pl.ds(pl.multiple_of(2 * HID + HALF * b0 + 256 * j, 256), 256)]
            total = dot(XT[...], right) + dot(XTp[...], GPp[2, :, cols])
            TT[0:512, cols] = total[0:512, :]
            TT[0:512, low_cols] = total[512:1024, :]
            return c
        lax.fori_loop(0, 2, tile_step, 0)

    def y_grad():
        wait_x(1, ATp)
        for t in range(3):
            wait_x(4 + t, GDLp.at[pl.ds(ROWS * t, ROWS)])
        weight_grad(
            s["DWY"], 128, AT,
            lambda j: GDL[:, pl.ds(pl.multiple_of(YHALF * b0 + 128 * j, 128), 128)],
            ATp, lambda cols: GDLp[:, cols])
        sY.stage1()

    head_step(0, 0)
    gV.cross()
    head_step(0, 1)
    head_step(0, 2)
    send_half(1)
    gV.finish()
    head_step(1, 0)
    wait_x(0, XTp)
    wait_x(2, GPp.at[1])
    first_grad(1, s["DWA"])
    sR.stage1()
    head_step(1, 1)
    head_step(1, 2)
    send_half(2)
    launch(rcopy(s["DWH"].at[1 - b0], s["DWHp"], xs.at[10], xr.at[10], pc))
    for t in range(3):
        loads.append(pltpu.make_async_copy(
            tgt.at[t], X.at[pl.ds(ROWS * t, n_tok), pl.ds(0, LAT)], s["ls"].at[5 + t]))
        loads[-1].start()
    sR.stage2()
    for c in loads[2:]:
        c.wait()
    dyn_backward(2)
    sR.stage3()
    wait_x(3, GPp.at[2])
    value_grad()
    sR.release()
    sV.stage1()
    inputs_backward(2)
    wait_x(10, s["DWHp"])
    s["DWH"][b0] = s["DWH"][b0] + s["DWHp"][...]
    sH.stage1()
    dyn_backward(1)
    sR.stage4()
    sV.stage2()
    sH.stage2()
    inputs_backward(1)
    sR.stage5()
    dyn_backward(0, y_grad)
    sV.stage3()
    sH.stage3()
    for t in range(3):
        wait_x(7 + t, GPp.at[0, pl.ds(ROWS * t, ROWS)])
    first_grad(0, s["DWA"])
    sV.release()
    sD.stage1()
    sR.stage6()
    inputs_backward(0)

    def write_latent(i, c):
        rows = block_rows(i)
        DU[rows, :] = unpack_tiles(PRE[rows, 0:896])
        return c
    loop(0, NB, write_latent, 0)
    lg_copy = pltpu.make_async_copy(DU.at[pl.ds(0, n_tok)], lg, s["ls"].at[8])
    lg_copy.start()
    ge = GEMB[...]
    g1 = ge.astype(bf16)
    g2 = (ge - g1.astype(f32)).astype(bf16)
    g3 = (ge - g1.astype(f32) - g2.astype(f32)).astype(bf16)
    pk = PKT[...]
    by_task = dot(pk, g1) + dot(pk, g2) + dot(pk, g3)
    M = s["MS"]
    M[128:256, :] = pltpu.roll(by_task, BLK - TASK_LANE, 1)[:, 0:128]
    for r in range(12):
        acc, n, first = (VA.at[r // 3], 8, 8 * r) if r < 9 else (VT, 6, 72 + 6 * (r - 9))
        k = r % 3
        row = jnp.sum(acc[8 * k : 8 * k + 8, :], 0, keepdims=True)
        for j in range(n):
            M[first + j : first + j + 1, :] = row[:, 128 * j : 128 * j + 128]

    vs, vr = s["vs"], s["vr"]

    def small(at, src, dst, device):
        return rcopy(src, dst, vs.at[at], vr.at[at], device)

    def rows_of(start, n):
        return pl.ds(pl.multiple_of(start, 32), n)

    halves = ((0, pc, b0, 128), (1, p1, b1, 64), (2, p2, b2, 32))

    def halve(step, start):
        at, device, bit, n = halves[step]
        launch(small(at, M.at[rows_of(start + n * (1 - bit), n)], s["MR%d" % step], device))

    def halved(step, start):
        at, device, bit, n = halves[step]
        small(at, s["MR%d" % step], s["MR%d" % step], device).wait_recv()
        mine = rows_of(start + n * bit, n)
        M[mine, :] = M[mine, :] + s["MR%d" % step][...]
        return start + n * bit

    halve(0, 0)
    sY.stage2()
    at = halved(0, 0)
    halve(1, at)
    sV.stage4()
    sH.stage4()
    at = halved(1, at)
    halve(2, at)
    sD.stage2(2, 1)
    sY.stage3()
    sD.stage2(3, 0)
    at = halved(2, at)
    MZ = s["MZ"]
    MZ[z] = M[rows_of(at, 32), :]
    for d in (2, 1, 3):
        launch(small(2 + d, MZ.at[z], MZ.at[z], zs[d]))
    sV.stage5()
    sH.stage5()
    sD.stage3()
    sY.stage4()
    for d in (1, 3, 2):
        small(2 + d, MZ.at[from_z[d]], MZ.at[from_z[d]], pc).wait_recv()
    total = (MZ[0] + MZ[1]) + (MZ[2] + MZ[3])
    for u in range(ups_n):
        s["MF"][u] = total
        launch(small(9 + u, s["MF"].at[u], s["MFR"].at[u], ups[u]))
        small(9 + u, s["MFR"].at[u], s["MFR"].at[u], ups[u]).wait_recv()
        total = total + s["MFR"][u]
    MO = s["MO"]
    MO[rows_of(at, 32), :] = total
    launch(small(6, MO.at[rows_of(at, 32)], MO.at[rows_of(at, 32)], p2))
    sV.stage6()
    sH.stage6()
    outs = [lg_copy]
    outs.append(sR.stage7(qf.at[1], s["ls"].at[9]))
    sY.stage5()
    o = at + 32 - 64 * b2
    small(6, MO.at[rows_of(o, 32)], MO.at[rows_of(o, 32)], p2).wait_recv()
    at = at - 32 * b2
    launch(small(7, MO.at[rows_of(at, 64)], MO.at[rows_of(at, 64)], p1))
    sD.stage4()
    sY.stage6()
    o = at + 64 - 128 * b1
    small(7, MO.at[rows_of(o, 64)], MO.at[rows_of(o, 64)], p1).wait_recv()
    at = at - 64 * b1
    launch(small(8, MO.at[rows_of(at, 128)], MO.at[rows_of(at, 128)], pc))
    outs.append(sV.stage7(qf.at[2], s["ls"].at[10]))
    outs.append(sH.stage7(qh, s["ls"].at[11]))
    sD.stage5()
    outs.append(sY.stage7(qy, s["ls"].at[12]))
    o = at + 128 - 256 * b0
    small(8, MO.at[rows_of(o, 128)], MO.at[rows_of(o, 128)], pc).wait_recv()
    c = pltpu.make_async_copy(MO, misc, s["ls"].at[13])
    c.start()
    outs.append(c)
    sD.stage6()
    outs.append(sD.stage7(qf.at[0], s["ls"].at[14]))
    for c in outs:
        c.wait()
    for st in (sD, sR, sV, sY, sH):
        st.release()
    for c in sends:
        c.wait_send()


def step_call(wide, token_count, n_task, lat, actT, ids, steps, tgt, rb, rf, vb, vf, fw, dw, hw, tab, vec):
    n_tok = lat.shape[0]
    ups_n = wide.bit_length() - 4
    V = pltpu.VMEM
    D = pltpu.SemaphoreType.DMA
    scratch = dict(
        WF=V((HID, 3 * HID), bf16), WD=V((HID, LAT), bf16), HT=V((2, 128, HID), bf16),
        SM=V((NZ, 64, 128), bf16), VR=V((40, 128), f32), VEC=V((16, HID), f32), VFULL=V((96, 128), f32),
        X=V((ALL, HID), bf16), XT=V((HID, ALL), bf16), XTp=V((HID, ALL), bf16),
        U=V((ALL, HID), f32), AT=V((HID, ALL), bf16), ATp=V((HID, ALL), bf16),
        DU=V((ALL, LAT), f32),
        PRE=V((ROWS, HID), f32), TT=V((2 * ROWS, HID), f32), ACT=V((ROWS, HID), bf16),
        GP=V((ALL, 3 * HID), bf16), GPp=V((3, ALL, HALF), bf16), GDL=V((ALL, LAT), bf16), GDLp=V((ALL, YHALF), bf16),
        INV=V((ALL, 128), f32), HINV=V((ROWS, 128), f32),
        SIDE=V((ROWS, 40), f32), SD=V((3, ROWS, BLK), bf16), ONES=V((256, 256), bf16),
        VA=V((3, 24, HID), f32), VT=V((24, LAT), f32), GEMB=V((ROWS, BLK), f32),
        ST=V((40, 384), f32), IDR=V((8, 384), i32), PKT=V((128, ROWS), bf16), AC=V((16, 384), f32),
        DWA=V((HID, HALF), f32), DWY=V((HID, YHALF), f32), STG=V((2, SHARD, HALF), f32),
        DWH=V((2, 128, HID), f32), DWHp=V((128, HID), f32),
        MS=V((256, 128), f32), MO=V((256, 128), f32), MZ=V((NZ, 32, 128), f32),
        MR0=V((128, 128), f32), MR1=V((64, 128), f32), MR2=V((32, 128), f32),
        QF=V((3, 8, SENT + 16, 128), i16), QY=V((8, 80, YHALF), i16), QH=V((8, 48, BLK), i16),
    )
    for name, rows, cols in (("", SENT + 16, 128), ("Y", 80, YHALF), ("H", 48, BLK)):
        scratch["E1" + name] = V((4, 2, rows, cols), i16)
        scratch["E2" + name] = V((4, rows, cols), i16)
        scratch["E3" + name] = V((3, rows, cols), i16)
    for name, rows, cols in (("D", SENT + 16, 128), ("R", SENT + 16, 128), ("V", SENT + 16, 128), ("Y", 80, YHALF), ("H", 48, BLK)):
        scratch["R1" + name] = V((4, 2, rows, cols), i16)
        scratch["R2" + name] = V((4, rows, cols), i16)
        scratch["R3" + name] = V((3, rows, cols), i16)
    if ups_n:
        for i, (rows, cols) in enumerate(((SENT, 128),) * 3 + ((64, YHALF), (32, BLK))):
            scratch["FR%d" % i] = V((ups_n, rows, cols), f32)
        scratch["F"] = V((SENT, YHALF), f32)
        scratch["MF"] = V((ups_n, 32, 128), f32)
        scratch["MFR"] = V((ups_n, 32, 128), f32)
    scratch.update(
        ls=D((16,)), gs=D((5, 3, 6)), gr=D((5, 3, 6)), ms=D((4,)), mr=D((4,)),
        xs=D((11,)), xr=D((11,)), ss=D((5, 16 + ups_n)), sr=D((5, 16 + ups_n)), vs=D((9 + ups_n,)), vr=D((9 + ups_n,)),
    )
    vm, hb = pl.BlockSpec(memory_space=pltpu.VMEM), pl.BlockSpec(memory_space=pl.ANY)
    return pl.pallas_call(
        functools.partial(step_kernel, wide, token_count, n_tok, n_task),
        out_shape=(
            jax.ShapeDtypeStruct((n_tok, LAT), f32),
            jax.ShapeDtypeStruct((3, 8, SENT + 16, 128), i16),
            jax.ShapeDtypeStruct((8, 80, YHALF), i16),
            jax.ShapeDtypeStruct((8, 48, BLK), i16),
            jax.ShapeDtypeStruct((256, 128), f32),
        ),
        in_specs=[hb, vm, vm, vm, hb, vm, vm, vm, vm, hb, hb, vm, vm, vm],
        out_specs=[hb] * 5,
        scratch_shapes=scratch,
        compiler_params=pltpu.CompilerParams(
            collective_id=0, has_side_effects=True, vmem_limit_bytes=64 * 2**20),
    )(lat, actT, ids, steps, tgt, rb, rf, vb, vf, fw, dw, hw, tab, vec)


def adam(master, moment, second, gradient, rate):
    moment_new = moment_decay * moment + (1.0 - moment_decay) * gradient
    second_new = moment_decay * second + (1.0 - moment_decay) * gradient * gradient
    correct = 1.0 - moment_decay**STEP
    normed = moment_new / correct / (jnp.sqrt(second_new / correct) + adam_eps)
    return master - rate * (normed + weight_decay * master), moment_new, second_new


def adam_kernel(qf, qy, qh, fw, fm, fs, dw, dm, ds, hw, hm, hs, ofw, ofm, ofs, odw, odm, ods, ohw, ohm, ohs, gh):
    for j in range(4):
        cols = slice(128 * j, 128 * j + 128)
        g = decode(qf.at[0, j])[0:SHARD, :]
        ofw[:, cols], ofm[:, cols], ofs[:, cols] = adam(fw[:, cols], fm[:, cols], fs[:, cols], g, matrix_rate)
    for j in range(4):
        rows = slice(64 * j, 64 * j + 64)
        odw[rows, :], odm[rows, :], ods[rows, :] = adam(dw[rows, :], dm[rows, :], ds[rows, :], decode(qy.at[j]), matrix_rate)

    @pl.when(pl.program_id(0) == 0)
    def _():
        for k in range(2):
            for j in range(4):
                gh[32 * j : 32 * j + 32, :] = decode(qh.at[4 * k + j])
            new = adam(hw[:, k, :], hm[:, k, :], hs[:, k, :], gh[0:BINS, :], matrix_rate)
            ohw[:, k, :], ohm[:, k, :], ohs[:, k, :] = new


def adam_call(qf, qy, qh, first, dyn, heads):
    fblock = pl.BlockSpec((SHARD, HALF), lambda i: (0, i))
    dblock = pl.BlockSpec((BLK, 128), lambda i: (0, i))
    whole = pl.BlockSpec(heads[0].shape, lambda i: (0, 0, 0))
    out = [jax.ShapeDtypeStruct(a.shape, f32) for a in first + dyn + heads]
    return pl.pallas_call(
        adam_kernel,
        grid=(6,),
        out_shape=out,
        in_specs=[
            pl.BlockSpec((1, 4, SENT + 16, 128), lambda i: (i // 2, i % 2, 0, 0)),
            pl.BlockSpec((4, 80, 128), lambda i: (i // 3, 0, i % 3)),
            pl.BlockSpec(qh.shape, lambda i: (0, 0, 0)),
        ] + [fblock] * 3 + [dblock] * 3 + [whole] * 3,
        out_specs=[fblock] * 3 + [dblock] * 3 + [whole] * 3,
        scratch_shapes=[pltpu.VMEM((128, BLK), f32)],
        compiler_params=pltpu.CompilerParams(vmem_limit_bytes=64 * 2**20),
    )(qf, qy, qh, *first, *dyn, *heads)


def per_device(
    latents, actions, task_ids, steps_left, target_latents, reward_bins, reward_frac, value_bins, value_frac,
    first_weight, first_moment, first_second, dynamics_weight, dynamics_moment, dynamics_second,
    heads_weight, heads_moment, heads_second, task_table, table_moment, table_second,
    vector_params, vector_moment, vector_second,
):
    n_tok = latents.shape[0]
    wide = lax.axis_size("wide")
    token_count = float(HORIZON * n_tok * wide * lax.axis_size("narrow"))
    z = lax.axis_index("narrow")
    n_task = task_table.shape[0]
    n_vec = vector_params.shape[0]
    to_class = lambda a: a.transpose(2, 0, 1)
    lg, qf, qy, qh, misc = step_call(
        wide, token_count, n_task, latents, actions.transpose(1, 2, 0), task_ids,
        steps_left, target_latents.transpose(1, 0, 2),
        reward_bins.T, reward_frac.T, value_bins.T, value_frac.T,
        first_weight, dynamics_weight, to_class(heads_weight), task_table, vector_params)
    new = adam_call(
        qf, qy, qh, [first_weight, first_moment, first_second], [dynamics_weight, dynamics_moment, dynamics_second],
        [to_class(a) for a in (heads_weight, heads_moment, heads_second)])
    heads_new = [a.transpose(1, 2, 0) for a in new[6:]]
    grad_vec = lax.dynamic_slice(misc[0:90].reshape(-1), (n_vec * z,), (n_vec,))
    grad_tab = lax.dynamic_slice(misc, (128 + 32 * z, 0), (n_task, TEMB))
    table_new = adam(task_table, table_moment, table_second, grad_tab, vector_rate)
    vector_new = adam(vector_params, vector_moment, vector_second, grad_vec, vector_rate)
    return (lg, *new[:6], *heads_new, *table_new, *vector_new)


def solution(mesh):
    tokens = ("wide", "narrow")
    in_specs = (
        P(tokens, None), P(tokens, None, None), P(tokens), P(tokens), P(tokens, None, None),
        P(tokens, None), P(tokens, None), P(tokens, None), P(tokens, None),
        *(P("narrow", None),) * 6, *(P(None, "narrow", None),) * 3, *(P("narrow", None),) * 3, *(P("narrow"),) * 3,
    )
    out_specs = (
        P(tokens, None), *(P("narrow", None),) * 6, *(P(None, "narrow", None),) * 3,
        *(P("narrow", None),) * 3, *(P("narrow"),) * 3,
    )
    return jax.shard_map(per_device, mesh=mesh, in_specs=in_specs, out_specs=out_specs, check_vma=False)
```

```python
import functools

import jax
import jax.numpy as jnp
from jax import lax
from jax.experimental import pallas as pl
from jax.experimental.pallas import tpu as pltpu
from jax.sharding import PartitionSpec as P

f32, bf16, i16, i32 = jnp.float32, jnp.bfloat16, jnp.int16, jnp.int32
MESH = pl.DeviceIdType.MESH

LAT = 768
HID = 1024
BINS = 101
TEMB = 96
ACTN = 8
HORIZON = 3
STEP = 5
NZ = 4
SHARD = 218
SENT = 224
BLK = 256
ROWS = 320
RB = 320
NB = ROWS // RB
ALL = HORIZON * ROWS
HALF = HID // 2
YHALF = LAT // 2
BOTT = 112
TASK_LANE = LAT + ACTN - 3 * SHARD
ACT_LANE = LAT - 3 * SHARD

norm_eps = 1e-05
adam_eps = 1e-08
moment_decay = 0.5
horizon_decay = 0.5
weight_decay = 0.01
matrix_rate = 0.03
vector_rate = 0.3
consistency_coef = 20.0
head_coef = 0.1

NN = (((1,), (0,)), ((), ()))
NT = (((1,), (1,)), ((), ()))
TN = (((0,), (0,)), ((), ()))


def dot(a, b, dims=NN):
    return lax.dot_general(a, b, dims, preferred_element_type=f32)


def loop(start, end, body, carry):
    for i in range(start, end):
        carry = body(i, carry)
    return carry


def whole_of(start, unit):
    return start if isinstance(start, int) else pl.multiple_of(start, unit)


def lanes(n):
    return lax.broadcasted_iota(i32, (1, n), 1)


def block_rows(i, base=0):
    return pl.ds(base + i * RB, RB)


def encode(v, ref):
    rows = v.shape[0]
    top = jnp.max(jnp.abs(v), 0, keepdims=True)
    e = jnp.clip(jnp.ceil(jnp.log2(jnp.maximum(top, 1e-37))), -100.0, 120.0)
    ref[0:rows, :] = jnp.round(v * jnp.exp2(14.9 - e)).astype(i32).astype(i16)
    ref[rows : rows + 16, :] = jnp.broadcast_to(e, (16, v.shape[1])).astype(i32).astype(i16)


def decode(ref):
    rows = ref.shape[0] - 16
    e = ref[rows : rows + 16, :].astype(i32).astype(f32)[0:1, :]
    return ref[0:rows, :].astype(i32).astype(f32) * jnp.exp2(e - 14.9)


def pack_tiles(x):
    inside = lanes(BLK) < SHARD
    b0 = jnp.where(inside, x[:, 0:256], 0.0)
    b1 = jnp.where(inside, pltpu.roll(x[:, 128:512], 384 - 90, 1)[:, 0:256], 0.0)
    b2 = jnp.where(inside, pltpu.roll(x[:, 384:768], 384 - 52, 1)[:, 0:256], 0.0)
    b3 = jnp.where(lanes(128) < ACT_LANE, pltpu.roll(x[:, 640:768], 128 - 14, 1), 0.0)
    return b0, b1, b2, b3


def unpack_tiles(g):
    inside = lanes(BLK) < SHARD
    empty = jnp.zeros((g.shape[0], 128), f32)
    b0 = jnp.where(inside, g[:, 0:256], 0.0)
    b1 = pltpu.roll(jnp.concatenate([jnp.where(inside, g[:, 256:512], 0.0), empty], 1), 90, 1)
    b2 = pltpu.roll(jnp.concatenate([jnp.where(inside, g[:, 512:768], 0.0), empty], 1), 52, 1)
    b3 = pltpu.roll(jnp.where(lanes(128) < ACT_LANE, g[:, 768:896], 0.0), 14, 1)
    return jnp.concatenate(
        [
            b0[:, 0:128],
            b0[:, 128:256] + b1[:, 0:128],
            b1[:, 128:256],
            b1[:, 256:384] + b2[:, 0:128],
            b2[:, 128:256],
            b2[:, 256:384] + b3,
        ],
        1,
    )


def group_sums(x, ones):
    parts = []
    for j in range(0, x.shape[1], 256):
        v = x[:, j : j + 256]
        high = v.astype(bf16)
        low = (v - high.astype(f32)).astype(bf16)
        parts.append(dot(high, ones) + dot(low, ones))
    return jnp.concatenate(parts, 1)


def mish_parts(n):
    u = jnp.exp(jnp.minimum(n, 40.0))
    q = u * (u + 2.0)
    r = 1.0 / (q + 2.0)
    bent = q * r
    return bent, bent + (4.0 * n) * (u * (u + 1.0)) * (r * r)


def add_columns(acc, values):
    for k, v in enumerate(values):
        total = acc[8 * k : 8 * k + 8, :]
        for j in range(v.shape[0] // 8):
            total = total + v[8 * j : 8 * j + 8, :]
        acc[8 * k : 8 * k + 8, :] = total


def rcopy(src, dst, send_sem, recv_sem, device):
    return pltpu.make_async_remote_copy(
        src_ref=src, dst_ref=dst, send_sem=send_sem, recv_sem=recv_sem, device_id=device, device_id_type=MESH
    )


def step_kernel(wide, token_count, n_tok, n_task, lat, actT, ids, steps, tgt, rb, rf, vb, vf, fw, dw, hw, tab, vec,
                lg, qf, qy, qh, misc, **s):
    ups_n = wide.bit_length() - 4
    w, z = lax.axis_index("wide"), lax.axis_index("narrow")
    b0, b1, b2 = lax.rem(w, 2), lax.rem(lax.div(w, 2), 2), lax.rem(lax.div(w, 4), 2)
    pc, p1, p2 = (w + 1 - 2 * b0, z), (w + 2 - 4 * b1, z), (w + 4 - 8 * b2, z)
    zs = [(w, lax.rem(z + d, NZ)) for d in range(NZ)]
    from_z = [lax.rem(z + NZ - d, NZ) for d in range(NZ)]
    ups = []
    for u in range(ups_n):
        bit = 8 << u
        ups.append((w + bit - 2 * bit * lax.rem(lax.div(w, bit), 2), z))
    me = b0 * 4 + b1 * 2 + b2
    own = b1 * 2 + b2
    me_1, me_2, me_12 = me + 2 - 4 * b1, me + 1 - 2 * b2, 4 * b0 + 3 - own
    mine_of_8 = 4 * b0
    sends = []

    def pick(odd, even_value, odd_value):
        return even_value + odd * (odd_value - even_value)

    def launch(make):
        make().start()
        sends.append(make)

    X, XT, XTp, U, AT, ATp, DU = s["X"], s["XT"], s["XTp"], s["U"], s["AT"], s["ATp"], s["DU"]
    WF, WD, HT, SM, VEC = s["WF"], s["WD"], s["HT"], s["SM"], s["VEC"]
    PRE, ACT, TT = s["PRE"], s["ACT"], s["TT"]
    TU, TS = TT.at[pl.ds(0, ROWS)], TT.at[pl.ds(ROWS, ROWS)]
    GP, GPp, GDL, GDLp = s["GP"], s["GPp"], s["GDL"], s["GDLp"]
    INV, SIDE, ONES, VA, VT, GEMB = (
        s["INV"], s["SIDE"], s["ONES"], s["VA"], s["VT"], s["GEMB"])

    barrier = pltpu.get_barrier_semaphore()
    peers = [pc, p1, p2] + zs[1:] + ups
    for p in peers:
        pl.semaphore_signal(barrier, inc=1, device_id=p, device_id_type=MESH)

    STG = s["STG"]
    loads = []

    def load_first(part):
        return pltpu.make_async_copy(
            fw.at[:, pl.ds(HALF * part, HALF)], STG.at[part % 2], s["ls"].at[part % 2])

    loads.append(pltpu.make_async_copy(dw, DU.at[pl.ds(0, BLK)], s["ls"].at[3]))
    loads.append(pltpu.make_async_copy(lat, GDL.at[pl.ds(0, n_tok)], s["ls"].at[4]))
    load_first(0).start()
    load_first(1).start()
    for c in loads:
        c.start()

    def cast_first(br):
        for part in (2 * br, 2 * br + 1):
            load_first(part).wait()
            rows = jnp.concatenate([STG[part % 2].astype(bf16), jnp.zeros((SENT - SHARD, HALF), bf16)], 0)
            WF[pl.ds(whole_of(BLK * z, BLK), SENT), HALF * part : HALF * part + HALF] = rows
            if part < 4:
                load_first(part + 2).start()

    cast_first(0)
    pl.semaphore_wait(barrier, len(peers))

    gs, gr = s["gs"], s["gr"]

    class Item:
        def __init__(self, index, view):
            self.i, self.view = index, view

        def _copy(self, d, kind, piece, device):
            view = self.view(*piece)
            return rcopy(view, view, gs.at[self.i, d - 1, kind], gr.at[self.i, d - 1, kind], device)

        def _recv(self, d, kind, *piece):
            self._copy(d, kind, piece, pc).wait_recv()

        def _send(self, d, kind, device, *piece):
            launch(lambda: self._copy(d, kind, piece, device))

        def start(self):
            for d in (1, 3, 2):
                self._send(d, 0, zs[d], z, me, 1, None)

        def spread(self, *ds):
            for d in ds or (1, 3, 2):
                self._recv(d, 0, from_z[d], me, 1, None)
                self._send(d, 1, p1, from_z[d], me, 1, None)
                self._send(d, 2, p2, from_z[d], me, 1, None)

        def forward(self, *ds):
            for d in ds or (1, 3, 2):
                q = from_z[d]
                self._recv(d, 1, q, me_1, 1, None)
                self._send(d, 3, p2, q, me_1, 1, 0)
                self._recv(d, 2, q, me_2, 1, None)
                self._send(d, 4, p1, q, me_2, 1, 1)

        def cross(self, *ds):
            for d in ds or (1, 3, 2):
                q = from_z[d]
                self._recv(d, 3, q, me_12, 1, 0)
                self._recv(d, 4, q, me_12, 1, 1)
                self._send(d, 5, pc, q, mine_of_8, 4, None)

        def finish(self):
            for d in (1, 3, 2):
                self._recv(d, 5, from_z[d], 4 - 4 * b0, 4, None)

    def first_view(br):
        def view(q, at, n, half):
            lo, size = (0, SENT) if half is None else (BOTT * half, BOTT)
            return WF.at[pl.ds(whole_of(BLK * q + lo, 16), size), pl.ds(whole_of(HID * br + 128 * at, 128), 128 * n)]
        return view

    def dyn_view(q, at, n, half):
        lo, size = (0, 32 * n) if half is None else (16 * half, 16)
        return WD.at[pl.ds(whole_of(BLK * q + 32 * at + lo, 16), size)]

    def heads_view(q, at, n, half):
        cols = pl.ds(whole_of(BLK * q, BLK), BLK)
        rows = pl.ds(whole_of(16 * at, 16), 16 * n)
        if half is None:
            return HT.at[:, rows, cols]
        return HT.at[pl.ds(half, 1), rows, cols]

    gD, gY, gR, gV, gH = (
        Item(0, first_view(0)), Item(1, dyn_view), Item(2, first_view(1)), Item(3, first_view(2)), Item(4, heads_view))

    def vec_rows():
        n_vec = vec.shape[0]
        whole = n_vec // 128
        VR = s["VR"]
        VR[...] = jnp.zeros_like(VR)
        for r in range(whole):
            VR[r + 1 : r + 2, :] = vec[pl.ds(128 * r, 128)].reshape(1, 128)
        left = n_vec - 128 * whole
        VR[whole + 1 : whole + 2, 0:left] = vec[pl.ds(128 * whole, left)].reshape(1, left)
        plain = VR[1:33, :]
        moved = jnp.where(lanes(128) < 64, pltpu.roll(VR[0:32, :], 64, 1), pltpu.roll(plain, 64, 1))
        return jnp.where(lax.rem(z, 2) == 1, moved, plain).astype(bf16)

    gD.start()
    frame = vec_rows()
    SM[z, 0:32, :] = frame
    SM[z, 32:64, :] = jnp.zeros((32, 128), bf16)
    SM[z, 32 : 32 + n_task, 0:TEMB] = tab[...].astype(bf16)
    for d in (1, 3, 2):
        launch(lambda d=d: rcopy(SM.at[z], SM.at[z], s["ms"].at[d], s["mr"].at[d], zs[d]))
    loads[0].wait()
    WD[pl.ds(whole_of(BLK * z, BLK), BLK), :] = DU[0:BLK, :].astype(bf16)
    gY.start()
    cast_first(1)
    gR.start()
    gD.spread(1, 3)
    own_cols = pl.ds(whole_of(BLK * z, BLK), BLK)
    for k in range(2):
        PRE[0:128, 0:BLK] = jnp.zeros((128, BLK), f32)
        PRE[0:BINS, 0:BLK] = hw[:, k, :]
        HT[k, :, own_cols] = PRE[0:128, 0:BLK].astype(bf16)
    gH.start()
    gD.spread(2)
    cast_first(2)
    gV.start()

    GDL[n_tok:ROWS, :] = jnp.zeros((ROWS - n_tok, LAT), bf16)
    for q in range(NZ):
        WF[BLK * q + SENT : BLK * q + BLK, :] = jnp.zeros((BLK - SENT, 3 * HID), bf16)
    loads[1].wait()

    gD.forward(1, 3)
    gY.spread(1, 3)
    idr = s["IDR"]
    idr[...] = jnp.full_like(idr, -1)
    idr[0:1, 0:n_tok] = ids[...].reshape(1, n_tok)
    slot = lax.broadcasted_iota(i32, (128, 1), 0)
    task = jnp.where(slot % 32 < n_task, n_task * (slot // 32) + slot % 32, -2)
    PKT = s["PKT"]
    PKT[...] = jnp.where(idr[0:1, 0:ROWS] == task, 1.0, 0.0).astype(bf16)
    gD.forward(2)
    gY.spread(2)
    gD.cross(1, 3)

    for d in (1, 3, 2):
        q = from_z[d]
        rcopy(SM.at[q], SM.at[q], s["ms"].at[d], s["mr"].at[d], pc).wait_recv()
    full = s["VFULL"]
    full[...] = jnp.zeros_like(full)
    for q, at in enumerate((0, 22, 45, 67)):
        full[at : at + 24, :] = full[at : at + 24, :] + SM[q, 0:32, :].astype(f32)[0:24, :]
    for r in range(12):
        n, first = (8, 8 * r) if r < 9 else (6, 72 + 6 * (r - 9))
        for j in range(n):
            VEC[r : r + 1, 128 * j : 128 * j + 128] = full[first + j : first + j + 1, :]
    place = jnp.concatenate([SM[q, 32:64, :] for q in range(NZ)], 0).astype(f32)
    table = pltpu.roll(jnp.concatenate([place, jnp.zeros_like(place)], 1), TASK_LANE, 1).astype(bf16)
    AC = s["AC"]
    AC[...] = jnp.zeros_like(AC)
    act_to = jnp.where(
        lax.broadcasted_iota(i32, (16, BLK), 0) + ACT_LANE == lax.broadcasted_iota(i32, (16, BLK), 1), 1.0, 0.0
    ).astype(bf16)
    rows_of_task = dot(PKT[...], table, TN)
    gD.cross(2)
    for t in range(3):
        AC[0:ACTN, 0:n_tok] = actT[t].astype(f32)
        X[ROWS * t : ROWS * t + ROWS, 768:1024] = (rows_of_task + dot(AC[:, 0:ROWS].astype(bf16), act_to, TN)).astype(bf16)

    gY.forward(1, 3)

    def later_setup():
        tile = lax.broadcasted_iota(i32, (256, 256), 0) // 8 == lax.broadcasted_iota(i32, (256, 256), 1) // 8
        ONES[...] = jnp.where(tile, 1.0, 0.0).astype(bf16)
        st = s["ST"]
        st[...] = jnp.zeros_like(st)
        st[0:1, 0:n_tok] = steps[...].reshape(1, n_tok).astype(f32)
        for t in range(3):
            for k, ref in enumerate((rb, rf, vb, vf)):
                st[k + 1 : k + 2, 0:n_tok] = ref[t : t + 1, :].astype(f32)
            SIDE[t] = st[...].T[0:ROWS, :]
        for ref in (VA, VT, GEMB, s["DWH"], s["MS"]):
            ref[...] = jnp.zeros_like(ref)

    def put_latents(rows, values):
        b0, b1, b2, b3 = pack_tiles(values)
        X[rows, 0:768] = jnp.concatenate((b0, b1, b2), 1).astype(bf16)
        X[rows, 768:896] = (X[rows, 768:896].astype(f32) + b3).astype(bf16)

    put_latents(block_rows(0), GDL[0:ROWS, :].astype(f32))
    gD.finish()

    def matmul(out, orows, n, width, left, right, dims=NN):
        def tile_step(j, c):
            cols = pl.ds(j * width, width)
            out[orows, cols] = dot(left, right(cols), dims)
            return c
        loop(0, n // width, tile_step, 0)

    def first_forward(br, base):
        def tile_step(j, c):
            cols = pl.ds(j * 512, 512)
            from_cols = pl.ds(whole_of(HID * br + j * 512, 512), 512)
            PRE[:, cols] = dot(X[pl.ds(base, ROWS), :], WF[:, from_cols])
            return c
        loop(0, 2, tile_step, 0)

    def norm_mish(br, unit, inv, unit_base, slope):
        bias, gain, shift = (VEC[pl.ds(3 * br + k, 1), :] for k in range(3))

        def step(i, c):
            rows = block_rows(i)
            p = PRE[rows, :] + bias
            ce = p - jnp.mean(p, -1, keepdims=True)
            iv = lax.rsqrt(jnp.mean(ce * ce, -1, keepdims=True) + norm_eps)
            un = ce * iv
            n = un * gain + shift
            bent, sl = mish_parts(n)
            ACT[rows, :] = (n * bent).astype(bf16)
            if slope is not None:
                slope[rows, :] = sl
            unit[block_rows(i, unit_base), :] = un
            inv[block_rows(i, unit_base), :] = jnp.broadcast_to(iv, (RB, 128))
            return c
        loop(0, NB, step, 0)

    def dyn_forward(t, between):
        base = ROWS * t
        first_forward(0, base)
        between(0)
        norm_mish(0, U, INV, base, None)
        between(1)
        matmul(TU, pl.ds(0, ROWS), LAT, 384, ACT[...], lambda cols: WD[:, cols])
        AT[:, base : base + ROWS] = ACT[...].T
        bias, gain, shift = (VEC[9 + k : 10 + k, 0:LAT] for k in range(3))

        def step(i, c):
            rows, at = block_rows(i), block_rows(i, base)
            p = TU[rows, 0:LAT] + bias
            ce = p - jnp.mean(p, -1, keepdims=True)
            iv = lax.rsqrt(jnp.mean(ce * ce, -1, keepdims=True) + norm_eps)
            un = ce * iv
            DU[at, :] = un
            INV[at, 64:128] = jnp.broadcast_to(iv, (RB, 64))
            if t < 2:
                e = jnp.exp(un * gain + shift)
                put_latents(block_rows(i, base + ROWS), e / group_sums(e, ONES[...]))
            return c
        loop(0, NB, step, 0)

    def between_0(at):
        if at == 0:
            gY.forward(2)
        else:
            gY.cross()
            gR.spread()
            later_setup()
            gY.finish()

    def between_1(at):
        if at == 1:
            gR.forward()

    def between_2(at):
        if at == 1:
            gH.cross()

    dyn_forward(0, between_0)
    gH.spread()
    dyn_forward(1, between_1)
    gR.cross()
    gH.forward()
    gV.spread()
    dyn_forward(2, between_2)
    XT[...] = X[...].T
    xs, xr = s["xs"], s["xr"]
    launch(lambda: rcopy(XT, XTp, xs.at[0], xr.at[0], pc))
    launch(lambda: rcopy(AT, ATp, xs.at[1], xr.at[1], pc))
    gR.finish()
    gH.finish()
    gV.forward()

    def norm_backward(br, unit, inv, unit_base, slope, out_base):
        gain, shift = VEC[pl.ds(3 * br + 1, 1), :], VEC[pl.ds(3 * br + 2, 1), :]
        acc = VA.at[br]

        def step(i, c):
            rows, at = block_rows(i), block_rows(i, unit_base)
            un = unit[at, :]
            sl = mish_parts(un * gain + shift)[1] if slope is None else slope[rows, :]
            gn = PRE[rows, :] * sl
            h = gn * gain
            gp = (h - jnp.mean(h, -1, keepdims=True) - un * jnp.mean(h * un, -1, keepdims=True)) * inv[at, 0:1]
            GP[block_rows(i, out_base), pl.ds(whole_of(HID * br, HID), HID)] = gp.astype(bf16)
            add_columns(acc, (gp, gn * un, gn))
            return c
        loop(0, NB, step, 0)

    def head_step(k, t):
        base = whole_of(ROWS * t, RB)
        first_forward(1 + k, base)
        norm_mish(1 + k, TU, s["HINV"], 0, TS)
        logits = dot(ACT[...], HT[k], NT)
        real = lanes(128) < BINS
        logits = jnp.where(real, logits, -1e30)
        e = jnp.exp(logits - jnp.max(logits, -1, keepdims=True))
        soft = e / jnp.sum(e, -1, keepdims=True)
        side = SIDE[t]
        at, frac = (jnp.where(k == 0, side[:, c : c + 1], side[:, c + 2 : c + 3]) for c in (1, 2))
        level = lanes(128).astype(f32)
        hot = jnp.where(level == at, 1.0 - frac, 0.0) + jnp.where(level == at + 1.0, frac, 0.0)
        decay = jnp.where(t == 0, 1.0, jnp.where(t == 1, horizon_decay, horizon_decay**2))
        weight = jnp.where(side[:, 0:1] > t.astype(f32), decay, 0.0) / token_count
        gl = jnp.where(real, weight * head_coef * (soft - hot), 0.0).astype(bf16)
        s["DWH"][k] = s["DWH"][k] + dot(gl.astype(f32).T.astype(bf16), ACT[...])
        PRE[...] = dot(gl, HT[k])
        norm_backward(1 + k, TU, s["HINV"], 0, TS, base)

    def dyn_backward(t, between=None):
        base = ROWS * t
        gain, shift = VEC[10:11, 0:LAT], VEC[11:12, 0:LAT]
        scale = 2.0 * consistency_coef / LAT

        def step(i, c):
            rows, at = block_rows(i), block_rows(i, base)
            un = DU[at, :]
            e = jnp.exp(un * gain + shift)
            sx = e / group_sums(e, ONES[...])
            weight = jnp.where(SIDE[0, rows, 0:1] > t, f32(horizon_decay**t), 0.0) / token_count
            g = weight * scale * (sx - X[at, 0:LAT].astype(f32))
            if t < 2:
                g = g + unpack_tiles(PRE[rows, 0:896])
            gn = sx * (g - group_sums(g * sx, ONES[...]))
            h = gn * gain
            gp = (h - jnp.mean(h, -1, keepdims=True) - un * jnp.mean(h * un, -1, keepdims=True)) * INV[at, 64:65]
            GDL[at, :] = gp.astype(bf16)
            add_columns(VT, (gp, gn * un, gn))
            return c
        loop(0, NB, step, 0)
        yc = pl.ds(whole_of(YHALF * (1 - b0), 128), YHALF)
        launch(lambda: rcopy(GDL.at[pl.ds(base, ROWS), yc], GDLp.at[pl.ds(base, ROWS)], xs.at[4 + t], xr.at[4 + t], pc))
        if between is not None:
            between()

        def tile_step(j, c):
            cols = pl.ds(j * 512, 512)
            PRE[:, cols] = dot(GDL[pl.ds(base, ROWS), :], WD[cols, :], NT)
            return c
        loop(0, 2, tile_step, 0)
        norm_backward(0, U, INV, base, None, base)
        gc = pl.ds(whole_of(HALF * (1 - b0), HALF), HALF)
        launch(lambda: rcopy(GP.at[pl.ds(base, ROWS), gc], GPp.at[0, pl.ds(base, ROWS)], xs.at[7 + t], xr.at[7 + t], pc))

    def inputs_backward(t):
        base = ROWS * t

        def tile_step(j, c):
            cols = pl.ds(j * 512, 512)
            PRE[:, cols] = dot(GP[pl.ds(base, ROWS), :], WF[cols, :], NT)
            return c
        loop(0, 2, tile_step, 0)
        GEMB[...] = GEMB[...] + PRE[:, 768:1024]

    rs_s, rs_r = s["ss"], s["sr"]

    class Stream:
        def __init__(self, index, grad, view, E, R, Q, half):
            self.i, self.grad, self.view, self.Q, self.half = index, grad, view, Q, half
            (self.E1, self.E2, self.E3), (self.R1, self.R2, self.R3) = E, R
            self.spent = []

        def _copy(self, at, src, dst, device):
            return rcopy(src, dst, rs_s.at[self.i, at], rs_r.at[self.i, at], device)

        def _recv(self, at, dst):
            self._copy(at, dst, dst, pc).wait_recv()

        def release(self):
            for first, count, ref in self.spent:
                if count == 1:
                    self._copy(first, ref, ref, pc).wait_send()
                else:
                    def one(i, c):
                        self._copy(first + i, ref.at[i], ref.at[i], pc).wait_send()
                        return c
                    lax.fori_loop(0, count, one, 0)
            self.spent = []

        def _send(self, at, src, dst, device):
            self._copy(at, src, dst, device).start()
            self.spent.append((at, 1, src))

        def stage1(self):
            def one(i, c):
                q = lax.rem(z + 1 + i, NZ)
                odd = lax.rem(q, 2)
                base = pick(odd, 2 - 2 * b1, 1 - b2)
                for j in range(2):
                    encode(self.grad[self.view(q, base + j * (1 + odd))], self.E1.at[i, j])
                self._copy(i, self.E1.at[i], self.R1.at[i], (pick(odd, p1[0], p2[0]), z)).start()
                return c
            lax.fori_loop(0, NZ, one, 0)
            self.spent.append((0, NZ, self.E1))

        def stage2(self):
            def one(i, c):
                q = lax.rem(z + 1 + i, NZ)
                odd = lax.rem(q, 2)
                self._recv(i, self.R1.at[i])
                keep = pick(odd, b2, b1)
                other = pick(odd, own + 1 - 2 * b2, own + 2 - 4 * b1)
                encode(self.grad[self.view(q, other)] + decode(self.R1.at[i, 1 - keep]), self.E2.at[i])
                self._copy(4 + i, self.E2.at[i], self.R2.at[i], (pick(odd, p2[0], p1[0]), z)).start()
                mine = self.view(q, own)
                self.grad[mine] = self.grad[mine] + decode(self.R1.at[i, keep])
                return c
            lax.fori_loop(0, NZ, one, 0)
            self.spent.append((4, NZ, self.E2))

        def stage3(self):
            def one(i, c):
                q = lax.rem(z + 1 + i, NZ)
                self._recv(4 + i, self.R2.at[i])
                encode(self.grad[self.view(q, own)] + decode(self.R2.at[i]), self.E3.at[i])
                self._copy(8 + i, self.E3.at[i], self.R3.at[i], (w, q)).start()
                return c
            lax.fori_loop(0, 3, one, 0)
            self.spent.append((8, 3, self.E3))

        def stage4(self):
            self._recv(7, self.R2.at[3])
            total = self.grad[self.view(z, own)] + decode(self.R2.at[3])
            for i in (0, 2, 1):
                self._recv(8 + i, self.R3.at[i])
                total = total + decode(self.R3.at[i])
            for u in range(ups_n):
                F, FR = self.Q.at[me], s["FR%d" % self.i]
                encode(total, F)
                c = self._copy(16 + u, F, FR.at[u], ups[u])
                c.start()
                self._recv(16 + u, FR.at[u])
                c.wait_send()
                total = decode(F) + decode(FR.at[u])
            encode(total, self.Q.at[me])
            self._send(11, self.Q.at[me], self.Q.at[me], p1)
            self._send(12, self.Q.at[me], self.Q.at[me], p2)

        def stage5(self):
            s1, s2 = me_1, me_2
            n = self.Q.shape[1]
            low, high = pl.ds(0, self.half), pl.ds(self.half, n - self.half)
            self._recv(11, self.Q.at[s1])
            self._send(13, self.Q.at[s1, low], self.Q.at[s1, low], p2)
            self._recv(12, self.Q.at[s2])
            self._send(14, self.Q.at[s2, high], self.Q.at[s2, high], p1)

        def stage6(self):
            s12 = me_12
            n = self.Q.shape[1]
            low, high = pl.ds(0, self.half), pl.ds(self.half, n - self.half)
            self._recv(13, self.Q.at[s12, low])
            self._recv(14, self.Q.at[s12, high])
            mine = self.Q.at[pl.ds(4 * b0, 4)]
            self._send(15, mine, mine, pc)

        def stage7(self, out, sem):
            self._recv(15, self.Q.at[pl.ds(4 - 4 * b0, 4)])
            c = pltpu.make_async_copy(self.Q, out, sem)
            c.start()
            return c

    def first_slice(q, at):
        return (pl.ds(whole_of(BLK * q, BLK), SENT), pl.ds(whole_of(128 * at, 128), 128))

    def value_slice(q, at):
        cols = HALF * lax.div(q, 2) + 128 * at
        return (pl.ds(whole_of(BLK * lax.rem(q, 2), BLK), SENT), pl.ds(whole_of(cols, 128), 128))

    def y_slice(q, at):
        return (pl.ds(whole_of(BLK * q + 64 * at, 64), 64), slice(None))

    def h_slice(q, at):
        return (b0, pl.ds(whole_of(32 * at, 32), 32), pl.ds(whole_of(BLK * q, BLK), BLK))

    EF = (s["E1"], s["E2"], s["E3"])
    streams = []
    for i, name in enumerate("DRV"):
        streams.append(Stream(
            i, *((TT, value_slice) if name == "V" else (s["DWA"], first_slice)), EF,
            tuple(s["R%d%s" % (k, name)] for k in (1, 2, 3)), s["QF"].at[i], 128))
    sD, sR, sV = streams
    sY = Stream(3, s["DWY"], y_slice, tuple(s["E%dY" % k] for k in (1, 2, 3)),
                tuple(s["R%dY" % k] for k in (1, 2, 3)), s["QY"], 48)
    sH = Stream(4, s["DWH"], h_slice, tuple(s["E%dH" % k] for k in (1, 2, 3)),
                tuple(s["R%dH" % k] for k in (1, 2, 3)), s["QH"], 32)

    def send_half(br):
        def make():
            cols = pl.ds(whole_of(HID * br + HALF * (1 - b0), HALF), HALF)
            return rcopy(GP.at[:, cols], GPp.at[br], xs.at[1 + br], xr.at[1 + br], pc)
        launch(make)

    def wait_x(at, dst):
        rcopy(dst, dst, xs.at[at], xr.at[at], pc).wait_recv()

    def weight_grad(out, n, left, right, left2, right2):
        def tile_step(j, c):
            cols = pl.ds(whole_of(j * n, n), n)
            out[:, cols] = dot(left[...], right(j)) + dot(left2[...], right2(cols))
            return c
        lax.fori_loop(0, out.shape[1] // n, tile_step, 0)

    def first_grad(br, out):
        weight_grad(
            out, 256, XT,
            lambda j: GP[:, pl.ds(whole_of(HID * br + HALF * b0 + 256 * j, 256), 256)],
            XTp, lambda cols: GPp[br, :, cols])

    def value_grad():
        def tile_step(j, c):
            cols = pl.ds(whole_of(j * 256, 256), 256)
            low_cols = pl.ds(whole_of(HALF + j * 256, 256), 256)
            right = GP[:, pl.ds(whole_of(2 * HID + HALF * b0 + 256 * j, 256), 256)]
            total = dot(XT[...], right) + dot(XTp[...], GPp[2, :, cols])
            TT[0:512, cols] = total[0:512, :]
            TT[0:512, low_cols] = total[512:1024, :]
            return c
        lax.fori_loop(0, 2, tile_step, 0)

    def y_grad():
        wait_x(1, ATp)
        for t in range(3):
            wait_x(4 + t, GDLp.at[pl.ds(ROWS * t, ROWS)])
        weight_grad(
            s["DWY"], 128, AT,
            lambda j: GDL[:, pl.ds(whole_of(YHALF * b0 + 128 * j, 128), 128)],
            ATp, lambda cols: GDLp[:, cols])
        sY.stage1()

    def head_steps(i, c):
        @pl.when(i == 1)
        def _():
            gV.cross()

        @pl.when(i == 3)
        def _():
            send_half(1)
            gV.finish()

        @pl.when(i == 4)
        def _():
            wait_x(0, XTp)
            wait_x(2, GPp.at[1])
            first_grad(1, s["DWA"])
            sR.stage1()

        head_step(lax.div(i, 3), lax.rem(i, 3))
        return c
    lax.fori_loop(0, 6, head_steps, 0)
    send_half(2)
    launch(lambda: rcopy(s["DWH"].at[1 - b0], s["DWHp"], xs.at[10], xr.at[10], pc))
    for t in range(3):
        loads.append(pltpu.make_async_copy(
            tgt.at[t], X.at[pl.ds(ROWS * t, n_tok), pl.ds(0, LAT)], s["ls"].at[5 + t]))
        loads[-1].start()
    sR.stage2()
    for c in loads[2:]:
        c.wait()
    dyn_backward(2)
    sR.stage3()
    wait_x(3, GPp.at[2])
    value_grad()
    sR.release()
    sV.stage1()
    inputs_backward(2)
    wait_x(10, s["DWHp"])
    s["DWH"][b0] = s["DWH"][b0] + s["DWHp"][...]
    sH.stage1()
    dyn_backward(1)
    sR.stage4()
    sV.stage2()
    sH.stage2()
    inputs_backward(1)
    sR.stage5()
    dyn_backward(0, y_grad)
    sV.stage3()
    sH.stage3()
    for t in range(3):
        wait_x(7 + t, GPp.at[0, pl.ds(ROWS * t, ROWS)])
    first_grad(0, s["DWA"])
    sV.release()
    sD.stage1()
    sR.stage6()
    inputs_backward(0)

    def write_latent(i, c):
        rows = block_rows(i)
        DU[rows, :] = unpack_tiles(PRE[rows, 0:896])
        return c
    loop(0, NB, write_latent, 0)
    lg_copy = pltpu.make_async_copy(DU.at[pl.ds(0, n_tok)], lg, s["ls"].at[8])
    lg_copy.start()
    ge = GEMB[...]
    g1 = ge.astype(bf16)
    g2 = (ge - g1.astype(f32)).astype(bf16)
    g3 = (ge - g1.astype(f32) - g2.astype(f32)).astype(bf16)
    pk = PKT[...]
    by_task = dot(pk, g1) + dot(pk, g2) + dot(pk, g3)
    M = s["MS"]
    M[128:256, :] = pltpu.roll(by_task, BLK - TASK_LANE, 1)[:, 0:128]
    for r in range(12):
        acc, n, first = (VA.at[r // 3], 8, 8 * r) if r < 9 else (VT, 6, 72 + 6 * (r - 9))
        k = r % 3
        row = jnp.sum(acc[8 * k : 8 * k + 8, :], 0, keepdims=True)
        for j in range(n):
            M[first + j : first + j + 1, :] = row[:, 128 * j : 128 * j + 128]

    vs, vr = s["vs"], s["vr"]

    def small(at, src, dst, device):
        return rcopy(src, dst, vs.at[at], vr.at[at], device)

    def rows_of(start, n):
        return pl.ds(whole_of(start, 32), n)

    halves = ((0, pc, b0, 128), (1, p1, b1, 64), (2, p2, b2, 32))

    def halve(step, start):
        at, device, bit, n = halves[step]
        launch(lambda: small(at, M.at[rows_of(start + n * (1 - bit), n)], s["MR%d" % step], device))

    def halved(step, start):
        at, device, bit, n = halves[step]
        small(at, s["MR%d" % step], s["MR%d" % step], device).wait_recv()
        mine = rows_of(start + n * bit, n)
        M[mine, :] = M[mine, :] + s["MR%d" % step][...]
        return start + n * bit

    halve(0, 0)
    sY.stage2()
    at = halved(0, 0)
    halve(1, at)
    sV.stage4()
    sH.stage4()
    at = halved(1, at)
    halve(2, at)
    sY.stage3()
    sD.stage2()
    at = halved(2, at)
    MZ = s["MZ"]
    MZ[z] = M[rows_of(at, 32), :]
    for d in (2, 1, 3):
        launch(lambda d=d: small(2 + d, MZ.at[z], MZ.at[z], zs[d]))
    sV.stage5()
    sH.stage5()
    sD.stage3()
    sY.stage4()
    for d in (1, 3, 2):
        small(2 + d, MZ.at[from_z[d]], MZ.at[from_z[d]], pc).wait_recv()
    total = (MZ[0] + MZ[1]) + (MZ[2] + MZ[3])
    for u in range(ups_n):
        s["MF"][u] = total
        launch(lambda u=u: small(9 + u, s["MF"].at[u], s["MFR"].at[u], ups[u]))
        small(9 + u, s["MFR"].at[u], s["MFR"].at[u], ups[u]).wait_recv()
        total = total + s["MFR"][u]
    MO = s["MO"]
    MO[rows_of(at, 32), :] = total
    launch(lambda at=at: small(6, MO.at[rows_of(at, 32)], MO.at[rows_of(at, 32)], p2))
    sV.stage6()
    sH.stage6()
    outs = [lg_copy]
    outs.append(sR.stage7(qf.at[1], s["ls"].at[9]))
    sY.stage5()
    o = at + 32 - 64 * b2
    small(6, MO.at[rows_of(o, 32)], MO.at[rows_of(o, 32)], p2).wait_recv()
    at = at - 32 * b2
    launch(lambda at=at: small(7, MO.at[rows_of(at, 64)], MO.at[rows_of(at, 64)], p1))
    sD.stage4()
    sY.stage6()
    o = at + 64 - 128 * b1
    small(7, MO.at[rows_of(o, 64)], MO.at[rows_of(o, 64)], p1).wait_recv()
    at = at - 64 * b1
    launch(lambda at=at: small(8, MO.at[rows_of(at, 128)], MO.at[rows_of(at, 128)], pc))
    outs.append(sV.stage7(qf.at[2], s["ls"].at[10]))
    outs.append(sH.stage7(qh, s["ls"].at[11]))
    sD.stage5()
    outs.append(sY.stage7(qy, s["ls"].at[12]))
    o = at + 128 - 256 * b0
    small(8, MO.at[rows_of(o, 128)], MO.at[rows_of(o, 128)], pc).wait_recv()
    c = pltpu.make_async_copy(MO, misc, s["ls"].at[13])
    c.start()
    outs.append(c)
    sD.stage6()
    outs.append(sD.stage7(qf.at[0], s["ls"].at[14]))
    for c in outs:
        c.wait()
    for st in (sD, sR, sV, sY, sH):
        st.release()
    for make in sends:
        make().wait_send()


def step_call(wide, token_count, n_task, lat, actT, ids, steps, tgt, rb, rf, vb, vf, fw, dw, hw, tab, vec):
    n_tok = lat.shape[0]
    ups_n = wide.bit_length() - 4
    V = pltpu.VMEM
    D = pltpu.SemaphoreType.DMA
    scratch = dict(
        WF=V((HID, 3 * HID), bf16), WD=V((HID, LAT), bf16), HT=V((2, 128, HID), bf16),
        SM=V((NZ, 64, 128), bf16), VR=V((40, 128), f32), VEC=V((16, HID), f32), VFULL=V((96, 128), f32),
        X=V((ALL, HID), bf16), XT=V((HID, ALL), bf16), XTp=V((HID, ALL), bf16),
        U=V((ALL, HID), f32), AT=V((HID, ALL), bf16), ATp=V((HID, ALL), bf16),
        DU=V((ALL, LAT), f32),
        PRE=V((ROWS, HID), f32), TT=V((2 * ROWS, HID), f32), ACT=V((ROWS, HID), bf16),
        GP=V((ALL, 3 * HID), bf16), GPp=V((3, ALL, HALF), bf16), GDL=V((ALL, LAT), bf16), GDLp=V((ALL, YHALF), bf16),
        INV=V((ALL, 128), f32), HINV=V((ROWS, 128), f32),
        SIDE=V((3, ROWS, 16), f32), ONES=V((256, 256), bf16),
        VA=V((3, 24, HID), f32), VT=V((24, LAT), f32), GEMB=V((ROWS, BLK), f32),
        ST=V((16, 384), f32), IDR=V((8, 384), i32), PKT=V((128, ROWS), bf16), AC=V((16, 384), f32),
        DWA=V((HID, HALF), f32), DWY=V((HID, YHALF), f32), STG=V((2, SHARD, HALF), f32),
        DWH=V((2, 128, HID), f32), DWHp=V((128, HID), f32),
        MS=V((256, 128), f32), MO=V((256, 128), f32), MZ=V((NZ, 32, 128), f32),
        MR0=V((128, 128), f32), MR1=V((64, 128), f32), MR2=V((32, 128), f32),
        QF=V((3, 8, SENT + 16, 128), i16), QY=V((8, 80, YHALF), i16), QH=V((8, 48, BLK), i16),
    )
    for name, rows, cols in (("", SENT + 16, 128), ("Y", 80, YHALF), ("H", 48, BLK)):
        scratch["E1" + name] = V((4, 2, rows, cols), i16)
        scratch["E2" + name] = V((4, rows, cols), i16)
        scratch["E3" + name] = V((3, rows, cols), i16)
    for name, rows, cols in (("D", SENT + 16, 128), ("R", SENT + 16, 128), ("V", SENT + 16, 128), ("Y", 80, YHALF), ("H", 48, BLK)):
        scratch["R1" + name] = V((4, 2, rows, cols), i16)
        scratch["R2" + name] = V((4, rows, cols), i16)
        scratch["R3" + name] = V((3, rows, cols), i16)
    if ups_n:
        for i, (rows, cols) in enumerate(((SENT + 16, 128),) * 3 + ((80, YHALF), (48, BLK))):
            scratch["FR%d" % i] = V((ups_n, rows, cols), i16)
        scratch["MF"] = V((ups_n, 32, 128), f32)
        scratch["MFR"] = V((ups_n, 32, 128), f32)
    scratch.update(
        ls=D((16,)), gs=D((5, 3, 6)), gr=D((5, 3, 6)), ms=D((4,)), mr=D((4,)),
        xs=D((11,)), xr=D((11,)), ss=D((5, 16 + ups_n)), sr=D((5, 16 + ups_n)), vs=D((9 + ups_n,)), vr=D((9 + ups_n,)),
    )
    vm, hb = pl.BlockSpec(memory_space=pltpu.VMEM), pl.BlockSpec(memory_space=pl.ANY)
    return pl.pallas_call(
        functools.partial(step_kernel, wide, token_count, n_tok, n_task),
        out_shape=(
            jax.ShapeDtypeStruct((n_tok, LAT), f32),
            jax.ShapeDtypeStruct((3, 8, SENT + 16, 128), i16),
            jax.ShapeDtypeStruct((8, 80, YHALF), i16),
            jax.ShapeDtypeStruct((8, 48, BLK), i16),
            jax.ShapeDtypeStruct((256, 128), f32),
        ),
        in_specs=[hb, vm, vm, vm, hb, vm, vm, vm, vm, hb, hb, vm, vm, vm],
        out_specs=[hb] * 5,
        scratch_shapes=scratch,
        compiler_params=pltpu.CompilerParams(
            collective_id=0, has_side_effects=True, vmem_limit_bytes=64 * 2**20),
    )(lat, actT, ids, steps, tgt, rb, rf, vb, vf, fw, dw, hw, tab, vec)


def adam(master, moment, second, gradient, rate):
    moment_new = moment_decay * moment + (1.0 - moment_decay) * gradient
    second_new = moment_decay * second + (1.0 - moment_decay) * gradient * gradient
    correct = 1.0 - moment_decay**STEP
    normed = moment_new / correct / (jnp.sqrt(second_new / correct) + adam_eps)
    return master - rate * (normed + weight_decay * master), moment_new, second_new


def adam_kernel(n_task, lg, qf, qy, qh, misc, *refs):
    arrays, refs = refs[:15], refs[15:]
    outs, (lg_out, fi, fo, di, do, hi, ho, sf, sy, sh, sl, gh, vr, sem) = refs[:15], refs[15:]
    first, dyn, heads, table, vecs = (arrays[3 * k : 3 * k + 3] for k in range(5))
    first_out, dyn_out, heads_out, table_out, vecs_out = (outs[3 * k : 3 * k + 3] for k in range(5))
    z = lax.axis_index("narrow")

    def part(i):
        return pl.ds(pl.multiple_of(HALF * i, HALF), HALF)

    def load_first(k, i):
        return pltpu.make_async_copy(first[k].at[:, part(i)], fi.at[k, :, part(i)], sem.at[k, i])

    def save_first(k, i):
        return pltpu.make_async_copy(fo.at[k, :, part(i)], first_out[k].at[:, part(i)], sem.at[3 + k, i])

    whole = [pltpu.make_async_copy(*c, sem.at[6, i]) for i, c in enumerate(((qf, sf), (qy, sy), (qh, sh), (lg, sl)))]
    others = [
        pltpu.make_async_copy(src[k], dst.at[k], sem.at[7 + j, k])
        for j, (src, dst) in enumerate(((dyn, di), (heads, hi))) for k in range(3)
    ]
    saves = [
        pltpu.make_async_copy(src.at[k], dst[k], sem.at[7 + j, 3 + k])
        for j, (dst, src) in enumerate(((dyn_out, do), (heads_out, ho))) for k in range(3)
    ]
    whole[0].start()
    for i in range(2):
        for k in range(3):
            load_first(k, i).start()
    whole[1].start()
    whole[2].start()
    for c in others:
        c.start()
    for i in range(2, 6):
        for k in range(3):
            load_first(k, i).start()
    whole[3].start()
    whole[0].wait()

    def first_part(i, c):
        for k in range(3):
            load_first(k, i).wait()
        for j in range(4):
            cols = pl.ds(pl.multiple_of(HALF * i + 128 * j, 128), 128)
            g = decode(sf.at[lax.div(i, 2), 4 * lax.rem(i, 2) + j])[0:SHARD, :]
            new = adam(fi[0, :, cols], fi[1, :, cols], fi[2, :, cols], g, matrix_rate)
            for k in range(3):
                fo[k, :, cols] = new[k]
        for k in range(3):
            save_first(k, i).start()
        return c
    lax.fori_loop(0, 2, first_part, 0)

    whole[1].wait()
    for c in others[0:3]:
        c.wait()

    def dyn_part(i, c):
        cols = pl.ds(pl.multiple_of(YHALF * lax.div(i, 4), 128), YHALF)
        rows = pl.ds(pl.multiple_of(64 * lax.rem(i, 4), 64), 64)
        new = adam(di[0, rows, cols], di[1, rows, cols], di[2, rows, cols], decode(sy.at[i]), matrix_rate)
        for k in range(3):
            do[k, rows, cols] = new[k]
        return c
    lax.fori_loop(0, 8, dyn_part, 0)
    for c in saves[0:3]:
        c.start()

    whole[2].wait()
    for c in others[3:6]:
        c.wait()
    for k in range(2):
        for j in range(4):
            gh[32 * j : 32 * j + 32, :] = decode(sh.at[4 * k + j])
        new = adam(hi[0, :, k, :], hi[1, :, k, :], hi[2, :, k, :], gh[0:BINS, :], matrix_rate)
        for i in range(3):
            ho[i, :, k, :] = new[i]
    for c in saves[3:6]:
        c.start()
    whole[3].wait()
    lg_save = pltpu.make_async_copy(sl, lg_out, sem.at[6, 4])
    lg_save.start()
    lax.fori_loop(2, 6, first_part, 0)

    g = misc[pl.ds(pl.multiple_of(128 + 32 * z, 32), 32), :]
    new = adam(*(r[...] for r in table), g[0:n_task, 0:TEMB], vector_rate)
    for k in range(3):
        table_out[k][...] = new[k]

    n_vec = vecs[0].shape[0]
    full = n_vec // 128
    left = n_vec - 128 * full
    g = sum(jnp.where(z == q, misc[at : at + 25, :], 0.0) for q, at in enumerate((0, 22, 45, 67)))
    turned = pltpu.roll(g, 64, 1)
    g = jnp.where(lax.rem(z, 2) == 1, jnp.where(lanes(128) < 64, turned[0:24, :], turned[1:25, :]), g[0:24, :])
    vr[...] = jnp.zeros_like(vr)
    for k in range(3):
        for r in range(full):
            vr[k, r : r + 1, :] = vecs[k][pl.ds(128 * r, 128)].reshape(1, 128)
        vr[k, full : full + 1, 0:left] = vecs[k][pl.ds(128 * full, left)].reshape(1, left)
    new = adam(vr[0], vr[1], vr[2], g, vector_rate)
    for k in range(3):
        for r in range(full):
            vecs_out[k][pl.ds(128 * r, 128)] = new[k][r : r + 1, :].reshape(128)
        vecs_out[k][pl.ds(128 * full, left)] = new[k][full : full + 1, 0:left].reshape(left)

    def first_saved(i, c):
        for k in range(3):
            save_first(k, i).wait()
        return c
    lax.fori_loop(0, 6, first_saved, 0)
    for c in saves:
        c.wait()
    lg_save.wait()


def adam_call(lg, qf, qy, qh, misc, arrays):
    V = pltpu.VMEM
    vm, hb = pl.BlockSpec(memory_space=pltpu.VMEM), pl.BlockSpec(memory_space=pl.ANY)
    first, dyn, heads = (arrays[k].shape for k in (0, 3, 6))
    out = [jax.ShapeDtypeStruct(a.shape, f32) for a in arrays] + [jax.ShapeDtypeStruct(lg.shape, f32)]
    return pl.pallas_call(
        functools.partial(adam_kernel, arrays[9].shape[0]),
        out_shape=out,
        in_specs=[hb] * 4 + [vm] + [hb] * 9 + [vm] * 6,
        out_specs=[hb] * 9 + [vm] * 6 + [hb],
        scratch_shapes=[
            V((3, *first), f32), V((3, *first), f32), V((3, *dyn), f32), V((3, *dyn), f32),
            V((3, *heads), f32), V((3, *heads), f32),
            V(qf.shape, i16), V(qy.shape, i16), V(qh.shape, i16), V(lg.shape, f32), V((128, BLK), f32), V((3, 24, 128), f32),
            pltpu.SemaphoreType.DMA((9, 6)),
        ],
        compiler_params=pltpu.CompilerParams(vmem_limit_bytes=64 * 2**20),
    )(lg, qf, qy, qh, misc, *arrays)


def per_device(
    latents, actions, task_ids, steps_left, target_latents, reward_bins, reward_frac, value_bins, value_frac,
    first_weight, first_moment, first_second, dynamics_weight, dynamics_moment, dynamics_second,
    heads_weight, heads_moment, heads_second, task_table, table_moment, table_second,
    vector_params, vector_moment, vector_second,
):
    n_tok = latents.shape[0]
    wide = lax.axis_size("wide")
    token_count = float(HORIZON * n_tok * wide * lax.axis_size("narrow"))
    n_task = task_table.shape[0]
    to_class = lambda a: a.transpose(2, 0, 1)
    lg, qf, qy, qh, misc = step_call(
        wide, token_count, n_task, latents, actions.transpose(1, 2, 0), task_ids,
        steps_left, target_latents.transpose(1, 0, 2),
        reward_bins.T, reward_frac.T, value_bins.T, value_frac.T,
        first_weight, dynamics_weight, to_class(heads_weight), task_table, vector_params)
    heads = [to_class(a) for a in (heads_weight, heads_moment, heads_second)]
    new = adam_call(lg, qf, qy, qh, misc, [
        first_weight, first_moment, first_second, dynamics_weight, dynamics_moment, dynamics_second, *heads,
        task_table, table_moment, table_second, vector_params, vector_moment, vector_second])
    return (new[15], *new[0:6], *(a.transpose(1, 2, 0) for a in new[6:9]), *new[9:15])


def solution(mesh):
    tokens = ("wide", "narrow")
    in_specs = (
        P(tokens, None), P(tokens, None, None), P(tokens), P(tokens), P(tokens, None, None),
        P(tokens, None), P(tokens, None), P(tokens, None), P(tokens, None),
        *(P("narrow", None),) * 6, *(P(None, "narrow", None),) * 3, *(P("narrow", None),) * 3, *(P("narrow"),) * 3,
    )
    out_specs = (
        P(tokens, None), *(P("narrow", None),) * 6, *(P(None, "narrow", None),) * 3,
        *(P("narrow", None),) * 3, *(P("narrow"),) * 3,
    )
    return jax.shard_map(per_device, mesh=mesh, in_specs=in_specs, out_specs=out_specs, check_vma=False)
```

```python
import functools

import jax
import jax.numpy as jnp
from jax import lax
from jax.experimental import pallas as pl
from jax.experimental.pallas import tpu as pltpu
from jax.sharding import PartitionSpec as P

f32, bf16, i16, i32 = jnp.float32, jnp.bfloat16, jnp.int16, jnp.int32
MESH = pl.DeviceIdType.MESH

LAT = 768
HID = 1024
BINS = 101
TEMB = 96
ACTN = 8
HORIZON = 3
STEP = 5
NZ = 4
SHARD = 218
SENT = 224
BLK = 256
ROWS = 320
RB = 320
NB = ROWS // RB
ALL = HORIZON * ROWS
HALF = HID // 2
YHALF = LAT // 2
BOTT = 112
TASK_LANE = LAT + ACTN - 3 * SHARD
ACT_LANE = LAT - 3 * SHARD

norm_eps = 1e-05
adam_eps = 1e-08
moment_decay = 0.5
horizon_decay = 0.5
weight_decay = 0.01
matrix_rate = 0.03
vector_rate = 0.3
consistency_coef = 20.0
head_coef = 0.1

NN = (((1,), (0,)), ((), ()))
NT = (((1,), (1,)), ((), ()))
TN = (((0,), (0,)), ((), ()))


def dot(a, b, dims=NN):
    return lax.dot_general(a, b, dims, preferred_element_type=f32)


def loop(start, end, body, carry):
    for i in range(start, end):
        carry = body(i, carry)
    return carry


def whole_of(start, unit):
    return start if isinstance(start, int) else pl.multiple_of(start, unit)


def lanes(n):
    return lax.broadcasted_iota(i32, (1, n), 1)


def block_rows(i, base=0):
    return pl.ds(whole_of(base + i * RB, RB), RB)


def encode(v, ref):
    rows = v.shape[0]
    top = jnp.max(jnp.abs(v), 0, keepdims=True)
    e = jnp.clip(jnp.ceil(jnp.log2(jnp.maximum(top, 1e-37))), -100.0, 120.0)
    ref[0:rows, :] = jnp.round(v * jnp.exp2(14.9 - e)).astype(i32).astype(i16)
    ref[rows : rows + 16, :] = jnp.broadcast_to(e, (16, v.shape[1])).astype(i32).astype(i16)


def decode(ref):
    rows = ref.shape[0] - 16
    e = ref[rows : rows + 16, :].astype(i32).astype(f32)[0:1, :]
    return ref[0:rows, :].astype(i32).astype(f32) * jnp.exp2(e - 14.9)


def pack_tiles(x):
    inside = lanes(BLK) < SHARD
    b0 = jnp.where(inside, x[:, 0:256], 0.0)
    b1 = jnp.where(inside, pltpu.roll(x[:, 128:512], 384 - 90, 1)[:, 0:256], 0.0)
    b2 = jnp.where(inside, pltpu.roll(x[:, 384:768], 384 - 52, 1)[:, 0:256], 0.0)
    b3 = jnp.where(lanes(128) < ACT_LANE, pltpu.roll(x[:, 640:768], 128 - 14, 1), 0.0)
    return b0, b1, b2, b3


def unpack_tiles(g):
    inside = lanes(BLK) < SHARD
    empty = jnp.zeros((g.shape[0], 128), f32)
    b0 = jnp.where(inside, g[:, 0:256], 0.0)
    b1 = pltpu.roll(jnp.concatenate([jnp.where(inside, g[:, 256:512], 0.0), empty], 1), 90, 1)
    b2 = pltpu.roll(jnp.concatenate([jnp.where(inside, g[:, 512:768], 0.0), empty], 1), 52, 1)
    b3 = pltpu.roll(jnp.where(lanes(128) < ACT_LANE, g[:, 768:896], 0.0), 14, 1)
    return jnp.concatenate(
        [
            b0[:, 0:128],
            b0[:, 128:256] + b1[:, 0:128],
            b1[:, 128:256],
            b1[:, 256:384] + b2[:, 0:128],
            b2[:, 128:256],
            b2[:, 256:384] + b3,
        ],
        1,
    )


def group_sums(x, ones):
    parts = []
    for j in range(0, x.shape[1], 256):
        v = x[:, j : j + 256]
        high = v.astype(bf16)
        low = (v - high.astype(f32)).astype(bf16)
        parts.append(dot(high, ones) + dot(low, ones))
    return jnp.concatenate(parts, 1)


def mish_parts(n):
    u = jnp.exp(jnp.minimum(n, 40.0))
    q = u * (u + 2.0)
    r = 1.0 / (q + 2.0)
    bent = q * r
    return bent, bent + (4.0 * n) * (u * (u + 1.0)) * (r * r)


def add_columns(acc, values):
    for k, v in enumerate(values):
        total = acc[8 * k : 8 * k + 8, :]
        for j in range(v.shape[0] // 8):
            total = total + v[8 * j : 8 * j + 8, :]
        acc[8 * k : 8 * k + 8, :] = total


def rcopy(src, dst, send_sem, recv_sem, device):
    return pltpu.make_async_remote_copy(
        src_ref=src, dst_ref=dst, send_sem=send_sem, recv_sem=recv_sem, device_id=device, device_id_type=MESH
    )


def step_kernel(wide, token_count, n_tok, n_task, lat, actT, ids, steps, tgt, rb, rf, vb, vf, fw, dw, hw, tab, vec,
                lg, qf, qy, qh, misc, **s):
    ups_n = wide.bit_length() - 4
    w, z = lax.axis_index("wide"), lax.axis_index("narrow")
    b0, b1, b2 = lax.rem(w, 2), lax.rem(lax.div(w, 2), 2), lax.rem(lax.div(w, 4), 2)
    pc, p1, p2 = (w + 1 - 2 * b0, z), (w + 2 - 4 * b1, z), (w + 4 - 8 * b2, z)
    zs = [(w, lax.rem(z + d, NZ)) for d in range(NZ)]
    from_z = [lax.rem(z + NZ - d, NZ) for d in range(NZ)]
    ups = []
    for u in range(ups_n):
        bit = 8 << u
        ups.append((w + bit - 2 * bit * lax.rem(lax.div(w, bit), 2), z))
    me = b0 * 4 + b1 * 2 + b2
    own = b1 * 2 + b2
    me_1, me_2, me_12 = me + 2 - 4 * b1, me + 1 - 2 * b2, 4 * b0 + 3 - own
    mine_of_8 = 4 * b0
    sends = []

    def pick(odd, even_value, odd_value):
        return even_value + odd * (odd_value - even_value)

    def launch(make):
        make().start()
        sends.append(make)

    X, XT, XTp, U, AT, ATp, DU = s["X"], s["XT"], s["XTp"], s["U"], s["AT"], s["ATp"], s["DU"]
    WF, WD, HT, SM, VEC = s["WF"], s["WD"], s["HT"], s["SM"], s["VEC"]
    PRE, ACT, TT = s["PRE"], s["ACT"], s["TT"]
    TU, TS = TT.at[pl.ds(0, ROWS)], TT.at[pl.ds(ROWS, ROWS)]
    GP, GPp, GDL, GDLp = s["GP"], s["GPp"], s["GDL"], s["GDLp"]
    INV, SIDE, ONES, VA, VT, GEMB = (
        s["INV"], s["SIDE"], s["ONES"], s["VA"], s["VT"], s["GEMB"])

    barrier = pltpu.get_barrier_semaphore()
    peers = [pc, p1, p2] + zs[1:] + ups
    for p in peers:
        pl.semaphore_signal(barrier, inc=1, device_id=p, device_id_type=MESH)

    STG = s["STG"]
    loads = []

    def load_first(part):
        return pltpu.make_async_copy(
            fw.at[:, pl.ds(HALF * part, HALF)], STG.at[part % 2], s["ls"].at[part % 2])

    loads.append(pltpu.make_async_copy(dw, DU.at[pl.ds(0, BLK)], s["ls"].at[3]))
    loads.append(pltpu.make_async_copy(lat, GDL.at[pl.ds(0, n_tok)], s["ls"].at[4]))
    load_first(0).start()
    load_first(1).start()
    for c in loads:
        c.start()

    def cast_first(br):
        for part in (2 * br, 2 * br + 1):
            load_first(part).wait()
            rows = jnp.concatenate([STG[part % 2].astype(bf16), jnp.zeros((SENT - SHARD, HALF), bf16)], 0)
            WF[pl.ds(whole_of(BLK * z, BLK), SENT), HALF * part : HALF * part + HALF] = rows
            if part < 4:
                load_first(part + 2).start()

    cast_first(0)
    pl.semaphore_wait(barrier, len(peers))

    gs, gr = s["gs"], s["gr"]

    class Item:
        def __init__(self, index, view):
            self.i, self.view = index, view

        def _copy(self, d, kind, piece, device):
            view = self.view(*piece)
            return rcopy(view, view, gs.at[self.i, d - 1, kind], gr.at[self.i, d - 1, kind], device)

        def _recv(self, d, kind, *piece):
            self._copy(d, kind, piece, pc).wait_recv()

        def _send(self, d, kind, device, *piece):
            launch(lambda: self._copy(d, kind, piece, device))

        def start(self):
            for d in (1, 3, 2):
                self._send(d, 0, zs[d], z, me, 1, None)

        def spread(self, *ds):
            for d in ds or (1, 3, 2):
                self._recv(d, 0, from_z[d], me, 1, None)
                self._send(d, 1, p1, from_z[d], me, 1, None)
                self._send(d, 2, p2, from_z[d], me, 1, None)

        def forward(self, *ds):
            for d in ds or (1, 3, 2):
                q = from_z[d]
                self._recv(d, 1, q, me_1, 1, None)
                self._send(d, 3, p2, q, me_1, 1, 0)
                self._recv(d, 2, q, me_2, 1, None)
                self._send(d, 4, p1, q, me_2, 1, 1)

        def cross(self, *ds):
            for d in ds or (1, 3, 2):
                q = from_z[d]
                self._recv(d, 3, q, me_12, 1, 0)
                self._recv(d, 4, q, me_12, 1, 1)
                self._send(d, 5, pc, q, mine_of_8, 4, None)

        def finish(self):
            for d in (1, 3, 2):
                self._recv(d, 5, from_z[d], 4 - 4 * b0, 4, None)

    def first_view(br):
        def view(q, at, n, half):
            lo, size = (0, SENT) if half is None else (BOTT * half, BOTT)
            return WF.at[pl.ds(whole_of(BLK * q + lo, 16), size), pl.ds(whole_of(HID * br + 128 * at, 128), 128 * n)]
        return view

    def dyn_view(q, at, n, half):
        lo, size = (0, 32 * n) if half is None else (16 * half, 16)
        return WD.at[pl.ds(whole_of(BLK * q + 32 * at + lo, 16), size)]

    def heads_view(q, at, n, half):
        cols = pl.ds(whole_of(BLK * q, BLK), BLK)
        rows = pl.ds(whole_of(16 * at, 16), 16 * n)
        if half is None:
            return HT.at[:, rows, cols]
        return HT.at[pl.ds(half, 1), rows, cols]

    gD, gY, gR, gV, gH = (
        Item(0, first_view(0)), Item(1, dyn_view), Item(2, first_view(1)), Item(3, first_view(2)), Item(4, heads_view))

    def vec_rows():
        n_vec = vec.shape[0]
        whole = n_vec // 128
        VR = s["VR"]
        VR[...] = jnp.zeros_like(VR)
        for r in range(whole):
            VR[r + 1 : r + 2, :] = vec[pl.ds(128 * r, 128)].reshape(1, 128)
        left = n_vec - 128 * whole
        VR[whole + 1 : whole + 2, 0:left] = vec[pl.ds(128 * whole, left)].reshape(1, left)
        plain = VR[1:33, :]
        moved = jnp.where(lanes(128) < 64, pltpu.roll(VR[0:32, :], 64, 1), pltpu.roll(plain, 64, 1))
        return jnp.where(lax.rem(z, 2) == 1, moved, plain).astype(bf16)

    gD.start()
    frame = vec_rows()
    SM[z, 0:32, :] = frame
    SM[z, 32:64, :] = jnp.zeros((32, 128), bf16)
    SM[z, 32 : 32 + n_task, 0:TEMB] = tab[...].astype(bf16)
    for d in (1, 3, 2):
        launch(lambda d=d: rcopy(SM.at[z], SM.at[z], s["ms"].at[d], s["mr"].at[d], zs[d]))
    loads[0].wait()
    WD[pl.ds(whole_of(BLK * z, BLK), BLK), :] = DU[0:BLK, :].astype(bf16)
    gY.start()
    cast_first(1)
    gD.spread(1, 3)
    own_cols = pl.ds(whole_of(BLK * z, BLK), BLK)
    for k in range(2):
        PRE[0:128, 0:BLK] = jnp.zeros((128, BLK), f32)
        PRE[0:BINS, 0:BLK] = hw[:, k, :]
        HT[k, :, own_cols] = PRE[0:128, 0:BLK].astype(bf16)
    gD.spread(2)
    gR.start()
    gH.start()
    cast_first(2)

    GDL[n_tok:ROWS, :] = jnp.zeros((ROWS - n_tok, LAT), bf16)
    for q in range(NZ):
        WF[BLK * q + SENT : BLK * q + BLK, :] = jnp.zeros((BLK - SENT, 3 * HID), bf16)
    loads[1].wait()

    gD.forward()
    idr = s["IDR"]
    idr[...] = jnp.full_like(idr, -1)
    idr[0:1, 0:n_tok] = ids[...].reshape(1, n_tok)
    slot = lax.broadcasted_iota(i32, (128, 1), 0)
    task = jnp.where(slot % 32 < n_task, n_task * (slot // 32) + slot % 32, -2)
    PKT = s["PKT"]
    PKT[...] = jnp.where(idr[0:1, 0:ROWS] == task, 1.0, 0.0).astype(bf16)
    gD.cross()
    gV.start()

    for d in (1, 3, 2):
        q = from_z[d]
        rcopy(SM.at[q], SM.at[q], s["ms"].at[d], s["mr"].at[d], pc).wait_recv()
    full = s["VFULL"]
    full[...] = jnp.zeros_like(full)
    for q, at in enumerate((0, 22, 45, 67)):
        full[at : at + 24, :] = full[at : at + 24, :] + SM[q, 0:32, :].astype(f32)[0:24, :]
    for r in range(12):
        n, first = (8, 8 * r) if r < 9 else (6, 72 + 6 * (r - 9))
        for j in range(n):
            VEC[r : r + 1, 128 * j : 128 * j + 128] = full[first + j : first + j + 1, :]
    place = jnp.concatenate([SM[q, 32:64, :] for q in range(NZ)], 0).astype(f32)
    table = pltpu.roll(jnp.concatenate([place, jnp.zeros_like(place)], 1), TASK_LANE, 1).astype(bf16)
    AC = s["AC"]
    AC[...] = jnp.zeros_like(AC)
    act_to = jnp.where(
        lax.broadcasted_iota(i32, (16, BLK), 0) + ACT_LANE == lax.broadcasted_iota(i32, (16, BLK), 1), 1.0, 0.0
    ).astype(bf16)
    rows_of_task = dot(PKT[...], table, TN)
    gY.spread()
    for t in range(3):
        AC[0:ACTN, 0:n_tok] = actT[t].astype(f32)
        X[ROWS * t : ROWS * t + ROWS, 768:1024] = (rows_of_task + dot(AC[:, 0:ROWS].astype(bf16), act_to, TN)).astype(bf16)

    def later_setup():
        tile = lax.broadcasted_iota(i32, (256, 256), 0) // 8 == lax.broadcasted_iota(i32, (256, 256), 1) // 8
        ONES[...] = jnp.where(tile, 1.0, 0.0).astype(bf16)
        st = s["ST"]
        st[...] = jnp.zeros_like(st)
        st[0:1, 0:n_tok] = steps[...].reshape(1, n_tok).astype(f32)
        for t in range(3):
            for k, ref in enumerate((rb, rf, vb, vf)):
                st[k + 1 : k + 2, 0:n_tok] = ref[t : t + 1, :].astype(f32)
            SIDE[t] = st[...].T[0:ROWS, :]
        for ref in (VA, VT, GEMB, s["DWH"], s["MS"]):
            ref[...] = jnp.zeros_like(ref)

    def put_latents(rows, values):
        b0, b1, b2, b3 = pack_tiles(values)
        X[rows, 0:768] = jnp.concatenate((b0, b1, b2), 1).astype(bf16)
        X[rows, 768:896] = (X[rows, 768:896].astype(f32) + b3).astype(bf16)

    put_latents(block_rows(0), GDL[0:ROWS, :].astype(f32))
    gD.finish()

    def matmul(out, orows, n, width, left, right, dims=NN):
        def tile_step(j, c):
            cols = pl.ds(j * width, width)
            out[orows, cols] = dot(left, right(cols), dims)
            return c
        loop(0, n // width, tile_step, 0)

    def first_forward(br, base):
        def tile_step(j, c):
            cols = pl.ds(j * 512, 512)
            from_cols = pl.ds(whole_of(HID * br + j * 512, 512), 512)
            PRE[:, cols] = dot(X[pl.ds(base, ROWS), :], WF[:, from_cols])
            return c
        loop(0, 2, tile_step, 0)

    def norm_mish(br, unit, inv, unit_base, slope):
        bias, gain, shift = (VEC[pl.ds(3 * br + k, 1), :] for k in range(3))

        def step(i, c):
            rows = block_rows(i)
            p = PRE[rows, :] + bias
            ce = p - jnp.mean(p, -1, keepdims=True)
            iv = lax.rsqrt(jnp.mean(ce * ce, -1, keepdims=True) + norm_eps)
            un = ce * iv
            n = un * gain + shift
            bent, sl = mish_parts(n)
            ACT[rows, :] = (n * bent).astype(bf16)
            if slope is not None:
                slope[rows, :] = sl
            unit[block_rows(i, unit_base), :] = un
            inv[block_rows(i, unit_base), :] = jnp.broadcast_to(iv, (RB, 128))
            return c
        loop(0, NB, step, 0)

    def dyn_forward(t, c):
        base = whole_of(ROWS * t, RB)
        first_forward(0, base)

        @pl.when(t == 0)
        def _():
            gY.forward()
        norm_mish(0, U, INV, base, None)

        @pl.when(t == 0)
        def _():
            gY.cross()
            gR.spread()
            later_setup()
            gY.finish()

        @pl.when(t == 1)
        def _():
            gR.forward()

        @pl.when(t == 2)
        def _():
            gH.cross()
        matmul(TU, pl.ds(0, ROWS), LAT, 384, ACT[...], lambda cols: WD[:, cols])
        for k in range(3):
            @pl.when(t == k)
            def _():
                AT[:, ROWS * k : ROWS * k + ROWS] = ACT[...].T
        bias, gain, shift = (VEC[9 + k : 10 + k, 0:LAT] for k in range(3))

        def step(i, c):
            rows, at = block_rows(i), block_rows(i, base)
            p = TU[rows, 0:LAT] + bias
            ce = p - jnp.mean(p, -1, keepdims=True)
            iv = lax.rsqrt(jnp.mean(ce * ce, -1, keepdims=True) + norm_eps)
            un = ce * iv
            DU[at, :] = un
            INV[at, 64:128] = jnp.broadcast_to(iv, (RB, 64))

            @pl.when(t < 2)
            def _():
                e = jnp.exp(un * gain + shift)
                put_latents(block_rows(i, base + ROWS), e / group_sums(e, ONES[...]))
            return c
        loop(0, NB, step, 0)

        @pl.when(t == 0)
        def _():
            gH.spread()

        @pl.when(t == 1)
        def _():
            gR.cross()
            gH.forward()
            gV.spread()
        return c

    lax.fori_loop(0, 3, dyn_forward, 0)
    XT[...] = X[...].T
    xs, xr = s["xs"], s["xr"]
    launch(lambda: rcopy(XT, XTp, xs.at[0], xr.at[0], pc))
    launch(lambda: rcopy(AT, ATp, xs.at[1], xr.at[1], pc))
    gR.finish()
    gH.finish()
    gV.forward()

    def norm_backward(br, unit, inv, unit_base, slope, out_base):
        gain, shift = VEC[pl.ds(3 * br + 1, 1), :], VEC[pl.ds(3 * br + 2, 1), :]
        acc = VA.at[br]

        def step(i, c):
            rows, at = block_rows(i), block_rows(i, unit_base)
            un = unit[at, :]
            sl = mish_parts(un * gain + shift)[1] if slope is None else slope[rows, :]
            gn = PRE[rows, :] * sl
            h = gn * gain
            gp = (h - jnp.mean(h, -1, keepdims=True) - un * jnp.mean(h * un, -1, keepdims=True)) * inv[at, 0:1]
            GP[block_rows(i, out_base), pl.ds(whole_of(HID * br, HID), HID)] = gp.astype(bf16)
            add_columns(acc, (gp, gn * un, gn))
            return c
        loop(0, NB, step, 0)

    def head_step(k, t):
        base = whole_of(ROWS * t, RB)
        first_forward(1 + k, base)
        norm_mish(1 + k, TU, s["HINV"], 0, TS)
        logits = dot(ACT[...], HT[k], NT)
        real = lanes(128) < BINS
        logits = jnp.where(real, logits, -1e30)
        e = jnp.exp(logits - jnp.max(logits, -1, keepdims=True))
        soft = e / jnp.sum(e, -1, keepdims=True)
        side = SIDE[t]
        at, frac = (jnp.where(k == 0, side[:, c : c + 1], side[:, c + 2 : c + 3]) for c in (1, 2))
        level = lanes(128).astype(f32)
        hot = jnp.where(level == at, 1.0 - frac, 0.0) + jnp.where(level == at + 1.0, frac, 0.0)
        decay = jnp.where(t == 0, 1.0, jnp.where(t == 1, horizon_decay, horizon_decay**2))
        weight = jnp.where(side[:, 0:1] > t.astype(f32), decay, 0.0) / token_count
        gl = jnp.where(real, weight * head_coef * (soft - hot), 0.0).astype(bf16)
        s["DWH"][k] = s["DWH"][k] + dot(gl.astype(f32).T.astype(bf16), ACT[...])
        PRE[...] = dot(gl, HT[k])
        norm_backward(1 + k, TU, s["HINV"], 0, TS, base)

    def y_rows(t):
        rows, cols = pl.ds(whole_of(ROWS * t, RB), ROWS), pl.ds(pl.multiple_of(YHALF * (1 - b0), 128), YHALF)
        return rcopy(GDL.at[rows, cols], GDLp.at[rows], xs.at[4 + t], xr.at[4 + t], pc)

    def d_rows(t):
        rows, cols = pl.ds(whole_of(ROWS * t, RB), ROWS), pl.ds(pl.multiple_of(HALF * (1 - b0), HALF), HALF)
        return rcopy(GP.at[rows, cols], GPp.at[0, rows], xs.at[7 + t], xr.at[7 + t], pc)

    def dyn_backward(t, between):
        base = whole_of(ROWS * t, RB)
        gain, shift = VEC[10:11, 0:LAT], VEC[11:12, 0:LAT]
        scale = 2.0 * consistency_coef / LAT

        def step(i, c):
            rows, at = block_rows(i), block_rows(i, base)
            un = DU[at, :]
            e = jnp.exp(un * gain + shift)
            sx = e / group_sums(e, ONES[...])
            decay = jnp.where(t == 0, 1.0, jnp.where(t == 1, horizon_decay, horizon_decay**2))
            weight = jnp.where(SIDE[0, rows, 0:1] > t.astype(f32), decay, 0.0) / token_count
            g = weight * scale * (sx - X[at, 0:LAT].astype(f32))
            g = g + jnp.where(t < 2, unpack_tiles(PRE[rows, 0:896]), 0.0)
            gn = sx * (g - group_sums(g * sx, ONES[...]))
            h = gn * gain
            gp = (h - jnp.mean(h, -1, keepdims=True) - un * jnp.mean(h * un, -1, keepdims=True)) * INV[at, 64:65]
            GDL[at, :] = gp.astype(bf16)
            add_columns(VT, (gp, gn * un, gn))
            return c
        loop(0, NB, step, 0)
        y_rows(t).start()
        between()

        def tile_step(j, c):
            cols = pl.ds(j * 512, 512)
            PRE[:, cols] = dot(GDL[pl.ds(base, ROWS), :], WD[cols, :], NT)
            return c
        loop(0, 2, tile_step, 0)
        norm_backward(0, U, INV, base, None, base)
        d_rows(t).start()

    def inputs_backward(t):
        base = whole_of(ROWS * t, RB)

        def tile_step(j, c):
            cols = pl.ds(j * 512, 512)
            PRE[:, cols] = dot(GP[pl.ds(base, ROWS), :], WF[cols, :], NT)
            return c
        loop(0, 2, tile_step, 0)
        GEMB[...] = GEMB[...] + PRE[:, 768:1024]

    rs_s, rs_r = s["ss"], s["sr"]

    class Stream:
        def __init__(self, index, grad, view, E, R, Q, half):
            self.i, self.grad, self.view, self.Q, self.half = index, grad, view, Q, half
            (self.E1, self.E2, self.E3), (self.R1, self.R2, self.R3) = E, R
            self.spent = []

        def _copy(self, at, src, dst, device):
            return rcopy(src, dst, rs_s.at[self.i, at], rs_r.at[self.i, at], device)

        def _recv(self, at, dst):
            self._copy(at, dst, dst, pc).wait_recv()

        def release(self):
            for first, span, ref in self.spent:
                if span is None:
                    self._copy(first, ref, ref, pc).wait_send()
                else:
                    def one(i, c):
                        self._copy(first + i, ref.at[i], ref.at[i], pc).wait_send()
                        return c
                    lax.fori_loop(*span, one, 0)
            self.spent = []

        def _send(self, at, src, dst, device):
            self._copy(at, src, dst, device).start()
            self.spent.append((at, None, src))

        def stage1(self, *span):
            span = span or (0, NZ)

            def one(i, c):
                q = lax.rem(z + 1 + i, NZ)
                odd = lax.rem(q, 2)
                base = pick(odd, 2 - 2 * b1, 1 - b2)
                for j in range(2):
                    encode(self.grad[self.view(q, base + j * (1 + odd))], self.E1.at[i, j])
                self._copy(i, self.E1.at[i], self.R1.at[i], (pick(odd, p1[0], p2[0]), z)).start()
                return c
            lax.fori_loop(*span, one, 0)
            self.spent.append((0, span, self.E1))

        def stage2(self, *span):
            span = span or (0, NZ)

            def one(i, c):
                q = lax.rem(z + 1 + i, NZ)
                odd = lax.rem(q, 2)
                self._recv(i, self.R1.at[i])
                keep = pick(odd, b2, b1)
                other = pick(odd, own + 1 - 2 * b2, own + 2 - 4 * b1)
                encode(self.grad[self.view(q, other)] + decode(self.R1.at[i, 1 - keep]), self.E2.at[i])
                self._copy(4 + i, self.E2.at[i], self.R2.at[i], (pick(odd, p2[0], p1[0]), z)).start()
                mine = self.view(q, own)
                self.grad[mine] = self.grad[mine] + decode(self.R1.at[i, keep])
                return c
            lax.fori_loop(*span, one, 0)
            self.spent.append((4, span, self.E2))

        def stage3(self):
            def one(i, c):
                q = lax.rem(z + 1 + i, NZ)
                self._recv(4 + i, self.R2.at[i])
                encode(self.grad[self.view(q, own)] + decode(self.R2.at[i]), self.E3.at[i])
                self._copy(8 + i, self.E3.at[i], self.R3.at[i], (w, q)).start()
                return c
            lax.fori_loop(0, 3, one, 0)
            self.spent.append((8, (0, 3), self.E3))

        def stage4(self):
            self._recv(7, self.R2.at[3])
            total = self.grad[self.view(z, own)] + decode(self.R2.at[3])
            for i in (0, 2, 1):
                self._recv(8 + i, self.R3.at[i])
                total = total + decode(self.R3.at[i])
            for u in range(ups_n):
                F, FR = self.Q.at[me], s["FR%d" % self.i]
                encode(total, F)
                c = self._copy(16 + u, F, FR.at[u], ups[u])
                c.start()
                self._recv(16 + u, FR.at[u])
                c.wait_send()
                total = decode(F) + decode(FR.at[u])
            encode(total, self.Q.at[me])
            self._send(11, self.Q.at[me], self.Q.at[me], p1)
            self._send(12, self.Q.at[me], self.Q.at[me], p2)

        def stage5(self):
            s1, s2 = me_1, me_2
            n = self.Q.shape[1]
            low, high = pl.ds(0, self.half), pl.ds(self.half, n - self.half)
            self._recv(11, self.Q.at[s1])
            self._send(13, self.Q.at[s1, low], self.Q.at[s1, low], p2)
            self._recv(12, self.Q.at[s2])
            self._send(14, self.Q.at[s2, high], self.Q.at[s2, high], p1)

        def stage6(self):
            s12 = me_12
            n = self.Q.shape[1]
            low, high = pl.ds(0, self.half), pl.ds(self.half, n - self.half)
            self._recv(13, self.Q.at[s12, low])
            self._recv(14, self.Q.at[s12, high])
            mine = self.Q.at[pl.ds(mine_of_8, 4)]
            self._send(15, mine, mine, pc)

        def stage7(self, out, sem):
            self._recv(15, self.Q.at[pl.ds(4 - 4 * b0, 4)])
            c = pltpu.make_async_copy(self.Q, out, sem)
            c.start()
            return c

    def first_slice(q, at):
        return (pl.ds(whole_of(BLK * q, BLK), SENT), pl.ds(whole_of(128 * at, 128), 128))

    def value_slice(q, at):
        cols = HALF * lax.div(q, 2) + 128 * at
        return (pl.ds(whole_of(BLK * lax.rem(q, 2), BLK), SENT), pl.ds(whole_of(cols, 128), 128))

    def y_slice(q, at):
        return (pl.ds(whole_of(BLK * q + 64 * at, 64), 64), slice(None))

    def h_slice(q, at):
        return (b0, pl.ds(whole_of(32 * at, 32), 32), pl.ds(whole_of(BLK * q, BLK), BLK))

    EF = (s["E1"], s["E2"], s["E3"])
    streams = []
    for i, name in enumerate("DRV"):
        streams.append(Stream(
            i, *((TT, value_slice) if name == "V" else (s["DWA"], first_slice)), EF,
            tuple(s["R%d%s" % (k, name)] for k in (1, 2, 3)), s["QF"].at[i], 128))
    sD, sR, sV = streams
    sY = Stream(3, s["DWY"], y_slice, tuple(s["E%dY" % k] for k in (1, 2, 3)),
                tuple(s["R%dY" % k] for k in (1, 2, 3)), s["QY"], 48)
    sH = Stream(4, s["DWH"], h_slice, tuple(s["E%dH" % k] for k in (1, 2, 3)),
                tuple(s["R%dH" % k] for k in (1, 2, 3)), s["QH"], 32)

    def send_half(br):
        def make():
            cols = pl.ds(whole_of(HID * br + HALF * (1 - b0), HALF), HALF)
            return rcopy(GP.at[:, cols], GPp.at[br], xs.at[1 + br], xr.at[1 + br], pc)
        launch(make)

    def wait_x(at, dst):
        rcopy(dst, dst, xs.at[at], xr.at[at], pc).wait_recv()

    def weight_grad(out, n, left, right, arrived, left2, right2):
        def own_tile(j, c):
            cols = pl.ds(pl.multiple_of(j * n, n), n)
            out[:, cols] = dot(left[...], right(j))
            return c
        lax.fori_loop(0, out.shape[1] // n, own_tile, 0)
        arrived()

        def other_tile(j, c):
            cols = pl.ds(pl.multiple_of(j * n, n), n)
            out[:, cols] = out[:, cols] + dot(left2[...], right2(cols))
            return c
        lax.fori_loop(0, out.shape[1] // n, other_tile, 0)

    def first_grad(br, out, arrived):
        weight_grad(
            out, 256, XT,
            lambda j: GP[:, pl.ds(pl.multiple_of(HID * br + HALF * b0 + 256 * j, 256), 256)], arrived,
            XTp, lambda cols: GPp[br, :, cols])

    def value_grad():
        def tile_step(j, c):
            cols = pl.ds(whole_of(j * 256, 256), 256)
            low_cols = pl.ds(whole_of(HALF + j * 256, 256), 256)
            right = GP[:, pl.ds(whole_of(2 * HID + HALF * b0 + 256 * j, 256), 256)]
            total = dot(XT[...], right) + dot(XTp[...], GPp[2, :, cols])
            TT[0:512, cols] = total[0:512, :]
            TT[0:512, low_cols] = total[512:1024, :]
            return c
        lax.fori_loop(0, 2, tile_step, 0)

    def y_grad():
        def arrived():
            wait_x(1, ATp)
            for t in range(3):
                wait_x(4 + t, GDLp.at[pl.ds(ROWS * t, ROWS)])
        weight_grad(
            s["DWY"], 128, AT,
            lambda j: GDL[:, pl.ds(whole_of(YHALF * b0 + 128 * j, 128), 128)], arrived,
            ATp, lambda cols: GDLp[:, cols])
        sY.stage1()

    def head_steps(i, c):
        @pl.when(i == 1)
        def _():
            gV.cross()

        @pl.when(i == 3)
        def _():
            send_half(1)
            gV.finish()

        @pl.when(i == 4)
        def _():
            def arrived():
                wait_x(0, XTp)
                wait_x(2, GPp.at[1])
            first_grad(1, s["DWA"], arrived)
            sR.stage1()

        head_step(lax.div(i, 3), lax.rem(i, 3))
        return c
    lax.fori_loop(0, 6, head_steps, 0)
    send_half(2)
    launch(lambda: rcopy(s["DWH"].at[1 - b0], s["DWHp"], xs.at[10], xr.at[10], pc))
    for t in range(3):
        loads.append(pltpu.make_async_copy(
            tgt.at[t], X.at[pl.ds(ROWS * t, n_tok), pl.ds(0, LAT)], s["ls"].at[5 + t]))
        loads[-1].start()
    sR.stage2()
    for c in loads[2:]:
        c.wait()
    def backward(i, c):
        t = 2 - i

        def last_y():
            @pl.when(i == 2)
            def _():
                y_grad()
        dyn_backward(t, last_y)

        @pl.when(i == 0)
        def _():
            sR.stage3()
            wait_x(3, GPp.at[2])
            value_grad()
            sR.release()
            sV.stage1()
            wait_x(10, s["DWHp"])
            s["DWH"][b0] = s["DWH"][b0] + s["DWHp"][...]
            sH.stage1()

        @pl.when(i == 1)
        def _():
            sR.stage4()
            sV.stage2()
            sH.stage2()

        @pl.when(i == 2)
        def _():
            sR.stage5()
            sV.stage3()
            sH.stage3()
            def arrived():
                for k in range(3):
                    wait_x(7 + k, GPp.at[0, pl.ds(ROWS * k, ROWS)])
            first_grad(0, s["DWA"], arrived)
            sV.release()
            sD.stage1()
            sR.stage6()
        inputs_backward(t)
        return c
    lax.fori_loop(0, 3, backward, 0)
    for k in range(3):
        sends.extend((lambda k=k: y_rows(k), lambda k=k: d_rows(k)))

    def write_latent(i, c):
        rows = block_rows(i)
        DU[rows, :] = unpack_tiles(PRE[rows, 0:896])
        return c
    loop(0, NB, write_latent, 0)
    lg_copy = pltpu.make_async_copy(DU.at[pl.ds(0, n_tok)], lg, s["ls"].at[8])
    lg_copy.start()
    ge = GEMB[...]
    g1 = ge.astype(bf16)
    g2 = (ge - g1.astype(f32)).astype(bf16)
    g3 = (ge - g1.astype(f32) - g2.astype(f32)).astype(bf16)
    pk = PKT[...]
    by_task = dot(pk, g1) + dot(pk, g2) + dot(pk, g3)
    M = s["MS"]
    M[128:256, :] = pltpu.roll(by_task, BLK - TASK_LANE, 1)[:, 0:128]
    for r in range(12):
        acc, n, first = (VA.at[r // 3], 8, 8 * r) if r < 9 else (VT, 6, 72 + 6 * (r - 9))
        k = r % 3
        row = jnp.sum(acc[8 * k : 8 * k + 8, :], 0, keepdims=True)
        for j in range(n):
            M[first + j : first + j + 1, :] = row[:, 128 * j : 128 * j + 128]

    vs, vr = s["vs"], s["vr"]

    def small(at, src, dst, device):
        return rcopy(src, dst, vs.at[at], vr.at[at], device)

    def rows_of(start, n):
        return pl.ds(whole_of(start, 32), n)

    halves = ((0, pc, b0, 128), (1, p1, b1, 64), (2, p2, b2, 32))

    def halve(step, start):
        at, device, bit, n = halves[step]
        launch(lambda: small(at, M.at[rows_of(start + n * (1 - bit), n)], s["MR%d" % step], device))

    def halved(step, start):
        at, device, bit, n = halves[step]
        small(at, s["MR%d" % step], s["MR%d" % step], device).wait_recv()
        mine = rows_of(start + n * bit, n)
        M[mine, :] = M[mine, :] + s["MR%d" % step][...]
        return start + n * bit

    halve(0, 0)
    sY.stage2()
    at = halved(0, 0)
    halve(1, at)
    sD.stage2(0, 2)
    sY.stage3()
    sD.stage2(2, 4)
    at = halved(1, at)
    halve(2, at)
    sV.stage4()
    sH.stage4()
    at = halved(2, at)
    MZ = s["MZ"]
    MZ[z] = M[rows_of(at, 32), :]
    for d in (2, 1, 3):
        launch(lambda d=d: small(2 + d, MZ.at[z], MZ.at[z], zs[d]))
    sD.stage3()
    sV.stage5()
    sH.stage5()
    sY.stage4()
    for d in (1, 3, 2):
        small(2 + d, MZ.at[from_z[d]], MZ.at[from_z[d]], pc).wait_recv()
    total = (MZ[0] + MZ[1]) + (MZ[2] + MZ[3])
    for u in range(ups_n):
        s["MF"][u] = total
        launch(lambda u=u: small(9 + u, s["MF"].at[u], s["MFR"].at[u], ups[u]))
        small(9 + u, s["MFR"].at[u], s["MFR"].at[u], ups[u]).wait_recv()
        total = total + s["MFR"][u]
    MO = s["MO"]
    MO[rows_of(at, 32), :] = total
    launch(lambda at=at: small(6, MO.at[rows_of(at, 32)], MO.at[rows_of(at, 32)], p2))
    sV.stage6()
    sH.stage6()
    outs = [lg_copy]
    outs.append(sR.stage7(qf.at[1], s["ls"].at[9]))
    sY.stage5()
    o = at + 32 - 64 * b2
    small(6, MO.at[rows_of(o, 32)], MO.at[rows_of(o, 32)], p2).wait_recv()
    at = at - 32 * b2
    launch(lambda at=at: small(7, MO.at[rows_of(at, 64)], MO.at[rows_of(at, 64)], p1))
    sD.stage4()
    sY.stage6()
    o = at + 64 - 128 * b1
    small(7, MO.at[rows_of(o, 64)], MO.at[rows_of(o, 64)], p1).wait_recv()
    at = at - 64 * b1
    launch(lambda at=at: small(8, MO.at[rows_of(at, 128)], MO.at[rows_of(at, 128)], pc))
    outs.append(sV.stage7(qf.at[2], s["ls"].at[10]))
    outs.append(sH.stage7(qh, s["ls"].at[11]))
    sD.stage5()
    outs.append(sY.stage7(qy, s["ls"].at[12]))
    o = at + 128 - 256 * b0
    small(8, MO.at[rows_of(o, 128)], MO.at[rows_of(o, 128)], pc).wait_recv()
    c = pltpu.make_async_copy(MO, misc, s["ls"].at[13])
    c.start()
    outs.append(c)
    sD.stage6()
    outs.append(sD.stage7(qf.at[0], s["ls"].at[14]))
    for c in outs:
        c.wait()
    for st in (sD, sR, sV, sY, sH):
        st.release()
    for make in sends:
        make().wait_send()


def step_call(wide, token_count, n_task, lat, actT, ids, steps, tgt, rb, rf, vb, vf, fw, dw, hw, tab, vec):
    n_tok = lat.shape[0]
    ups_n = wide.bit_length() - 4
    V = pltpu.VMEM
    D = pltpu.SemaphoreType.DMA
    scratch = dict(
        WF=V((HID, 3 * HID), bf16), WD=V((HID, LAT), bf16), HT=V((2, 128, HID), bf16),
        SM=V((NZ, 64, 128), bf16), VR=V((40, 128), f32), VEC=V((16, HID), f32), VFULL=V((96, 128), f32),
        X=V((ALL, HID), bf16), XT=V((HID, ALL), bf16), XTp=V((HID, ALL), bf16),
        U=V((ALL, HID), f32), AT=V((HID, ALL), bf16), ATp=V((HID, ALL), bf16),
        DU=V((ALL, LAT), f32),
        PRE=V((ROWS, HID), f32), TT=V((2 * ROWS, HID), f32), ACT=V((ROWS, HID), bf16),
        GP=V((ALL, 3 * HID), bf16), GPp=V((3, ALL, HALF), bf16), GDL=V((ALL, LAT), bf16), GDLp=V((ALL, YHALF), bf16),
        INV=V((ALL, 128), f32), HINV=V((ROWS, 128), f32),
        SIDE=V((3, ROWS, 16), f32), ONES=V((256, 256), bf16),
        VA=V((3, 24, HID), f32), VT=V((24, LAT), f32), GEMB=V((ROWS, BLK), f32),
        ST=V((16, 384), f32), IDR=V((8, 384), i32), PKT=V((128, ROWS), bf16), AC=V((16, 384), f32),
        DWA=V((HID, HALF), f32), DWY=V((HID, YHALF), f32), STG=V((2, SHARD, HALF), f32),
        DWH=V((2, 128, HID), f32), DWHp=V((128, HID), f32),
        MS=V((256, 128), f32), MO=V((256, 128), f32), MZ=V((NZ, 32, 128), f32),
        MR0=V((128, 128), f32), MR1=V((64, 128), f32), MR2=V((32, 128), f32),
        QF=V((3, 8, SENT + 16, 128), i16), QY=V((8, 80, YHALF), i16), QH=V((8, 48, BLK), i16),
    )
    for name, rows, cols in (("", SENT + 16, 128), ("Y", 80, YHALF), ("H", 48, BLK)):
        scratch["E1" + name] = V((4, 2, rows, cols), i16)
        scratch["E2" + name] = V((4, rows, cols), i16)
        scratch["E3" + name] = V((3, rows, cols), i16)
    for name, rows, cols in (("D", SENT + 16, 128), ("R", SENT + 16, 128), ("V", SENT + 16, 128), ("Y", 80, YHALF), ("H", 48, BLK)):
        scratch["R1" + name] = V((4, 2, rows, cols), i16)
        scratch["R2" + name] = V((4, rows, cols), i16)
        scratch["R3" + name] = V((3, rows, cols), i16)
    if ups_n:
        for i, (rows, cols) in enumerate(((SENT + 16, 128),) * 3 + ((80, YHALF), (48, BLK))):
            scratch["FR%d" % i] = V((ups_n, rows, cols), i16)
        scratch["MF"] = V((ups_n, 32, 128), f32)
        scratch["MFR"] = V((ups_n, 32, 128), f32)
    scratch.update(
        ls=D((16,)), gs=D((5, 3, 6)), gr=D((5, 3, 6)), ms=D((4,)), mr=D((4,)),
        xs=D((11,)), xr=D((11,)), ss=D((5, 16 + ups_n)), sr=D((5, 16 + ups_n)), vs=D((9 + ups_n,)), vr=D((9 + ups_n,)),
    )
    vm, hb = pl.BlockSpec(memory_space=pltpu.VMEM), pl.BlockSpec(memory_space=pl.ANY)
    return pl.pallas_call(
        functools.partial(step_kernel, wide, token_count, n_tok, n_task),
        out_shape=(
            jax.ShapeDtypeStruct((n_tok, LAT), f32),
            jax.ShapeDtypeStruct((3, 8, SENT + 16, 128), i16),
            jax.ShapeDtypeStruct((8, 80, YHALF), i16),
            jax.ShapeDtypeStruct((8, 48, BLK), i16),
            jax.ShapeDtypeStruct((256, 128), f32),
        ),
        in_specs=[hb, vm, vm, vm, hb, vm, vm, vm, vm, hb, hb, vm, vm, vm],
        out_specs=[hb] * 5,
        scratch_shapes=scratch,
        compiler_params=pltpu.CompilerParams(
            collective_id=0, has_side_effects=True, vmem_limit_bytes=64 * 2**20),
    )(lat, actT, ids, steps, tgt, rb, rf, vb, vf, fw, dw, hw, tab, vec)


def adam(master, moment, second, gradient, rate):
    moment_new = moment_decay * moment + (1.0 - moment_decay) * gradient
    second_new = moment_decay * second + (1.0 - moment_decay) * gradient * gradient
    correct = 1.0 - moment_decay**STEP
    normed = moment_new / correct / (jnp.sqrt(second_new / correct) + adam_eps)
    return master - rate * (normed + weight_decay * master), moment_new, second_new


def adam_kernel(n_task, lg, qf, qy, qh, misc, *refs):
    arrays, refs = refs[:15], refs[15:]
    outs, (lg_out, fi, fo, di, do, hi, ho, sf, sy, sh, sl, gh, vr, sem) = refs[:15], refs[15:]
    first, dyn, heads, table, vecs = (arrays[3 * k : 3 * k + 3] for k in range(5))
    first_out, dyn_out, heads_out, table_out, vecs_out = (outs[3 * k : 3 * k + 3] for k in range(5))
    z = lax.axis_index("narrow")

    def part(i):
        return pl.ds(pl.multiple_of(HALF * i, HALF), HALF)

    def load_first(k, i):
        return pltpu.make_async_copy(first[k], fi.at[k], sem.at[k, 0])

    def save_first(k, i):
        return pltpu.make_async_copy(fo.at[k, :, part(i)], first_out[k].at[:, part(i)], sem.at[3 + k, i])

    whole = [pltpu.make_async_copy(*c, sem.at[6, i]) for i, c in enumerate(((qf, sf), (qy, sy), (qh, sh), (lg, sl)))]
    others = [
        pltpu.make_async_copy(src[k], dst.at[k], sem.at[7 + j, k])
        for j, (src, dst) in enumerate(((dyn, di), (heads, hi))) for k in range(3)
    ]
    saves = [
        pltpu.make_async_copy(src.at[k], dst[k], sem.at[7 + j, 3 + k])
        for j, (dst, src) in enumerate(((dyn_out, do), (heads_out, ho))) for k in range(3)
    ]
    whole[0].start()
    for k in range(3):
        load_first(k, 0).start()
    whole[1].start()
    whole[2].start()
    for c in others:
        c.start()
    whole[3].start()
    whole[0].wait()
    for k in range(3):
        load_first(k, 0).wait()

    def first_part(i, c):
        for j in range(4):
            cols = pl.ds(pl.multiple_of(HALF * i + 128 * j, 128), 128)
            g = decode(sf.at[lax.div(i, 2), 4 * lax.rem(i, 2) + j])[0:SHARD, :]
            new = adam(fi[0, :, cols], fi[1, :, cols], fi[2, :, cols], g, matrix_rate)
            for k in range(3):
                fo[k, :, cols] = new[k]
        for k in range(3):
            save_first(k, i).start()
        return c
    lax.fori_loop(0, 2, first_part, 0)

    whole[1].wait()
    for c in others[0:3]:
        c.wait()

    def dyn_part(i, c):
        cols = pl.ds(pl.multiple_of(YHALF * lax.div(i, 4), 128), YHALF)
        rows = pl.ds(pl.multiple_of(64 * lax.rem(i, 4), 64), 64)
        new = adam(di[0, rows, cols], di[1, rows, cols], di[2, rows, cols], decode(sy.at[i]), matrix_rate)
        for k in range(3):
            do[k, rows, cols] = new[k]
        return c
    lax.fori_loop(0, 8, dyn_part, 0)
    for c in saves[0:3]:
        c.start()

    whole[2].wait()
    for c in others[3:6]:
        c.wait()
    for k in range(2):
        for j in range(4):
            gh[32 * j : 32 * j + 32, :] = decode(sh.at[4 * k + j])
        new = adam(hi[0, :, k, :], hi[1, :, k, :], hi[2, :, k, :], gh[0:BINS, :], matrix_rate)
        for i in range(3):
            ho[i, :, k, :] = new[i]
    for c in saves[3:6]:
        c.start()
    whole[3].wait()
    lg_save = pltpu.make_async_copy(sl, lg_out, sem.at[6, 4])
    lg_save.start()
    lax.fori_loop(2, 6, first_part, 0)

    g = misc[pl.ds(pl.multiple_of(128 + 32 * z, 32), 32), :]
    new = adam(*(r[...] for r in table), g[0:n_task, 0:TEMB], vector_rate)
    for k in range(3):
        table_out[k][...] = new[k]

    n_vec = vecs[0].shape[0]
    full = n_vec // 128
    left = n_vec - 128 * full
    g = sum(jnp.where(z == q, misc[at : at + 25, :], 0.0) for q, at in enumerate((0, 22, 45, 67)))
    turned = pltpu.roll(g, 64, 1)
    g = jnp.where(lax.rem(z, 2) == 1, jnp.where(lanes(128) < 64, turned[0:24, :], turned[1:25, :]), g[0:24, :])
    vr[...] = jnp.zeros_like(vr)
    for k in range(3):
        for r in range(full):
            vr[k, r : r + 1, :] = vecs[k][pl.ds(128 * r, 128)].reshape(1, 128)
        vr[k, full : full + 1, 0:left] = vecs[k][pl.ds(128 * full, left)].reshape(1, left)
    new = adam(vr[0], vr[1], vr[2], g, vector_rate)
    for k in range(3):
        for r in range(full):
            vecs_out[k][pl.ds(128 * r, 128)] = new[k][r : r + 1, :].reshape(128)
        vecs_out[k][pl.ds(128 * full, left)] = new[k][full : full + 1, 0:left].reshape(left)

    def first_saved(i, c):
        for k in range(3):
            save_first(k, i).wait()
        return c
    lax.fori_loop(0, 6, first_saved, 0)
    for c in saves:
        c.wait()
    lg_save.wait()


def adam_call(lg, qf, qy, qh, misc, arrays):
    V = pltpu.VMEM
    vm, hb = pl.BlockSpec(memory_space=pltpu.VMEM), pl.BlockSpec(memory_space=pl.ANY)
    first, dyn, heads = (arrays[k].shape for k in (0, 3, 6))
    out = [jax.ShapeDtypeStruct(a.shape, f32) for a in arrays] + [jax.ShapeDtypeStruct(lg.shape, f32)]
    return pl.pallas_call(
        functools.partial(adam_kernel, arrays[9].shape[0]),
        out_shape=out,
        in_specs=[hb] * 4 + [vm] + [hb] * 9 + [vm] * 6,
        out_specs=[hb] * 9 + [vm] * 6 + [hb],
        scratch_shapes=[
            V((3, *first), f32), V((3, *first), f32), V((3, *dyn), f32), V((3, *dyn), f32),
            V((3, *heads), f32), V((3, *heads), f32),
            V(qf.shape, i16), V(qy.shape, i16), V(qh.shape, i16), V(lg.shape, f32), V((128, BLK), f32), V((3, 24, 128), f32),
            pltpu.SemaphoreType.DMA((9, 6)),
        ],
        compiler_params=pltpu.CompilerParams(vmem_limit_bytes=64 * 2**20),
    )(lg, qf, qy, qh, misc, *arrays)


def per_device(
    latents, actions, task_ids, steps_left, target_latents, reward_bins, reward_frac, value_bins, value_frac,
    first_weight, first_moment, first_second, dynamics_weight, dynamics_moment, dynamics_second,
    heads_weight, heads_moment, heads_second, task_table, table_moment, table_second,
    vector_params, vector_moment, vector_second,
):
    n_tok = latents.shape[0]
    wide = lax.axis_size("wide")
    token_count = float(HORIZON * n_tok * wide * lax.axis_size("narrow"))
    n_task = task_table.shape[0]
    to_class = lambda a: a.transpose(2, 0, 1)
    lg, qf, qy, qh, misc = step_call(
        wide, token_count, n_task, latents, actions.transpose(1, 2, 0), task_ids,
        steps_left, target_latents.transpose(1, 0, 2),
        reward_bins.T, reward_frac.T, value_bins.T, value_frac.T,
        first_weight, dynamics_weight, to_class(heads_weight), task_table, vector_params)
    heads = [to_class(a) for a in (heads_weight, heads_moment, heads_second)]
    new = adam_call(lg, qf, qy, qh, misc, [
        first_weight, first_moment, first_second, dynamics_weight, dynamics_moment, dynamics_second, *heads,
        task_table, table_moment, table_second, vector_params, vector_moment, vector_second])
    return (new[15], *new[0:6], *(a.transpose(1, 2, 0) for a in new[6:9]), *new[9:15])


def solution(mesh):
    tokens = ("wide", "narrow")
    in_specs = (
        P(tokens, None), P(tokens, None, None), P(tokens), P(tokens), P(tokens, None, None),
        P(tokens, None), P(tokens, None), P(tokens, None), P(tokens, None),
        *(P("narrow", None),) * 6, *(P(None, "narrow", None),) * 3, *(P("narrow", None),) * 3, *(P("narrow"),) * 3,
    )
    out_specs = (
        P(tokens, None), *(P("narrow", None),) * 6, *(P(None, "narrow", None),) * 3,
        *(P("narrow", None),) * 3, *(P("narrow"),) * 3,
    )
    return jax.shard_map(per_device, mesh=mesh, in_specs=in_specs, out_specs=out_specs, check_vma=False)
```

```python
import functools

import jax
import jax.numpy as jnp
from jax import lax
from jax.experimental import pallas as pl
from jax.experimental.pallas import tpu as pltpu
from jax.sharding import PartitionSpec as P

f32, bf16, i16, i32 = jnp.float32, jnp.bfloat16, jnp.int16, jnp.int32
MESH = pl.DeviceIdType.MESH

LAT = 768
HID = 1024
BINS = 101
TEMB = 96
ACTN = 8
HORIZON = 3
STEP = 5
NZ = 4
SHARD = 218
SENT = 224
BLK = 256
ROWS = 320
RB = 320
NB = ROWS // RB
ALL = HORIZON * ROWS
HALF = HID // 2
YHALF = LAT // 2
TASK_LANE = LAT + ACTN - 3 * SHARD
ACT_LANE = LAT - 3 * SHARD

norm_eps = 1e-05
adam_eps = 1e-08
moment_decay = 0.5
horizon_decay = 0.5
weight_decay = 0.01
matrix_rate = 0.03
vector_rate = 0.3
consistency_coef = 20.0
head_coef = 0.1

NN = (((1,), (0,)), ((), ()))
NT = (((1,), (1,)), ((), ()))
TN = (((0,), (0,)), ((), ()))


def dot(a, b, dims=NN):
    return lax.dot_general(a, b, dims, preferred_element_type=f32)


def loop(start, end, body, carry):
    for i in range(start, end):
        carry = body(i, carry)
    return carry


def whole_of(start, unit):
    return start if isinstance(start, int) else pl.multiple_of(start, unit)


def lanes(n):
    return lax.broadcasted_iota(i32, (1, n), 1)


def block_rows(i, base=0):
    return pl.ds(whole_of(base + i * RB, RB), RB)


def encode(v, ref):
    rows = v.shape[0]
    top = jnp.max(jnp.abs(v), 0, keepdims=True)
    e = jnp.clip(jnp.ceil(jnp.log2(jnp.maximum(top, 1e-37))), -100.0, 120.0)
    ref[0:rows, :] = jnp.round(v * jnp.exp2(14.9 - e)).astype(i32).astype(i16)
    ref[rows : rows + 16, :] = jnp.broadcast_to(e, (16, v.shape[1])).astype(i32).astype(i16)


def decode(ref):
    rows = ref.shape[0] - 16
    e = ref[rows : rows + 16, :].astype(i32).astype(f32)[0:1, :]
    return ref[0:rows, :].astype(i32).astype(f32) * jnp.exp2(e - 14.9)


def pack_tiles(x):
    inside = lanes(BLK) < SHARD
    b0 = jnp.where(inside, x[:, 0:256], 0.0)
    b1 = jnp.where(inside, pltpu.roll(x[:, 128:512], 384 - 90, 1)[:, 0:256], 0.0)
    b2 = jnp.where(inside, pltpu.roll(x[:, 384:768], 384 - 52, 1)[:, 0:256], 0.0)
    b3 = jnp.where(lanes(128) < ACT_LANE, pltpu.roll(x[:, 640:768], 128 - 14, 1), 0.0)
    return b0, b1, b2, b3


def unpack_tiles(g):
    inside = lanes(BLK) < SHARD
    empty = jnp.zeros((g.shape[0], 128), f32)
    b0 = jnp.where(inside, g[:, 0:256], 0.0)
    b1 = pltpu.roll(jnp.concatenate([jnp.where(inside, g[:, 256:512], 0.0), empty], 1), 90, 1)
    b2 = pltpu.roll(jnp.concatenate([jnp.where(inside, g[:, 512:768], 0.0), empty], 1), 52, 1)
    b3 = pltpu.roll(jnp.where(lanes(128) < ACT_LANE, g[:, 768:896], 0.0), 14, 1)
    return jnp.concatenate(
        [
            b0[:, 0:128],
            b0[:, 128:256] + b1[:, 0:128],
            b1[:, 128:256],
            b1[:, 256:384] + b2[:, 0:128],
            b2[:, 128:256],
            b2[:, 256:384] + b3,
        ],
        1,
    )


def group_sums(x, ones):
    parts = []
    for j in range(0, x.shape[1], 256):
        v = x[:, j : j + 256]
        high = v.astype(bf16)
        low = (v - high.astype(f32)).astype(bf16)
        parts.append(dot(high, ones) + dot(low, ones))
    return jnp.concatenate(parts, 1)


def mish_parts(n):
    u = jnp.exp(jnp.minimum(n, 40.0))
    q = u * (u + 2.0)
    r = 1.0 / (q + 2.0)
    bent = q * r
    return bent, bent + (4.0 * n) * (u * (u + 1.0)) * (r * r)


def add_columns(acc, values):
    for k, v in enumerate(values):
        total = acc[8 * k : 8 * k + 8, :]
        for j in range(v.shape[0] // 8):
            total = total + v[8 * j : 8 * j + 8, :]
        acc[8 * k : 8 * k + 8, :] = total


def rcopy(src, dst, send_sem, recv_sem, device):
    return pltpu.make_async_remote_copy(
        src_ref=src, dst_ref=dst, send_sem=send_sem, recv_sem=recv_sem, device_id=device, device_id_type=MESH
    )


def step_kernel(wide, token_count, n_tok, n_task, lat, actT, ids, steps, tgt, rb, rf, vb, vf, fw, dw, hw, tab, vec,
                lg, qf, qy, qh, misc, **s):
    ups_n = wide.bit_length() - 4
    w, z = lax.axis_index("wide"), lax.axis_index("narrow")
    b0, b1, b2 = lax.rem(w, 2), lax.rem(lax.div(w, 2), 2), lax.rem(lax.div(w, 4), 2)
    pc, p1, p2 = (w + 1 - 2 * b0, z), (w + 2 - 4 * b1, z), (w + 4 - 8 * b2, z)
    p12 = (w + 6 - 4 * b1 - 8 * b2, z)
    zs = [(w, lax.rem(z + d, NZ)) for d in range(NZ)]
    from_z = [lax.rem(z + NZ - d, NZ) for d in range(NZ)]
    ups = []
    for u in range(ups_n):
        bit = 8 << u
        ups.append((w + bit - 2 * bit * lax.rem(lax.div(w, bit), 2), z))
    me = b0 * 4 + b1 * 2 + b2
    own = b1 * 2 + b2
    me_1, me_2, me_12 = me + 2 - 4 * b1, me + 1 - 2 * b2, 4 * b0 + 3 - own
    mine_of_8 = 4 * b0
    sends = []

    def pick(odd, even_value, odd_value):
        return even_value + odd * (odd_value - even_value)

    def launch(make):
        make().start()
        sends.append(make)

    X, XT, XTp, U, AT, ATp, DU = s["X"], s["XT"], s["XTp"], s["U"], s["AT"], s["ATp"], s["DU"]
    WF, WD, HT, SM, VEC = s["WF"], s["WD"], s["HT"], s["SM"], s["VEC"]
    PRE, PRE2, ACT, TT = s["PRE"], s["PRE2"], s["ACT"], s["TT"]
    TU, TS = TT.at[pl.ds(0, ROWS)], TT.at[pl.ds(ROWS, ROWS)]
    GP, GPp, GDL, GDLp = s["GP"], s["GPp"], s["GDL"], s["GDLp"]
    INV, SIDE, ONES, VA, VT, GEMB = (
        s["INV"], s["SIDE"], s["ONES"], s["VA"], s["VT"], s["GEMB"])

    barrier = pltpu.get_barrier_semaphore()
    peers = [pc, p1, p2, p12] + zs[1:] + ups
    for p in peers:
        pl.semaphore_signal(barrier, inc=1, device_id=p, device_id_type=MESH)

    STG = s["STG"]
    loads = []

    def load_first(part):
        return pltpu.make_async_copy(
            fw.at[:, pl.ds(HALF * part, HALF)], STG.at[part % 2], s["ls"].at[part % 2])

    loads.append(pltpu.make_async_copy(dw, DU.at[pl.ds(0, BLK)], s["ls"].at[3]))
    loads.append(pltpu.make_async_copy(lat, GDL.at[pl.ds(0, n_tok)], s["ls"].at[4]))
    load_first(0).start()
    load_first(1).start()
    for c in loads:
        c.start()

    def cast_first(br):
        for part in (2 * br, 2 * br + 1):
            load_first(part).wait()
            rows = jnp.concatenate([STG[part % 2].astype(bf16), jnp.zeros((SENT - SHARD, HALF), bf16)], 0)
            WF[pl.ds(whole_of(BLK * z, BLK), SENT), HALF * part : HALF * part + HALF] = rows
            if part < 4:
                load_first(part + 2).start()

    cast_first(0)
    pl.semaphore_wait(barrier, len(peers))

    gs, gr = s["gs"], s["gr"]

    class Item:
        def __init__(self, index, view):
            self.i, self.view = index, view

        def _copy(self, d, kind, piece, device):
            view = self.view(*piece)
            return rcopy(view, view, gs.at[self.i, d - 1, kind], gr.at[self.i, d - 1, kind], device)

        def _recv(self, d, kind, *piece):
            self._copy(d, kind, piece, pc).wait_recv()

        def _send(self, d, kind, device, *piece):
            launch(lambda: self._copy(d, kind, piece, device))

        def start(self):
            for d in (1, 3, 2):
                self._send(d, 0, zs[d], z, me, 1)

        def spread(self, *ds):
            for d in ds or (1, 3, 2):
                self._recv(d, 0, from_z[d], me, 1)
                self._send(d, 1, p1, from_z[d], me, 1)
                self._send(d, 2, p2, from_z[d], me, 1)
                self._send(d, 3, p12, from_z[d], me, 1)

        def cross(self, *ds):
            for d in ds or (1, 3, 2):
                q = from_z[d]
                self._recv(d, 1, q, me_1, 1)
                self._recv(d, 2, q, me_2, 1)
                self._recv(d, 3, q, me_12, 1)
                self._send(d, 5, pc, q, mine_of_8, 4)

        def finish(self):
            for d in (1, 3, 2):
                self._recv(d, 5, from_z[d], 4 - 4 * b0, 4)

    def first_view(br):
        def view(q, at, n):
            return WF.at[pl.ds(whole_of(BLK * q, BLK), SENT), pl.ds(whole_of(HID * br + 128 * at, 128), 128 * n)]
        return view

    def dyn_view(q, at, n):
        return WD.at[pl.ds(whole_of(BLK * q + 32 * at, 32), 32 * n)]

    def heads_view(q, at, n):
        cols = pl.ds(whole_of(BLK * q, BLK), BLK)
        rows = pl.ds(whole_of(16 * at, 16), 16 * n)
        return HT.at[:, rows, cols]

    gD, gY, gR, gV, gH = (
        Item(0, first_view(0)), Item(1, dyn_view), Item(2, first_view(1)), Item(3, first_view(2)), Item(4, heads_view))

    def vec_rows():
        n_vec = vec.shape[0]
        whole = n_vec // 128
        VR = s["VR"]
        VR[...] = jnp.zeros_like(VR)
        for r in range(whole):
            VR[r + 1 : r + 2, :] = vec[pl.ds(128 * r, 128)].reshape(1, 128)
        left = n_vec - 128 * whole
        VR[whole + 1 : whole + 2, 0:left] = vec[pl.ds(128 * whole, left)].reshape(1, left)
        plain = VR[1:33, :]
        moved = jnp.where(lanes(128) < 64, pltpu.roll(VR[0:32, :], 64, 1), pltpu.roll(plain, 64, 1))
        return jnp.where(lax.rem(z, 2) == 1, moved, plain).astype(bf16)

    gD.start()
    frame = vec_rows()
    SM[z, 0:32, :] = frame
    SM[z, 32:64, :] = jnp.zeros((32, 128), bf16)
    SM[z, 32 : 32 + n_task, 0:TEMB] = tab[...].astype(bf16)
    for d in (1, 3, 2):
        launch(lambda d=d: rcopy(SM.at[z], SM.at[z], s["ms"].at[d], s["mr"].at[d], zs[d]))
    loads[0].wait()
    WD[pl.ds(whole_of(BLK * z, BLK), BLK), :] = DU[0:BLK, :].astype(bf16)
    gY.start()
    cast_first(1)
    gD.spread(1, 3)
    own_cols = pl.ds(whole_of(BLK * z, BLK), BLK)
    for k in range(2):
        PRE[0:128, 0:BLK] = jnp.zeros((128, BLK), f32)
        PRE[0:BINS, 0:BLK] = hw[:, k, :]
        HT[k, :, own_cols] = PRE[0:128, 0:BLK].astype(bf16)
    gD.spread(2)
    gR.start()
    gH.start()
    cast_first(2)

    GDL[n_tok:ROWS, :] = jnp.zeros((ROWS - n_tok, LAT), bf16)
    for q in range(NZ):
        WF[BLK * q + SENT : BLK * q + BLK, :] = jnp.zeros((BLK - SENT, 3 * HID), bf16)
    loads[1].wait()

    idr = s["IDR"]
    idr[...] = jnp.full_like(idr, -1)
    idr[0:1, 0:n_tok] = ids[...].reshape(1, n_tok)
    slot = lax.broadcasted_iota(i32, (128, 1), 0)
    task = jnp.where(slot % 32 < n_task, n_task * (slot // 32) + slot % 32, -2)
    PKT = s["PKT"]
    PKT[...] = jnp.where(idr[0:1, 0:ROWS] == task, 1.0, 0.0).astype(bf16)
    gD.cross()
    gV.start()

    for d in (1, 3, 2):
        q = from_z[d]
        rcopy(SM.at[q], SM.at[q], s["ms"].at[d], s["mr"].at[d], pc).wait_recv()
    full = s["VFULL"]
    full[...] = jnp.zeros_like(full)
    for q, at in enumerate((0, 22, 45, 67)):
        full[at : at + 24, :] = full[at : at + 24, :] + SM[q, 0:32, :].astype(f32)[0:24, :]
    for r in range(12):
        n, first = (8, 8 * r) if r < 9 else (6, 72 + 6 * (r - 9))
        for j in range(n):
            VEC[r : r + 1, 128 * j : 128 * j + 128] = full[first + j : first + j + 1, :]
    place = jnp.concatenate([SM[q, 32:64, :] for q in range(NZ)], 0).astype(f32)
    table = pltpu.roll(jnp.concatenate([place, jnp.zeros_like(place)], 1), TASK_LANE, 1).astype(bf16)
    AC = s["AC"]
    AC[...] = jnp.zeros_like(AC)
    act_to = jnp.where(
        lax.broadcasted_iota(i32, (16, BLK), 0) + ACT_LANE == lax.broadcasted_iota(i32, (16, BLK), 1), 1.0, 0.0
    ).astype(bf16)
    rows_of_task = dot(PKT[...], table, TN)
    gY.spread()
    for t in range(3):
        AC[0:ACTN, 0:n_tok] = actT[t].astype(f32)
        X[ROWS * t : ROWS * t + ROWS, 768:1024] = (rows_of_task + dot(AC[:, 0:ROWS].astype(bf16), act_to, TN)).astype(bf16)

    def later_setup():
        tile = lax.broadcasted_iota(i32, (256, 256), 0) // 8 == lax.broadcasted_iota(i32, (256, 256), 1) // 8
        ONES[...] = jnp.where(tile, 1.0, 0.0).astype(bf16)
        st = s["ST"]
        st[...] = jnp.zeros_like(st)
        st[0:1, 0:n_tok] = steps[...].reshape(1, n_tok).astype(f32)
        for t in range(3):
            for k, ref in enumerate((rb, rf, vb, vf)):
                st[k + 1 : k + 2, 0:n_tok] = ref[t : t + 1, :].astype(f32)
            SIDE[t] = st[...].T[0:ROWS, :]
        for ref in (VA, VT, GEMB, s["DWH"], s["MS"]):
            ref[...] = jnp.zeros_like(ref)

    def put_latents(rows, values):
        b0, b1, b2, b3 = pack_tiles(values)
        X[rows, 0:768] = jnp.concatenate((b0, b1, b2), 1).astype(bf16)
        X[rows, 768:896] = (X[rows, 768:896].astype(f32) + b3).astype(bf16)

    put_latents(block_rows(0), GDL[0:ROWS, :].astype(f32))
    gD.finish()

    def matmul(out, orows, n, width, left, right, dims=NN):
        def tile_step(j, c):
            cols = pl.ds(j * width, width)
            out[orows, cols] = dot(left, right(cols), dims)
            return c
        loop(0, n // width, tile_step, 0)

    def first_forward(br, base, pre):
        def tile_step(j, c):
            cols = pl.ds(j * 512, 512)
            from_cols = pl.ds(whole_of(HID * br + j * 512, 512), 512)
            pre[:, cols] = dot(X[pl.ds(base, ROWS), :], WF[:, from_cols])
            return c
        loop(0, 2, tile_step, 0)

    def norm_mish(br, pre, unit, inv, unit_base, slope):
        bias, gain, shift = (VEC[pl.ds(3 * br + k, 1), :] for k in range(3))

        def step(i, c):
            rows = block_rows(i)
            p = pre[rows, :] + bias
            ce = p - jnp.mean(p, -1, keepdims=True)
            iv = lax.rsqrt(jnp.mean(ce * ce, -1, keepdims=True) + norm_eps)
            un = ce * iv
            n = un * gain + shift
            bent, sl = mish_parts(n)
            ACT[rows, :] = (n * bent).astype(bf16)
            if slope is not None:
                slope[rows, :] = sl
            unit[block_rows(i, unit_base), :] = un
            inv[block_rows(i, unit_base), :] = jnp.broadcast_to(iv, (RB, 128))
            return c
        loop(0, NB, step, 0)

    def dyn_forward(t, c):
        base = whole_of(ROWS * t, RB)
        first_forward(0, base, PRE)

        norm_mish(0, PRE, U, INV, base, None)

        @pl.when(t == 0)
        def _():
            gY.cross()
            gR.spread()
            later_setup()
            gY.finish()

        @pl.when(t == 2)
        def _():
            gH.cross()
        matmul(TU, pl.ds(0, ROWS), LAT, 384, ACT[...], lambda cols: WD[:, cols])
        for k in range(3):
            @pl.when(t == k)
            def _():
                AT[:, ROWS * k : ROWS * k + ROWS] = ACT[...].T
        bias, gain, shift = (VEC[9 + k : 10 + k, 0:LAT] for k in range(3))

        def step(i, c):
            rows, at = block_rows(i), block_rows(i, base)
            p = TU[rows, 0:LAT] + bias
            ce = p - jnp.mean(p, -1, keepdims=True)
            iv = lax.rsqrt(jnp.mean(ce * ce, -1, keepdims=True) + norm_eps)
            un = ce * iv
            DU[at, :] = un
            INV[at, 64:128] = jnp.broadcast_to(iv, (RB, 64))

            @pl.when(t < 2)
            def _():
                e = jnp.exp(un * gain + shift)
                put_latents(block_rows(i, base + ROWS), e / group_sums(e, ONES[...]))
            return c
        loop(0, NB, step, 0)

        @pl.when(t == 0)
        def _():
            gH.spread()

        @pl.when(t == 1)
        def _():
            gR.cross()
            gV.spread()
        return c

    lax.fori_loop(0, 3, dyn_forward, 0)
    XT[...] = X[...].T
    xs, xr = s["xs"], s["xr"]
    launch(lambda: rcopy(XT, XTp, xs.at[0], xr.at[0], pc))
    launch(lambda: rcopy(AT, ATp, xs.at[1], xr.at[1], pc))
    gR.finish()
    gH.finish()

    def norm_backward(br, pre, unit, inv, unit_base, slope, out_base):
        gain, shift = VEC[pl.ds(3 * br + 1, 1), :], VEC[pl.ds(3 * br + 2, 1), :]
        acc = VA.at[br]

        def step(i, c):
            rows, at = block_rows(i), block_rows(i, unit_base)
            un = unit[at, :]
            sl = mish_parts(un * gain + shift)[1] if slope is None else slope[rows, :]
            gn = pre[rows, :] * sl
            h = gn * gain
            gp = (h - jnp.mean(h, -1, keepdims=True) - un * jnp.mean(h * un, -1, keepdims=True)) * inv[at, 0:1]
            GP[block_rows(i, out_base), pl.ds(whole_of(HID * br, HID), HID)] = gp.astype(bf16)
            add_columns(acc, (gp, gn * un, gn))
            return c
        loop(0, NB, step, 0)

    def head_step(k, t, pre, following):
        base = whole_of(ROWS * t, RB)
        norm_mish(1 + k, pre, TU, s["HINV"], 0, TS)
        following()
        logits = dot(ACT[...], HT[k], NT)
        real = lanes(128) < BINS
        logits = jnp.where(real, logits, -1e30)
        e = jnp.exp(logits - jnp.max(logits, -1, keepdims=True))
        soft = e / jnp.sum(e, -1, keepdims=True)
        side = SIDE[t]
        at, frac = (jnp.where(k == 0, side[:, c : c + 1], side[:, c + 2 : c + 3]) for c in (1, 2))
        level = lanes(128).astype(f32)
        hot = jnp.where(level == at, 1.0 - frac, 0.0) + jnp.where(level == at + 1.0, frac, 0.0)
        decay = jnp.where(t == 0, 1.0, jnp.where(t == 1, horizon_decay, horizon_decay**2))
        weight = jnp.where(side[:, 0:1] > t.astype(f32), decay, 0.0) / token_count
        gl = jnp.where(real, weight * head_coef * (soft - hot), 0.0).astype(bf16)
        s["DWH"][k] = s["DWH"][k] + dot(gl.astype(f32).T.astype(bf16), ACT[...])
        pre[...] = dot(gl, HT[k])
        norm_backward(1 + k, pre, TU, s["HINV"], 0, TS, base)

    def heads_inputs(t):
        rows = pl.ds(whole_of(ROWS * t, RB), ROWS)
        for j in range(2):
            cols = pl.ds(512 * j, 512)
            PRE2[:, cols] = dot(GP[rows, HID : 3 * HID], WF[cols, HID : 3 * HID], NT)

    def y_rows(t):
        rows, cols = pl.ds(whole_of(ROWS * t, RB), ROWS), pl.ds(pl.multiple_of(YHALF * (1 - b0), 128), YHALF)
        return rcopy(GDL.at[rows, cols], GDLp.at[rows], xs.at[4 + t], xr.at[4 + t], pc)

    def d_rows(t):
        rows, cols = pl.ds(whole_of(ROWS * t, RB), ROWS), pl.ds(pl.multiple_of(HALF * (1 - b0), HALF), HALF)
        return rcopy(GP.at[rows, cols], GPp.at[0, rows], xs.at[7 + t], xr.at[7 + t], pc)

    def dyn_backward(t, between):
        base = whole_of(ROWS * t, RB)
        gain, shift = VEC[10:11, 0:LAT], VEC[11:12, 0:LAT]
        scale = 2.0 * consistency_coef / LAT

        def step(i, c):
            rows, at = block_rows(i), block_rows(i, base)
            un = DU[at, :]
            e = jnp.exp(un * gain + shift)
            sx = e / group_sums(e, ONES[...])
            decay = jnp.where(t == 0, 1.0, jnp.where(t == 1, horizon_decay, horizon_decay**2))
            weight = jnp.where(SIDE[0, rows, 0:1] > t.astype(f32), decay, 0.0) / token_count
            g = weight * scale * (sx - X[at, 0:LAT].astype(f32))
            g = g + jnp.where(t < 2, unpack_tiles(PRE[rows, 0:896]), 0.0)
            gn = sx * (g - group_sums(g * sx, ONES[...]))
            h = gn * gain
            gp = (h - jnp.mean(h, -1, keepdims=True) - un * jnp.mean(h * un, -1, keepdims=True)) * INV[at, 64:65]
            GDL[at, :] = gp.astype(bf16)
            add_columns(VT, (gp, gn * un, gn))
            return c
        loop(0, NB, step, 0)
        y_rows(t).start()
        between()

        def tile_step(j, c):
            cols = pl.ds(j * 512, 512)
            PRE[:, cols] = dot(GDL[pl.ds(base, ROWS), :], WD[cols, :], NT)
            return c
        loop(0, 2, tile_step, 0)
        norm_backward(0, PRE, U, INV, base, None, base)
        d_rows(t).start()

    def inputs_backward(t):
        base = whole_of(ROWS * t, RB)

        def tile_step(j, c):
            cols = pl.ds(j * 512, 512)
            PRE[:, cols] = dot(GP[pl.ds(base, ROWS), :], WF[cols, :], NT)
            return c
        loop(0, 2, tile_step, 0)
        GEMB[...] = GEMB[...] + PRE[:, 768:1024]

    rs_s, rs_r = s["ss"], s["sr"]

    class Stream:
        def __init__(self, index, grad, view, E, R, Q):
            self.i, self.grad, self.view, self.Q = index, grad, view, Q
            (self.E1, self.E2, self.E3), (self.R1, self.R2, self.R3) = E, R
            self.spent = []

        def _copy(self, at, src, dst, device):
            return rcopy(src, dst, rs_s.at[self.i, at], rs_r.at[self.i, at], device)

        def _recv(self, at, dst):
            self._copy(at, dst, dst, pc).wait_recv()

        def release(self):
            for first, span, ref in self.spent:
                if span is None:
                    self._copy(first, ref, ref, pc).wait_send()
                else:
                    def one(i, c):
                        self._copy(first + i, ref.at[i], ref.at[i], pc).wait_send()
                        return c
                    lax.fori_loop(*span, one, 0)
            self.spent = []

        def _send(self, at, src, dst, device):
            self._copy(at, src, dst, device).start()
            self.spent.append((at, None, src))

        def stage1(self, *span):
            span = span or (0, NZ)

            def one(i, c):
                q = lax.rem(z + 1 + i, NZ)
                odd = lax.rem(q, 2)
                base = pick(odd, 2 - 2 * b1, 1 - b2)
                for j in range(2):
                    encode(self.grad[self.view(q, base + j * (1 + odd))], self.E1.at[i, j])
                self._copy(i, self.E1.at[i], self.R1.at[i], (pick(odd, p1[0], p2[0]), z)).start()
                return c
            lax.fori_loop(*span, one, 0)
            self.spent.append((0, span, self.E1))

        def stage2(self, *span):
            span = span or (0, NZ)

            def one(i, c):
                q = lax.rem(z + 1 + i, NZ)
                odd = lax.rem(q, 2)
                self._recv(i, self.R1.at[i])
                keep = pick(odd, b2, b1)
                other = pick(odd, own + 1 - 2 * b2, own + 2 - 4 * b1)
                encode(self.grad[self.view(q, other)] + decode(self.R1.at[i, 1 - keep]), self.E2.at[i])
                self._copy(4 + i, self.E2.at[i], self.R2.at[i], (pick(odd, p2[0], p1[0]), z)).start()
                mine = self.view(q, own)
                self.grad[mine] = self.grad[mine] + decode(self.R1.at[i, keep])
                return c
            lax.fori_loop(*span, one, 0)
            self.spent.append((4, span, self.E2))

        def stage3(self):
            def one(i, c):
                q = lax.rem(z + 1 + i, NZ)
                self._recv(4 + i, self.R2.at[i])
                encode(self.grad[self.view(q, own)] + decode(self.R2.at[i]), self.E3.at[i])
                self._copy(8 + i, self.E3.at[i], self.R3.at[i], (w, q)).start()
                return c
            lax.fori_loop(0, 3, one, 0)
            self.spent.append((8, (0, 3), self.E3))

        def stage4(self):
            self._recv(7, self.R2.at[3])
            total = self.grad[self.view(z, own)] + decode(self.R2.at[3])
            for i in (0, 2, 1):
                self._recv(8 + i, self.R3.at[i])
                total = total + decode(self.R3.at[i])
            for u in range(ups_n):
                F, FR = self.Q.at[me], s["FR%d" % self.i]
                encode(total, F)
                c = self._copy(16 + u, F, FR.at[u], ups[u])
                c.start()
                self._recv(16 + u, FR.at[u])
                c.wait_send()
                total = decode(F) + decode(FR.at[u])
            encode(total, self.Q.at[me])
            self._send(11, self.Q.at[me], self.Q.at[me], p1)
            self._send(12, self.Q.at[me], self.Q.at[me], p2)
            self._send(13, self.Q.at[me], self.Q.at[me], p12)

        def stage6(self):
            self._recv(11, self.Q.at[me_1])
            self._recv(12, self.Q.at[me_2])
            self._recv(13, self.Q.at[me_12])
            mine = self.Q.at[pl.ds(mine_of_8, 4)]
            self._send(15, mine, mine, pc)

        def stage7(self, out, sem):
            self._recv(15, self.Q.at[pl.ds(4 - 4 * b0, 4)])
            c = pltpu.make_async_copy(self.Q, out, sem)
            c.start()
            return c

    def first_slice(q, at):
        return (pl.ds(whole_of(BLK * q, BLK), SENT), pl.ds(whole_of(128 * at, 128), 128))

    def value_slice(q, at):
        cols = HALF * lax.div(q, 2) + 128 * at
        return (pl.ds(whole_of(BLK * lax.rem(q, 2), BLK), SENT), pl.ds(whole_of(cols, 128), 128))

    def y_slice(q, at):
        return (pl.ds(whole_of(BLK * q + 64 * at, 64), 64), slice(None))

    def h_slice(q, at):
        return (b0, pl.ds(whole_of(32 * at, 32), 32), pl.ds(whole_of(BLK * q, BLK), BLK))

    EF = (s["E1"], s["E2"], s["E3"])
    streams = []
    for i, name in enumerate("DRV"):
        streams.append(Stream(
            i, *((TT, value_slice) if name == "V" else (s["DWA"], first_slice)), EF,
            tuple(s["R%d%s" % (k, name)] for k in (1, 2, 3)), s["QF"].at[i]))
    sD, sR, sV = streams
    sY = Stream(3, s["DWY"], y_slice, tuple(s["E%dY" % k] for k in (1, 2, 3)),
                tuple(s["R%dY" % k] for k in (1, 2, 3)), s["QY"])
    sH = Stream(4, s["DWH"], h_slice, tuple(s["E%dH" % k] for k in (1, 2, 3)),
                tuple(s["R%dH" % k] for k in (1, 2, 3)), s["QH"])

    def send_half(br):
        def make():
            cols = pl.ds(whole_of(HID * br + HALF * (1 - b0), HALF), HALF)
            return rcopy(GP.at[:, cols], GPp.at[br], xs.at[1 + br], xr.at[1 + br], pc)
        launch(make)

    def wait_x(at, dst):
        rcopy(dst, dst, xs.at[at], xr.at[at], pc).wait_recv()

    def weight_grad(out, n, left, right, arrived, left2, right2):
        def own_tile(j, c):
            cols = pl.ds(pl.multiple_of(j * n, n), n)
            out[:, cols] = dot(left[...], right(j))
            return c
        lax.fori_loop(0, out.shape[1] // n, own_tile, 0)
        arrived()

        def other_tile(j, c):
            cols = pl.ds(pl.multiple_of(j * n, n), n)
            out[:, cols] = out[:, cols] + dot(left2[...], right2(cols))
            return c
        lax.fori_loop(0, out.shape[1] // n, other_tile, 0)

    def first_grad(br, out, arrived):
        weight_grad(
            out, 256, XT,
            lambda j: GP[:, pl.ds(pl.multiple_of(HID * br + HALF * b0 + 256 * j, 256), 256)], arrived,
            XTp, lambda cols: GPp[br, :, cols])

    def value_grad():
        def tile_step(j, c):
            cols = pl.ds(whole_of(j * 256, 256), 256)
            low_cols = pl.ds(whole_of(HALF + j * 256, 256), 256)
            right = GP[:, pl.ds(whole_of(2 * HID + HALF * b0 + 256 * j, 256), 256)]
            total = dot(XT[...], right) + dot(XTp[...], GPp[2, :, cols])
            TT[0:512, cols] = total[0:512, :]
            TT[0:512, low_cols] = total[512:1024, :]
            return c
        lax.fori_loop(0, 2, tile_step, 0)

    def y_grad():
        def arrived():
            wait_x(1, ATp)
            for t in range(3):
                wait_x(4 + t, GDLp.at[pl.ds(ROWS * t, ROWS)])
        weight_grad(
            s["DWY"], 128, AT,
            lambda j: GDL[:, pl.ds(whole_of(YHALF * b0 + 128 * j, 128), 128)], arrived,
            ATp, lambda cols: GDLp[:, cols])
        sY.stage1()

    def head_forward(j, pre):
        first_forward(1 + lax.div(j, 3), whole_of(ROWS * lax.rem(j, 3), RB), pre)

    def head_steps(i, c):
        @pl.when(i == 1)
        def _():
            gV.finish()

        @pl.when(i == 2)
        def _():
            def arrived():
                wait_x(0, XTp)
                wait_x(2, GPp.at[1])
            first_grad(1, s["DWA"], arrived)
            sR.stage1()
        j = 2 * i
        head_step(lax.div(j, 3), lax.rem(j, 3), PRE, lambda: head_forward(j + 1, PRE2))

        @pl.when(i == 0)
        def _():
            gV.cross()

        @pl.when(i == 1)
        def _():
            send_half(1)
        head_step(lax.div(j + 1, 3), lax.rem(j + 1, 3), PRE2, lambda: head_forward(lax.min(j + 2, 5), PRE))
        return c
    first_forward(1, 0, PRE)
    lax.fori_loop(0, 3, head_steps, 0)
    send_half(2)
    launch(lambda: rcopy(s["DWH"].at[1 - b0], s["DWHp"], xs.at[10], xr.at[10], pc))
    for t in range(3):
        loads.append(pltpu.make_async_copy(
            tgt.at[t], X.at[pl.ds(ROWS * t, n_tok), pl.ds(0, LAT)], s["ls"].at[5 + t]))
        loads[-1].start()
    sR.stage2()
    for c in loads[2:]:
        c.wait()
    def backward(i, c):
        t = 2 - i

        def last_y():
            @pl.when(i == 2)
            def _():
                y_grad()
        dyn_backward(t, last_y)

        @pl.when(i == 0)
        def _():
            sR.stage3()
            wait_x(3, GPp.at[2])
            value_grad()
            sR.release()
            sV.stage1()
            wait_x(10, s["DWHp"])
            s["DWH"][b0] = s["DWH"][b0] + s["DWHp"][...]
            sH.stage1()

        @pl.when(i == 1)
        def _():
            sR.stage4()
            sV.stage2()
            sH.stage2()

        @pl.when(i == 2)
        def _():
            sV.stage3()
            sH.stage3()
            def arrived():
                for k in range(3):
                    wait_x(7 + k, GPp.at[0, pl.ds(ROWS * k, ROWS)])
            first_grad(0, s["DWA"], arrived)
            sV.release()
            sD.stage1()
            sR.stage6()
        inputs_backward(t)
        return c
    lax.fori_loop(0, 3, backward, 0)
    for k in range(3):
        sends.extend((lambda k=k: y_rows(k), lambda k=k: d_rows(k)))

    def write_latent(i, c):
        rows = block_rows(i)
        DU[rows, :] = unpack_tiles(PRE[rows, 0:896])
        return c
    loop(0, NB, write_latent, 0)
    lg_copy = pltpu.make_async_copy(DU.at[pl.ds(0, n_tok)], lg, s["ls"].at[8])
    lg_copy.start()
    ge = GEMB[...]
    g1 = ge.astype(bf16)
    g2 = (ge - g1.astype(f32)).astype(bf16)
    g3 = (ge - g1.astype(f32) - g2.astype(f32)).astype(bf16)
    pk = PKT[...]
    by_task = dot(pk, g1) + dot(pk, g2) + dot(pk, g3)
    M = s["MS"]
    M[128:256, :] = pltpu.roll(by_task, BLK - TASK_LANE, 1)[:, 0:128]
    for r in range(12):
        acc, n, first = (VA.at[r // 3], 8, 8 * r) if r < 9 else (VT, 6, 72 + 6 * (r - 9))
        k = r % 3
        row = jnp.sum(acc[8 * k : 8 * k + 8, :], 0, keepdims=True)
        for j in range(n):
            M[first + j : first + j + 1, :] = row[:, 128 * j : 128 * j + 128]

    vs, vr = s["vs"], s["vr"]

    def small(at, src, dst, device):
        return rcopy(src, dst, vs.at[at], vr.at[at], device)

    def rows_of(start, n):
        return pl.ds(whole_of(start, 32), n)

    halves = ((0, pc, b0, 128), (1, p1, b1, 64), (2, p2, b2, 32))

    def halve(step, start):
        at, device, bit, n = halves[step]
        launch(lambda: small(at, M.at[rows_of(start + n * (1 - bit), n)], s["MR%d" % step], device))

    def halved(step, start):
        at, device, bit, n = halves[step]
        small(at, s["MR%d" % step], s["MR%d" % step], device).wait_recv()
        mine = rows_of(start + n * bit, n)
        M[mine, :] = M[mine, :] + s["MR%d" % step][...]
        return start + n * bit

    halve(0, 0)
    sY.stage2()
    at = halved(0, 0)
    halve(1, at)
    sD.stage2(0, 2)
    sY.stage3()
    sD.stage2(2, 4)
    at = halved(1, at)
    halve(2, at)
    sV.stage4()
    sH.stage4()
    at = halved(2, at)
    MZ = s["MZ"]
    MZ[z] = M[rows_of(at, 32), :]
    for d in (2, 1, 3):
        launch(lambda d=d: small(2 + d, MZ.at[z], MZ.at[z], zs[d]))
    sD.stage3()
    sY.stage4()
    for d in (1, 3, 2):
        small(2 + d, MZ.at[from_z[d]], MZ.at[from_z[d]], pc).wait_recv()
    total = (MZ[0] + MZ[1]) + (MZ[2] + MZ[3])
    for u in range(ups_n):
        s["MF"][u] = total
        launch(lambda u=u: small(9 + u, s["MF"].at[u], s["MFR"].at[u], ups[u]))
        small(9 + u, s["MFR"].at[u], s["MFR"].at[u], ups[u]).wait_recv()
        total = total + s["MFR"][u]
    MO = s["MO"]
    MO[rows_of(at, 32), :] = total
    for n, device in ((6, p1), (7, p2), (9 + ups_n, p12)):
        launch(lambda at=at, n=n, device=device: small(n, MO.at[rows_of(at, 32)], MO.at[rows_of(at, 32)], device))
    sV.stage6()
    sH.stage6()
    outs = [lg_copy]
    outs.append(sR.stage7(qf.at[1], s["ls"].at[9]))
    sD.stage4()
    sY.stage6()
    for n, slot in ((6, me_1), (7, me_2), (9 + ups_n, me_12)):
        o = 32 * slot
        small(n, MO.at[rows_of(o, 32)], MO.at[rows_of(o, 32)], pc).wait_recv()
    at = 128 * b0
    launch(lambda at=at: small(8, MO.at[rows_of(at, 128)], MO.at[rows_of(at, 128)], pc))
    outs.append(sV.stage7(qf.at[2], s["ls"].at[10]))
    outs.append(sH.stage7(qh, s["ls"].at[11]))
    outs.append(sY.stage7(qy, s["ls"].at[12]))
    o = at + 128 - 256 * b0
    small(8, MO.at[rows_of(o, 128)], MO.at[rows_of(o, 128)], pc).wait_recv()
    c = pltpu.make_async_copy(MO, misc, s["ls"].at[13])
    c.start()
    outs.append(c)
    sD.stage6()
    outs.append(sD.stage7(qf.at[0], s["ls"].at[14]))
    for c in outs:
        c.wait()
    for st in (sD, sR, sV, sY, sH):
        st.release()
    for make in sends:
        make().wait_send()


def step_call(wide, token_count, n_task, lat, actT, ids, steps, tgt, rb, rf, vb, vf, fw, dw, hw, tab, vec):
    n_tok = lat.shape[0]
    ups_n = wide.bit_length() - 4
    V = pltpu.VMEM
    D = pltpu.SemaphoreType.DMA
    scratch = dict(
        WF=V((HID, 3 * HID), bf16), WD=V((HID, LAT), bf16), HT=V((2, 128, HID), bf16),
        SM=V((NZ, 64, 128), bf16), VR=V((40, 128), f32), VEC=V((16, HID), f32), VFULL=V((96, 128), f32),
        X=V((ALL, HID), bf16), XT=V((HID, ALL), bf16), XTp=V((HID, ALL), bf16),
        U=V((ALL, HID), f32), AT=V((HID, ALL), bf16), ATp=V((HID, ALL), bf16),
        DU=V((ALL, LAT), f32),
        PRE=V((ROWS, HID), f32), PRE2=V((ROWS, HID), f32), TT=V((2 * ROWS, HID), f32), ACT=V((ROWS, HID), bf16),
        GP=V((ALL, 3 * HID), bf16), GPp=V((3, ALL, HALF), bf16), GDL=V((ALL, LAT), bf16), GDLp=V((ALL, YHALF), bf16),
        INV=V((ALL, 128), f32), HINV=V((ROWS, 128), f32),
        SIDE=V((3, ROWS, 16), f32), ONES=V((256, 256), bf16),
        VA=V((3, 24, HID), f32), VT=V((24, LAT), f32), GEMB=V((ROWS, BLK), f32),
        ST=V((16, 384), f32), IDR=V((8, 384), i32), PKT=V((128, ROWS), bf16), AC=V((16, 384), f32),
        DWA=V((HID, HALF), f32), DWY=V((HID, YHALF), f32), STG=V((2, SHARD, HALF), f32),
        DWH=V((2, 128, HID), f32), DWHp=V((128, HID), f32),
        MS=V((256, 128), f32), MO=V((256, 128), f32), MZ=V((NZ, 32, 128), f32),
        MR0=V((128, 128), f32), MR1=V((64, 128), f32), MR2=V((32, 128), f32),
        QF=V((3, 8, SENT + 16, 128), i16), QY=V((8, 80, YHALF), i16), QH=V((8, 48, BLK), i16),
    )
    for name, rows, cols in (("", SENT + 16, 128), ("Y", 80, YHALF), ("H", 48, BLK)):
        scratch["E1" + name] = V((4, 2, rows, cols), i16)
        scratch["E2" + name] = V((4, rows, cols), i16)
        scratch["E3" + name] = V((3, rows, cols), i16)
    for name, rows, cols in (("D", SENT + 16, 128), ("R", SENT + 16, 128), ("V", SENT + 16, 128), ("Y", 80, YHALF), ("H", 48, BLK)):
        scratch["R1" + name] = V((4, 2, rows, cols), i16)
        scratch["R2" + name] = V((4, rows, cols), i16)
        scratch["R3" + name] = V((3, rows, cols), i16)
    if ups_n:
        for i, (rows, cols) in enumerate(((SENT + 16, 128),) * 3 + ((80, YHALF), (48, BLK))):
            scratch["FR%d" % i] = V((ups_n, rows, cols), i16)
        scratch["MF"] = V((ups_n, 32, 128), f32)
        scratch["MFR"] = V((ups_n, 32, 128), f32)
    scratch.update(
        ls=D((16,)), gs=D((5, 3, 6)), gr=D((5, 3, 6)), ms=D((4,)), mr=D((4,)),
        xs=D((11,)), xr=D((11,)), ss=D((5, 16 + ups_n)), sr=D((5, 16 + ups_n)), vs=D((10 + ups_n,)), vr=D((10 + ups_n,)),
    )
    vm, hb = pl.BlockSpec(memory_space=pltpu.VMEM), pl.BlockSpec(memory_space=pl.ANY)
    return pl.pallas_call(
        functools.partial(step_kernel, wide, token_count, n_tok, n_task),
        out_shape=(
            jax.ShapeDtypeStruct((n_tok, LAT), f32),
            jax.ShapeDtypeStruct((3, 8, SENT + 16, 128), i16),
            jax.ShapeDtypeStruct((8, 80, YHALF), i16),
            jax.ShapeDtypeStruct((8, 48, BLK), i16),
            jax.ShapeDtypeStruct((256, 128), f32),
        ),
        in_specs=[hb, vm, vm, vm, hb, vm, vm, vm, vm, hb, hb, vm, vm, vm],
        out_specs=[hb] * 5,
        scratch_shapes=scratch,
        compiler_params=pltpu.CompilerParams(
            collective_id=0, has_side_effects=True, vmem_limit_bytes=64 * 2**20),
    )(lat, actT, ids, steps, tgt, rb, rf, vb, vf, fw, dw, hw, tab, vec)


def adam(master, moment, second, gradient, rate):
    moment_new = moment_decay * moment + (1.0 - moment_decay) * gradient
    second_new = moment_decay * second + (1.0 - moment_decay) * gradient * gradient
    correct = 1.0 - moment_decay**STEP
    normed = moment_new / correct / (jnp.sqrt(second_new / correct) + adam_eps)
    return master - rate * (normed + weight_decay * master), moment_new, second_new


def adam_kernel(n_task, lg, qf, qy, qh, misc, *refs):
    arrays, refs = refs[:15], refs[15:]
    outs, (lg_out, fi, fo, di, do, hi, ho, sf, sy, sh, sl, gh, vr, sem) = refs[:15], refs[15:]
    first, dyn, heads, table, vecs = (arrays[3 * k : 3 * k + 3] for k in range(5))
    first_out, dyn_out, heads_out, table_out, vecs_out = (outs[3 * k : 3 * k + 3] for k in range(5))
    z = lax.axis_index("narrow")

    def part(i):
        return pl.ds(pl.multiple_of(HALF * i, HALF), HALF)

    def load_first(k, i):
        return pltpu.make_async_copy(first[k], fi.at[k], sem.at[k, 0])

    def save_first(k, i):
        return pltpu.make_async_copy(fo.at[k, :, part(i)], first_out[k].at[:, part(i)], sem.at[3 + k, i])

    whole = [pltpu.make_async_copy(*c, sem.at[6, i]) for i, c in enumerate(((qf, sf), (qy, sy), (qh, sh), (lg, sl)))]
    others = [
        pltpu.make_async_copy(src[k], dst.at[k], sem.at[7 + j, k])
        for j, (src, dst) in enumerate(((dyn, di), (heads, hi))) for k in range(3)
    ]
    saves = [
        pltpu.make_async_copy(src.at[k], dst[k], sem.at[7 + j, 3 + k])
        for j, (dst, src) in enumerate(((dyn_out, do), (heads_out, ho))) for k in range(3)
    ]
    whole[0].start()
    for k in range(3):
        load_first(k, 0).start()
    whole[1].start()
    whole[2].start()
    for c in others:
        c.start()
    whole[3].start()
    whole[0].wait()
    for k in range(3):
        load_first(k, 0).wait()

    def first_part(i, c):
        for j in range(4):
            cols = pl.ds(pl.multiple_of(HALF * i + 128 * j, 128), 128)
            g = decode(sf.at[lax.div(i, 2), 4 * lax.rem(i, 2) + j])[0:SHARD, :]
            new = adam(fi[0, :, cols], fi[1, :, cols], fi[2, :, cols], g, matrix_rate)
            for k in range(3):
                fo[k, :, cols] = new[k]
        for k in range(3):
            save_first(k, i).start()
        return c
    lax.fori_loop(0, 2, first_part, 0)

    whole[1].wait()
    for c in others[0:3]:
        c.wait()

    def dyn_part(i, c):
        cols = pl.ds(pl.multiple_of(YHALF * lax.div(i, 4), 128), YHALF)
        rows = pl.ds(pl.multiple_of(64 * lax.rem(i, 4), 64), 64)
        new = adam(di[0, rows, cols], di[1, rows, cols], di[2, rows, cols], decode(sy.at[i]), matrix_rate)
        for k in range(3):
            do[k, rows, cols] = new[k]
        return c
    lax.fori_loop(0, 8, dyn_part, 0)
    for c in saves[0:3]:
        c.start()

    whole[2].wait()
    for c in others[3:6]:
        c.wait()
    for k in range(2):
        for j in range(4):
            gh[32 * j : 32 * j + 32, :] = decode(sh.at[4 * k + j])
        new = adam(hi[0, :, k, :], hi[1, :, k, :], hi[2, :, k, :], gh[0:BINS, :], matrix_rate)
        for i in range(3):
            ho[i, :, k, :] = new[i]
    for c in saves[3:6]:
        c.start()
    whole[3].wait()
    lg_save = pltpu.make_async_copy(sl, lg_out, sem.at[6, 4])
    lg_save.start()
    lax.fori_loop(2, 6, first_part, 0)

    g = misc[pl.ds(pl.multiple_of(128 + 32 * z, 32), 32), :]
    new = adam(*(r[...] for r in table), g[0:n_task, 0:TEMB], vector_rate)
    for k in range(3):
        table_out[k][...] = new[k]

    n_vec = vecs[0].shape[0]
    full = n_vec // 128
    left = n_vec - 128 * full
    g = sum(jnp.where(z == q, misc[at : at + 25, :], 0.0) for q, at in enumerate((0, 22, 45, 67)))
    turned = pltpu.roll(g, 64, 1)
    g = jnp.where(lax.rem(z, 2) == 1, jnp.where(lanes(128) < 64, turned[0:24, :], turned[1:25, :]), g[0:24, :])
    vr[...] = jnp.zeros_like(vr)
    for k in range(3):
        for r in range(full):
            vr[k, r : r + 1, :] = vecs[k][pl.ds(128 * r, 128)].reshape(1, 128)
        vr[k, full : full + 1, 0:left] = vecs[k][pl.ds(128 * full, left)].reshape(1, left)
    new = adam(vr[0], vr[1], vr[2], g, vector_rate)
    for k in range(3):
        for r in range(full):
            vecs_out[k][pl.ds(128 * r, 128)] = new[k][r : r + 1, :].reshape(128)
        vecs_out[k][pl.ds(128 * full, left)] = new[k][full : full + 1, 0:left].reshape(left)

    def first_saved(i, c):
        for k in range(3):
            save_first(k, i).wait()
        return c
    lax.fori_loop(0, 6, first_saved, 0)
    for c in saves:
        c.wait()
    lg_save.wait()


def adam_call(lg, qf, qy, qh, misc, arrays):
    V = pltpu.VMEM
    vm, hb = pl.BlockSpec(memory_space=pltpu.VMEM), pl.BlockSpec(memory_space=pl.ANY)
    first, dyn, heads = (arrays[k].shape for k in (0, 3, 6))
    out = [jax.ShapeDtypeStruct(a.shape, f32) for a in arrays] + [jax.ShapeDtypeStruct(lg.shape, f32)]
    return pl.pallas_call(
        functools.partial(adam_kernel, arrays[9].shape[0]),
        out_shape=out,
        in_specs=[hb] * 4 + [vm] + [hb] * 9 + [vm] * 6,
        out_specs=[hb] * 9 + [vm] * 6 + [hb],
        scratch_shapes=[
            V((3, *first), f32), V((3, *first), f32), V((3, *dyn), f32), V((3, *dyn), f32),
            V((3, *heads), f32), V((3, *heads), f32),
            V(qf.shape, i16), V(qy.shape, i16), V(qh.shape, i16), V(lg.shape, f32), V((128, BLK), f32), V((3, 24, 128), f32),
            pltpu.SemaphoreType.DMA((9, 6)),
        ],
        compiler_params=pltpu.CompilerParams(vmem_limit_bytes=64 * 2**20),
    )(lg, qf, qy, qh, misc, *arrays)


def per_device(
    latents, actions, task_ids, steps_left, target_latents, reward_bins, reward_frac, value_bins, value_frac,
    first_weight, first_moment, first_second, dynamics_weight, dynamics_moment, dynamics_second,
    heads_weight, heads_moment, heads_second, task_table, table_moment, table_second,
    vector_params, vector_moment, vector_second,
):
    n_tok = latents.shape[0]
    wide = lax.axis_size("wide")
    token_count = float(HORIZON * n_tok * wide * lax.axis_size("narrow"))
    n_task = task_table.shape[0]
    to_class = lambda a: a.transpose(2, 0, 1)
    lg, qf, qy, qh, misc = step_call(
        wide, token_count, n_task, latents, actions.transpose(1, 2, 0), task_ids,
        steps_left, target_latents.transpose(1, 0, 2),
        reward_bins.T, reward_frac.T, value_bins.T, value_frac.T,
        first_weight, dynamics_weight, to_class(heads_weight), task_table, vector_params)
    heads = [to_class(a) for a in (heads_weight, heads_moment, heads_second)]
    new = adam_call(lg, qf, qy, qh, misc, [
        first_weight, first_moment, first_second, dynamics_weight, dynamics_moment, dynamics_second, *heads,
        task_table, table_moment, table_second, vector_params, vector_moment, vector_second])
    return (new[15], *new[0:6], *(a.transpose(1, 2, 0) for a in new[6:9]), *new[9:15])


def solution(mesh):
    tokens = ("wide", "narrow")
    in_specs = (
        P(tokens, None), P(tokens, None, None), P(tokens), P(tokens), P(tokens, None, None),
        P(tokens, None), P(tokens, None), P(tokens, None), P(tokens, None),
        *(P("narrow", None),) * 6, *(P(None, "narrow", None),) * 3, *(P("narrow", None),) * 3, *(P("narrow"),) * 3,
    )
    out_specs = (
        P(tokens, None), *(P("narrow", None),) * 6, *(P(None, "narrow", None),) * 3,
        *(P("narrow", None),) * 3, *(P("narrow"),) * 3,
    )
    return jax.shard_map(per_device, mesh=mesh, in_specs=in_specs, out_specs=out_specs, check_vma=False)
```

```python
import functools

import jax
import jax.numpy as jnp
from jax import lax
from jax.experimental import pallas as pl
from jax.experimental.pallas import tpu as pltpu
from jax.sharding import PartitionSpec as P

f32, bf16, i16, i32 = jnp.float32, jnp.bfloat16, jnp.int16, jnp.int32
MESH = pl.DeviceIdType.MESH

LAT = 768
HID = 1024
BINS = 101
TEMB = 96
ACTN = 8
HORIZON = 3
STEP = 5
NZ = 4
SHARD = 218
SENT = 224
BLK = 256
ROWS = 320
RB = 320
NB = ROWS // RB
ALL = HORIZON * ROWS
HALF = HID // 2
YHALF = LAT // 2
TASK_LANE = LAT + ACTN - 3 * SHARD
ACT_LANE = LAT - 3 * SHARD

norm_eps = 1e-05
adam_eps = 1e-08
moment_decay = 0.5
horizon_decay = 0.5
weight_decay = 0.01
matrix_rate = 0.03
vector_rate = 0.3
consistency_coef = 20.0
head_coef = 0.1

NN = (((1,), (0,)), ((), ()))
NT = (((1,), (1,)), ((), ()))
TN = (((0,), (0,)), ((), ()))


def dot(a, b, dims=NN):
    return lax.dot_general(a, b, dims, preferred_element_type=f32)


def loop(start, end, body, carry):
    for i in range(start, end):
        carry = body(i, carry)
    return carry


def whole_of(start, unit):
    return start if isinstance(start, int) else pl.multiple_of(start, unit)


def lanes(n):
    return lax.broadcasted_iota(i32, (1, n), 1)


def block_rows(i, base=0):
    return pl.ds(whole_of(base + i * RB, RB), RB)


def encode(v, ref):
    rows = v.shape[0]
    top = jnp.max(jnp.abs(v), 0, keepdims=True)
    e = jnp.clip(jnp.ceil(jnp.log2(jnp.maximum(top, 1e-37))), -100.0, 120.0)
    ref[0:rows, :] = jnp.round(v * jnp.exp2(14.9 - e)).astype(i32).astype(i16)
    ref[rows : rows + 16, :] = jnp.broadcast_to(e, (16, v.shape[1])).astype(i32).astype(i16)


def decode(ref):
    rows = ref.shape[0] - 16
    e = ref[rows : rows + 16, :].astype(i32).astype(f32)[0:1, :]
    return ref[0:rows, :].astype(i32).astype(f32) * jnp.exp2(e - 14.9)


def pack_tiles(x):
    inside = lanes(BLK) < SHARD
    b0 = jnp.where(inside, x[:, 0:256], 0.0)
    b1 = jnp.where(inside, pltpu.roll(x[:, 128:512], 384 - 90, 1)[:, 0:256], 0.0)
    b2 = jnp.where(inside, pltpu.roll(x[:, 384:768], 384 - 52, 1)[:, 0:256], 0.0)
    b3 = jnp.where(lanes(128) < ACT_LANE, pltpu.roll(x[:, 640:768], 128 - 14, 1), 0.0)
    return b0, b1, b2, b3


def unpack_tiles(g):
    inside = lanes(BLK) < SHARD
    empty = jnp.zeros((g.shape[0], 128), f32)
    b0 = jnp.where(inside, g[:, 0:256], 0.0)
    b1 = pltpu.roll(jnp.concatenate([jnp.where(inside, g[:, 256:512], 0.0), empty], 1), 90, 1)
    b2 = pltpu.roll(jnp.concatenate([jnp.where(inside, g[:, 512:768], 0.0), empty], 1), 52, 1)
    b3 = pltpu.roll(jnp.where(lanes(128) < ACT_LANE, g[:, 768:896], 0.0), 14, 1)
    return jnp.concatenate(
        [
            b0[:, 0:128],
            b0[:, 128:256] + b1[:, 0:128],
            b1[:, 128:256],
            b1[:, 256:384] + b2[:, 0:128],
            b2[:, 128:256],
            b2[:, 256:384] + b3,
        ],
        1,
    )


def group_sums(x, ones):
    parts = []
    for j in range(0, x.shape[1], 256):
        v = x[:, j : j + 256]
        high = v.astype(bf16)
        low = (v - high.astype(f32)).astype(bf16)
        parts.append(dot(high, ones) + dot(low, ones))
    return jnp.concatenate(parts, 1)


def mish_parts(n):
    u = jnp.exp(jnp.minimum(n, 40.0))
    q = u * (u + 2.0)
    r = 1.0 / (q + 2.0)
    bent = q * r
    return bent, bent + (4.0 * n) * (u * (u + 1.0)) * (r * r)


def add_columns(acc, values):
    for k, v in enumerate(values):
        total = acc[8 * k : 8 * k + 8, :]
        for j in range(v.shape[0] // 8):
            total = total + v[8 * j : 8 * j + 8, :]
        acc[8 * k : 8 * k + 8, :] = total


def rcopy(src, dst, send_sem, recv_sem, device):
    return pltpu.make_async_remote_copy(
        src_ref=src, dst_ref=dst, send_sem=send_sem, recv_sem=recv_sem, device_id=device, device_id_type=MESH
    )


def step_kernel(wide, token_count, n_tok, n_task, lat, actT, ids, steps, tgt, rb, rf, vb, vf, fw, dw, hw, tab, vec,
                lg, qf, qy, qh, misc, **s):
    ups_n = wide.bit_length() - 4
    w, z = lax.axis_index("wide"), lax.axis_index("narrow")
    b0, b1, b2 = lax.rem(w, 2), lax.rem(lax.div(w, 2), 2), lax.rem(lax.div(w, 4), 2)
    pc, p1, p2 = (w + 1 - 2 * b0, z), (w + 2 - 4 * b1, z), (w + 4 - 8 * b2, z)
    p12 = (w + 6 - 4 * b1 - 8 * b2, z)
    zs = [(w, lax.rem(z + d, NZ)) for d in range(NZ)]
    from_z = [lax.rem(z + NZ - d, NZ) for d in range(NZ)]
    ups = []
    for u in range(ups_n):
        bit = 8 << u
        ups.append((w + bit - 2 * bit * lax.rem(lax.div(w, bit), 2), z))
    me = b0 * 4 + b1 * 2 + b2
    own = b1 * 2 + b2
    me_1, me_2, me_12 = me + 2 - 4 * b1, me + 1 - 2 * b2, 4 * b0 + 3 - own
    mine_of_8 = 4 * b0
    sends = []

    def pick(odd, even_value, odd_value):
        return even_value + odd * (odd_value - even_value)

    def launch(make):
        make().start()
        sends.append(make)

    X, XT, XTp, U, AT, ATp, DU = s["X"], s["XT"], s["XTp"], s["U"], s["AT"], s["ATp"], s["DU"]
    WF, WD, HT, SM, VEC = s["WF"], s["WD"], s["HT"], s["SM"], s["VEC"]
    PRE, PRE2, ACT, TT = s["PRE"], s["PRE2"], s["ACT"], s["TT"]
    TU, TS = TT.at[pl.ds(0, ROWS)], TT.at[pl.ds(ROWS, ROWS)]
    GP, GPp, GDL, GDLp = s["GP"], s["GPp"], s["GDL"], s["GDLp"]
    INV, SIDE, ONES, VA, VT, GEMB = (
        s["INV"], s["SIDE"], s["ONES"], s["VA"], s["VT"], s["GEMB"])

    barrier = pltpu.get_barrier_semaphore()
    peers = [pc, p1, p2, p12] + zs[1:] + ups
    for p in peers:
        pl.semaphore_signal(barrier, inc=1, device_id=p, device_id_type=MESH)

    STG = s["STG"]
    loads = []

    def load_first(part):
        return pltpu.make_async_copy(
            fw.at[:, pl.ds(HALF * part, HALF)], STG.at[part % 2], s["ls"].at[part % 2])

    loads.append(pltpu.make_async_copy(dw, DU.at[pl.ds(0, BLK)], s["ls"].at[3]))
    loads.append(pltpu.make_async_copy(lat, GDL.at[pl.ds(0, n_tok)], s["ls"].at[4]))
    load_first(0).start()
    load_first(1).start()
    for c in loads:
        c.start()

    def cast_first(br):
        for part in (2 * br, 2 * br + 1):
            load_first(part).wait()
            rows = jnp.concatenate([STG[part % 2].astype(bf16), jnp.zeros((SENT - SHARD, HALF), bf16)], 0)
            WF[pl.ds(whole_of(BLK * z, BLK), SENT), HALF * part : HALF * part + HALF] = rows
            if part < 4:
                load_first(part + 2).start()

    cast_first(0)
    pl.semaphore_wait(barrier, len(peers))

    gs, gr = s["gs"], s["gr"]

    class Item:
        def __init__(self, index, view):
            self.i, self.view = index, view

        def _copy(self, d, kind, piece, device):
            view = self.view(*piece)
            return rcopy(view, view, gs.at[self.i, d - 1, kind], gr.at[self.i, d - 1, kind], device)

        def _recv(self, d, kind, *piece):
            self._copy(d, kind, piece, pc).wait_recv()

        def _send(self, d, kind, device, *piece):
            launch(lambda: self._copy(d, kind, piece, device))

        def start(self):
            for d in (1, 3, 2):
                self._send(d, 0, zs[d], z, me, 1)

        def spread(self, *ds):
            for d in ds or (1, 3, 2):
                self._recv(d, 0, from_z[d], me, 1)
                self._send(d, 1, p1, from_z[d], me, 1)
                self._send(d, 2, p2, from_z[d], me, 1)
                self._send(d, 3, p12, from_z[d], me, 1)

        def cross(self, *ds):
            for d in ds or (1, 3, 2):
                q = from_z[d]
                self._recv(d, 1, q, me_1, 1)
                self._recv(d, 2, q, me_2, 1)
                self._recv(d, 3, q, me_12, 1)
                self._send(d, 5, pc, q, mine_of_8, 4)

        def finish(self):
            for d in (1, 3, 2):
                self._recv(d, 5, from_z[d], 4 - 4 * b0, 4)

    def first_view(br):
        def view(q, at, n):
            return WF.at[pl.ds(whole_of(BLK * q, BLK), SENT), pl.ds(whole_of(HID * br + 128 * at, 128), 128 * n)]
        return view

    def dyn_view(q, at, n):
        return WD.at[pl.ds(whole_of(BLK * q + 32 * at, 32), 32 * n)]

    def heads_view(q, at, n):
        cols = pl.ds(whole_of(BLK * q, BLK), BLK)
        rows = pl.ds(whole_of(16 * at, 16), 16 * n)
        return HT.at[:, rows, cols]

    gD, gY, gR, gV, gH = (
        Item(0, first_view(0)), Item(1, dyn_view), Item(2, first_view(1)), Item(3, first_view(2)), Item(4, heads_view))

    def vec_rows():
        n_vec = vec.shape[0]
        whole = n_vec // 128
        VR = s["VR"]
        VR[...] = jnp.zeros_like(VR)
        for r in range(whole):
            VR[r + 1 : r + 2, :] = vec[pl.ds(128 * r, 128)].reshape(1, 128)
        left = n_vec - 128 * whole
        VR[whole + 1 : whole + 2, 0:left] = vec[pl.ds(128 * whole, left)].reshape(1, left)
        plain = VR[1:33, :]
        moved = jnp.where(lanes(128) < 64, pltpu.roll(VR[0:32, :], 64, 1), pltpu.roll(plain, 64, 1))
        return jnp.where(lax.rem(z, 2) == 1, moved, plain).astype(bf16)

    gD.start()
    frame = vec_rows()
    SM[z, 0:32, :] = frame
    SM[z, 32:64, :] = jnp.zeros((32, 128), bf16)
    SM[z, 32 : 32 + n_task, 0:TEMB] = tab[...].astype(bf16)
    for d in (1, 3, 2):
        launch(lambda d=d: rcopy(SM.at[z], SM.at[z], s["ms"].at[d], s["mr"].at[d], zs[d]))
    loads[0].wait()
    WD[pl.ds(whole_of(BLK * z, BLK), BLK), :] = DU[0:BLK, :].astype(bf16)
    gY.start()
    cast_first(1)
    gD.spread(1, 3)
    own_cols = pl.ds(whole_of(BLK * z, BLK), BLK)
    for k in range(2):
        PRE[0:128, 0:BLK] = jnp.zeros((128, BLK), f32)
        PRE[0:BINS, 0:BLK] = hw[:, k, :]
        HT[k, :, own_cols] = PRE[0:128, 0:BLK].astype(bf16)
    gD.spread(2)
    gR.start()
    gH.start()
    cast_first(2)

    GDL[n_tok:ROWS, :] = jnp.zeros((ROWS - n_tok, LAT), bf16)
    for q in range(NZ):
        WF[BLK * q + SENT : BLK * q + BLK, :] = jnp.zeros((BLK - SENT, 3 * HID), bf16)
    loads[1].wait()

    idr = s["IDR"]
    idr[...] = jnp.full_like(idr, -1)
    idr[0:1, 0:n_tok] = ids[...].reshape(1, n_tok)
    slot = lax.broadcasted_iota(i32, (128, 1), 0)
    task = jnp.where(slot % 32 < n_task, n_task * (slot // 32) + slot % 32, -2)
    PKT = s["PKT"]
    PKT[...] = jnp.where(idr[0:1, 0:ROWS] == task, 1.0, 0.0).astype(bf16)
    gD.cross()
    gV.start()

    for d in (1, 3, 2):
        q = from_z[d]
        rcopy(SM.at[q], SM.at[q], s["ms"].at[d], s["mr"].at[d], pc).wait_recv()
    full = s["VFULL"]
    full[...] = jnp.zeros_like(full)
    for q, at in enumerate((0, 22, 45, 67)):
        full[at : at + 24, :] = full[at : at + 24, :] + SM[q, 0:32, :].astype(f32)[0:24, :]
    for r in range(12):
        n, first = (8, 8 * r) if r < 9 else (6, 72 + 6 * (r - 9))
        for j in range(n):
            VEC[r : r + 1, 128 * j : 128 * j + 128] = full[first + j : first + j + 1, :]
    place = jnp.concatenate([SM[q, 32:64, :] for q in range(NZ)], 0).astype(f32)
    table = pltpu.roll(jnp.concatenate([place, jnp.zeros_like(place)], 1), TASK_LANE, 1).astype(bf16)
    AC = s["AC"]
    AC[...] = jnp.zeros_like(AC)
    act_to = jnp.where(
        lax.broadcasted_iota(i32, (16, BLK), 0) + ACT_LANE == lax.broadcasted_iota(i32, (16, BLK), 1), 1.0, 0.0
    ).astype(bf16)
    rows_of_task = dot(PKT[...], table, TN)
    gY.spread()
    for t in range(3):
        AC[0:ACTN, 0:n_tok] = actT[t].astype(f32)
        X[ROWS * t : ROWS * t + ROWS, 768:1024] = (rows_of_task + dot(AC[:, 0:ROWS].astype(bf16), act_to, TN)).astype(bf16)

    def later_setup():
        tile = lax.broadcasted_iota(i32, (256, 256), 0) // 8 == lax.broadcasted_iota(i32, (256, 256), 1) // 8
        ONES[...] = jnp.where(tile, 1.0, 0.0).astype(bf16)
        st = s["ST"]
        st[...] = jnp.zeros_like(st)
        st[0:1, 0:n_tok] = steps[...].reshape(1, n_tok).astype(f32)
        for t in range(3):
            for k, ref in enumerate((rb, rf, vb, vf)):
                st[k + 1 : k + 2, 0:n_tok] = ref[t : t + 1, :].astype(f32)
            SIDE[t] = st[...].T[0:ROWS, :]
        for ref in (VA, VT, GEMB, s["DWH"], s["MS"]):
            ref[...] = jnp.zeros_like(ref)

    def put_latents(rows, values):
        b0, b1, b2, b3 = pack_tiles(values)
        X[rows, 0:768] = jnp.concatenate((b0, b1, b2), 1).astype(bf16)
        X[rows, 768:896] = (X[rows, 768:896].astype(f32) + b3).astype(bf16)

    put_latents(block_rows(0), GDL[0:ROWS, :].astype(f32))
    gD.finish()

    def matmul(out, orows, n, width, left, right, dims=NN):
        def tile_step(j, c):
            cols = pl.ds(j * width, width)
            out[orows, cols] = dot(left, right(cols), dims)
            return c
        loop(0, n // width, tile_step, 0)

    def first_forward(br, base, pre):
        def tile_step(j, c):
            cols = pl.ds(j * 512, 512)
            from_cols = pl.ds(whole_of(HID * br + j * 512, 512), 512)
            pre[:, cols] = dot(X[pl.ds(base, ROWS), :], WF[:, from_cols])
            return c
        loop(0, 2, tile_step, 0)

    def norm_mish(br, pre, unit, inv, unit_base, slope):
        bias, gain, shift = (VEC[pl.ds(3 * br + k, 1), :] for k in range(3))

        def step(i, c):
            rows = block_rows(i)
            p = pre[rows, :] + bias
            ce = p - jnp.mean(p, -1, keepdims=True)
            iv = lax.rsqrt(jnp.mean(ce * ce, -1, keepdims=True) + norm_eps)
            un = ce * iv
            n = un * gain + shift
            bent, sl = mish_parts(n)
            ACT[rows, :] = (n * bent).astype(bf16)
            if slope is not None:
                slope[rows, :] = sl
            unit[block_rows(i, unit_base), :] = un
            inv[block_rows(i, unit_base), :] = jnp.broadcast_to(iv, (RB, 128))
            return c
        loop(0, NB, step, 0)

    def dyn_forward(t, c):
        base = whole_of(ROWS * t, RB)
        first_forward(0, base, PRE)

        norm_mish(0, PRE, U, INV, base, None)

        @pl.when(t == 0)
        def _():
            gY.cross()
            gR.spread()
            later_setup()
            gY.finish()

        @pl.when(t == 2)
        def _():
            gH.cross()
        matmul(TU, pl.ds(0, ROWS), LAT, 384, ACT[...], lambda cols: WD[:, cols])
        for k in range(3):
            @pl.when(t == k)
            def _():
                AT[:, ROWS * k : ROWS * k + ROWS] = ACT[...].T
        bias, gain, shift = (VEC[9 + k : 10 + k, 0:LAT] for k in range(3))

        def step(i, c):
            rows, at = block_rows(i), block_rows(i, base)
            p = TU[rows, 0:LAT] + bias
            ce = p - jnp.mean(p, -1, keepdims=True)
            iv = lax.rsqrt(jnp.mean(ce * ce, -1, keepdims=True) + norm_eps)
            un = ce * iv
            DU[at, :] = un
            INV[at, 64:128] = jnp.broadcast_to(iv, (RB, 64))

            @pl.when(t < 2)
            def _():
                e = jnp.exp(un * gain + shift)
                put_latents(block_rows(i, base + ROWS), e / group_sums(e, ONES[...]))
            return c
        loop(0, NB, step, 0)

        @pl.when(t == 0)
        def _():
            gH.spread()

        @pl.when(t == 1)
        def _():
            gR.cross()
            gV.spread()
        return c

    lax.fori_loop(0, 3, dyn_forward, 0)
    XT[...] = X[...].T
    xs, xr = s["xs"], s["xr"]
    launch(lambda: rcopy(XT, XTp, xs.at[0], xr.at[0], pc))
    launch(lambda: rcopy(AT, ATp, xs.at[1], xr.at[1], pc))
    gR.finish()
    gH.finish()

    def norm_backward(br, pre, unit, inv, unit_base, slope, out_base):
        gain, shift = VEC[pl.ds(3 * br + 1, 1), :], VEC[pl.ds(3 * br + 2, 1), :]
        acc = VA.at[br]

        def step(i, c):
            rows, at = block_rows(i), block_rows(i, unit_base)
            un = unit[at, :]
            sl = mish_parts(un * gain + shift)[1] if slope is None else slope[rows, :]
            gn = pre[rows, :] * sl
            h = gn * gain
            gp = (h - jnp.mean(h, -1, keepdims=True) - un * jnp.mean(h * un, -1, keepdims=True)) * inv[at, 0:1]
            GP[block_rows(i, out_base), pl.ds(whole_of(HID * br, HID), HID)] = gp.astype(bf16)
            add_columns(acc, (gp, gn * un, gn))
            return c
        loop(0, NB, step, 0)

    def head_step(k, t, pre, following):
        base = whole_of(ROWS * t, RB)
        norm_mish(1 + k, pre, TU, s["HINV"], 0, TS)
        following()
        logits = dot(ACT[...], HT[k], NT)
        real = lanes(128) < BINS
        logits = jnp.where(real, logits, -1e30)
        e = jnp.exp(logits - jnp.max(logits, -1, keepdims=True))
        soft = e / jnp.sum(e, -1, keepdims=True)
        side = SIDE[t]
        at, frac = (jnp.where(k == 0, side[:, c : c + 1], side[:, c + 2 : c + 3]) for c in (1, 2))
        level = lanes(128).astype(f32)
        hot = jnp.where(level == at, 1.0 - frac, 0.0) + jnp.where(level == at + 1.0, frac, 0.0)
        decay = jnp.where(t == 0, 1.0, jnp.where(t == 1, horizon_decay, horizon_decay**2))
        weight = jnp.where(side[:, 0:1] > t.astype(f32), decay, 0.0) / token_count
        gl = jnp.where(real, weight * head_coef * (soft - hot), 0.0).astype(bf16)
        s["DWH"][k] = s["DWH"][k] + dot(gl.astype(f32).T.astype(bf16), ACT[...])
        pre[...] = dot(gl, HT[k])
        norm_backward(1 + k, pre, TU, s["HINV"], 0, TS, base)

    def heads_inputs(t):
        rows = pl.ds(whole_of(ROWS * t, RB), ROWS)
        for j in range(2):
            cols = pl.ds(512 * j, 512)
            PRE2[:, cols] = dot(GP[rows, HID : 3 * HID], WF[cols, HID : 3 * HID], NT)

    def y_rows(t):
        rows, cols = pl.ds(whole_of(ROWS * t, RB), ROWS), pl.ds(pl.multiple_of(YHALF * (1 - b0), 128), YHALF)
        return rcopy(GDL.at[rows, cols], GDLp.at[rows], xs.at[4 + t], xr.at[4 + t], pc)

    def d_rows(t):
        rows, cols = pl.ds(whole_of(ROWS * t, RB), ROWS), pl.ds(pl.multiple_of(HALF * (1 - b0), HALF), HALF)
        return rcopy(GP.at[rows, cols], GPp.at[0, rows], xs.at[7 + t], xr.at[7 + t], pc)

    def dyn_backward(t, between):
        base = whole_of(ROWS * t, RB)
        gain, shift = VEC[10:11, 0:LAT], VEC[11:12, 0:LAT]
        scale = 2.0 * consistency_coef / LAT

        def step(i, c):
            rows, at = block_rows(i), block_rows(i, base)
            un = DU[at, :]
            e = jnp.exp(un * gain + shift)
            sx = e / group_sums(e, ONES[...])
            decay = jnp.where(t == 0, 1.0, jnp.where(t == 1, horizon_decay, horizon_decay**2))
            weight = jnp.where(SIDE[0, rows, 0:1] > t.astype(f32), decay, 0.0) / token_count
            g = weight * scale * (sx - X[at, 0:LAT].astype(f32))
            g = g + jnp.where(t < 2, unpack_tiles(PRE[rows, 0:896]), 0.0)
            gn = sx * (g - group_sums(g * sx, ONES[...]))
            h = gn * gain
            gp = (h - jnp.mean(h, -1, keepdims=True) - un * jnp.mean(h * un, -1, keepdims=True)) * INV[at, 64:65]
            GDL[at, :] = gp.astype(bf16)
            add_columns(VT, (gp, gn * un, gn))
            return c
        loop(0, NB, step, 0)
        y_rows(t).start()
        between()

        def tile_step(j, c):
            cols = pl.ds(j * 512, 512)
            PRE[:, cols] = dot(GDL[pl.ds(base, ROWS), :], WD[cols, :], NT)
            return c
        loop(0, 2, tile_step, 0)
        norm_backward(0, PRE, U, INV, base, None, base)
        d_rows(t).start()

    def inputs_backward(t):
        base = whole_of(ROWS * t, RB)

        def tile_step(j, c):
            cols = pl.ds(j * 512, 512)
            PRE[:, cols] = dot(GP[pl.ds(base, ROWS), :], WF[cols, :], NT)
            return c
        loop(0, 2, tile_step, 0)
        GEMB[...] = GEMB[...] + PRE[:, 768:1024]

    rs_s, rs_r = s["ss"], s["sr"]

    class Stream:
        def __init__(self, index, grad, view, E, R, Q):
            self.i, self.grad, self.view, self.Q = index, grad, view, Q
            (self.E1, self.E2, self.E3), (self.R1, self.R2, self.R3) = E, R
            self.spent = []

        def _copy(self, at, src, dst, device):
            return rcopy(src, dst, rs_s.at[self.i, at], rs_r.at[self.i, at], device)

        def _recv(self, at, dst):
            self._copy(at, dst, dst, pc).wait_recv()

        def release(self):
            for first, span, ref in self.spent:
                if span is None:
                    self._copy(first, ref, ref, pc).wait_send()
                else:
                    def one(i, c):
                        self._copy(first + i, ref.at[i], ref.at[i], pc).wait_send()
                        return c
                    lax.fori_loop(*span, one, 0)
            self.spent = []

        def _send(self, at, src, dst, device):
            self._copy(at, src, dst, device).start()
            self.spent.append((at, None, src))

        def stage1(self, *span):
            span = span or (0, NZ)

            def one(i, c):
                q = lax.rem(z + 1 + i, NZ)
                odd = lax.rem(q, 2)
                base = pick(odd, 2 - 2 * b1, 1 - b2)
                for j in range(2):
                    encode(self.grad[self.view(q, base + j * (1 + odd))], self.E1.at[i, j])
                self._copy(i, self.E1.at[i], self.R1.at[i], (pick(odd, p1[0], p2[0]), z)).start()
                return c
            lax.fori_loop(*span, one, 0)
            self.spent.append((0, span, self.E1))

        def stage2(self, *span):
            span = span or (0, NZ)

            def one(i, c):
                q = lax.rem(z + 1 + i, NZ)
                odd = lax.rem(q, 2)
                self._recv(i, self.R1.at[i])
                keep = pick(odd, b2, b1)
                other = pick(odd, own + 1 - 2 * b2, own + 2 - 4 * b1)
                encode(self.grad[self.view(q, other)] + decode(self.R1.at[i, 1 - keep]), self.E2.at[i])
                self._copy(4 + i, self.E2.at[i], self.R2.at[i], (pick(odd, p2[0], p1[0]), z)).start()
                mine = self.view(q, own)
                self.grad[mine] = self.grad[mine] + decode(self.R1.at[i, keep])
                return c
            lax.fori_loop(*span, one, 0)
            self.spent.append((4, span, self.E2))

        def stage3(self):
            def one(i, c):
                q = lax.rem(z + 1 + i, NZ)
                self._recv(4 + i, self.R2.at[i])
                encode(self.grad[self.view(q, own)] + decode(self.R2.at[i]), self.E3.at[i])
                self._copy(8 + i, self.E3.at[i], self.R3.at[i], (w, q)).start()
                return c
            lax.fori_loop(0, 3, one, 0)
            self.spent.append((8, (0, 3), self.E3))

        def stage4(self):
            self._recv(7, self.R2.at[3])
            total = self.grad[self.view(z, own)] + decode(self.R2.at[3])
            for i in (0, 2, 1):
                self._recv(8 + i, self.R3.at[i])
                total = total + decode(self.R3.at[i])
            for u in range(ups_n):
                F, FR = self.Q.at[me], s["FR%d" % self.i]
                encode(total, F)
                c = self._copy(16 + u, F, FR.at[u], ups[u])
                c.start()
                self._recv(16 + u, FR.at[u])
                c.wait_send()
                total = decode(F) + decode(FR.at[u])
            encode(total, self.Q.at[me])
            self._send(11, self.Q.at[me], self.Q.at[me], p1)
            self._send(12, self.Q.at[me], self.Q.at[me], p2)
            self._send(13, self.Q.at[me], self.Q.at[me], p12)

        def stage6(self):
            self._recv(11, self.Q.at[me_1])
            self._recv(12, self.Q.at[me_2])
            self._recv(13, self.Q.at[me_12])
            mine = self.Q.at[pl.ds(mine_of_8, 4)]
            self._send(15, mine, mine, pc)

        def stage7(self, out, sem):
            self._recv(15, self.Q.at[pl.ds(4 - 4 * b0, 4)])
            c = pltpu.make_async_copy(self.Q, out, sem)
            c.start()
            return c

    def first_slice(q, at):
        return (pl.ds(whole_of(BLK * q, BLK), SENT), pl.ds(whole_of(128 * at, 128), 128))

    def value_slice(q, at):
        cols = HALF * lax.div(q, 2) + 128 * at
        return (pl.ds(whole_of(BLK * lax.rem(q, 2), BLK), SENT), pl.ds(whole_of(cols, 128), 128))

    def y_slice(q, at):
        return (pl.ds(whole_of(BLK * q + 64 * at, 64), 64), slice(None))

    def h_slice(q, at):
        return (b0, pl.ds(whole_of(32 * at, 32), 32), pl.ds(whole_of(BLK * q, BLK), BLK))

    EF = (s["E1"], s["E2"], s["E3"])
    streams = []
    for i, name in enumerate("DRV"):
        streams.append(Stream(
            i, *((TT, value_slice) if name == "V" else (s["DWA"], first_slice)), EF,
            tuple(s["R%d%s" % (k, name)] for k in (1, 2, 3)), s["QF"].at[i]))
    sD, sR, sV = streams
    sY = Stream(3, s["DWY"], y_slice, tuple(s["E%dY" % k] for k in (1, 2, 3)),
                tuple(s["R%dY" % k] for k in (1, 2, 3)), s["QY"])
    sH = Stream(4, s["DWH"], h_slice, tuple(s["E%dH" % k] for k in (1, 2, 3)),
                tuple(s["R%dH" % k] for k in (1, 2, 3)), s["QH"])

    def send_half(br):
        def make():
            cols = pl.ds(whole_of(HID * br + HALF * (1 - b0), HALF), HALF)
            return rcopy(GP.at[:, cols], GPp.at[br], xs.at[1 + br], xr.at[1 + br], pc)
        launch(make)

    def wait_x(at, dst):
        rcopy(dst, dst, xs.at[at], xr.at[at], pc).wait_recv()

    def weight_grad(out, n, left, right, arrived, left2, right2):
        def own_tile(j, c):
            cols = pl.ds(pl.multiple_of(j * n, n), n)
            out[:, cols] = dot(left[...], right(j))
            return c
        lax.fori_loop(0, out.shape[1] // n, own_tile, 0)
        arrived()

        def other_tile(j, c):
            cols = pl.ds(pl.multiple_of(j * n, n), n)
            out[:, cols] = out[:, cols] + dot(left2[...], right2(cols))
            return c
        lax.fori_loop(0, out.shape[1] // n, other_tile, 0)

    def first_grad(br, out, arrived):
        weight_grad(
            out, 256, XT,
            lambda j: GP[:, pl.ds(pl.multiple_of(HID * br + HALF * b0 + 256 * j, 256), 256)], arrived,
            XTp, lambda cols: GPp[br, :, cols])

    def value_grad():
        def tile_step(j, c):
            cols = pl.ds(whole_of(j * 256, 256), 256)
            low_cols = pl.ds(whole_of(HALF + j * 256, 256), 256)
            right = GP[:, pl.ds(whole_of(2 * HID + HALF * b0 + 256 * j, 256), 256)]
            total = dot(XT[...], right) + dot(XTp[...], GPp[2, :, cols])
            TT[0:512, cols] = total[0:512, :]
            TT[0:512, low_cols] = total[512:1024, :]
            return c
        lax.fori_loop(0, 2, tile_step, 0)

    def y_grad():
        def arrived():
            wait_x(1, ATp)
            for t in range(3):
                wait_x(4 + t, GDLp.at[pl.ds(ROWS * t, ROWS)])
        weight_grad(
            s["DWY"], 128, AT,
            lambda j: GDL[:, pl.ds(whole_of(YHALF * b0 + 128 * j, 128), 128)], arrived,
            ATp, lambda cols: GDLp[:, cols])
        sY.stage1()

    def head_forward(j, pre):
        first_forward(1 + lax.div(j, 3), whole_of(ROWS * lax.rem(j, 3), RB), pre)

    def head_steps(i, c):
        @pl.when(i == 1)
        def _():
            gV.finish()

        @pl.when(i == 2)
        def _():
            def arrived():
                wait_x(0, XTp)
                wait_x(2, GPp.at[1])
            first_grad(1, s["DWA"], arrived)
            sR.stage1()
        j = 2 * i
        head_step(lax.div(j, 3), lax.rem(j, 3), PRE, lambda: head_forward(j + 1, PRE2))

        @pl.when(i == 0)
        def _():
            gV.cross()

        @pl.when(i == 1)
        def _():
            send_half(1)
        head_step(lax.div(j + 1, 3), lax.rem(j + 1, 3), PRE2, lambda: head_forward(lax.min(j + 2, 5), PRE))
        return c
    first_forward(1, 0, PRE)
    lax.fori_loop(0, 3, head_steps, 0)
    send_half(2)
    launch(lambda: rcopy(s["DWH"].at[1 - b0], s["DWHp"], xs.at[10], xr.at[10], pc))
    for t in range(3):
        loads.append(pltpu.make_async_copy(
            tgt.at[t], X.at[pl.ds(ROWS * t, n_tok), pl.ds(0, LAT)], s["ls"].at[5 + t]))
        loads[-1].start()
    sR.stage2()
    for c in loads[2:]:
        c.wait()
    def backward(i, c):
        t = 2 - i

        def last_y():
            @pl.when(i == 2)
            def _():
                y_grad()
        dyn_backward(t, last_y)

        @pl.when(i == 0)
        def _():
            sR.stage3()
            wait_x(3, GPp.at[2])
            value_grad()
            sR.release()
            sV.stage1()
            wait_x(10, s["DWHp"])
            s["DWH"][b0] = s["DWH"][b0] + s["DWHp"][...]
            sH.stage1()

        @pl.when(i == 1)
        def _():
            sR.stage4()
            sV.stage2()
            sH.stage2()

        @pl.when(i == 2)
        def _():
            sV.stage3()
            sH.stage3()
            def arrived():
                for k in range(3):
                    wait_x(7 + k, GPp.at[0, pl.ds(ROWS * k, ROWS)])
            first_grad(0, s["DWA"], arrived)
            sV.release()
            sD.stage1()
            sR.stage6()
        inputs_backward(t)
        return c
    lax.fori_loop(0, 3, backward, 0)
    for k in range(3):
        sends.extend((lambda k=k: y_rows(k), lambda k=k: d_rows(k)))

    def write_latent(i, c):
        rows = block_rows(i)
        DU[rows, :] = unpack_tiles(PRE[rows, 0:896])
        return c
    loop(0, NB, write_latent, 0)
    lg_copy = pltpu.make_async_copy(DU.at[pl.ds(0, n_tok)], lg, s["ls"].at[8])
    lg_copy.start()
    ge = GEMB[...]
    g1 = ge.astype(bf16)
    g2 = (ge - g1.astype(f32)).astype(bf16)
    g3 = (ge - g1.astype(f32) - g2.astype(f32)).astype(bf16)
    pk = PKT[...]
    by_task = dot(pk, g1) + dot(pk, g2) + dot(pk, g3)
    M = s["MS"]
    M[128:256, :] = pltpu.roll(by_task, BLK - TASK_LANE, 1)[:, 0:128]
    for r in range(12):
        acc, n, first = (VA.at[r // 3], 8, 8 * r) if r < 9 else (VT, 6, 72 + 6 * (r - 9))
        k = r % 3
        row = jnp.sum(acc[8 * k : 8 * k + 8, :], 0, keepdims=True)
        for j in range(n):
            M[first + j : first + j + 1, :] = row[:, 128 * j : 128 * j + 128]

    vs, vr = s["vs"], s["vr"]

    def small(at, src, dst, device):
        return rcopy(src, dst, vs.at[at], vr.at[at], device)

    def rows_of(start, n):
        return pl.ds(whole_of(start, 32), n)

    halves = ((0, pc, b0, 128), (1, p1, b1, 64), (2, p2, b2, 32))

    def halve(step, start):
        at, device, bit, n = halves[step]
        launch(lambda: small(at, M.at[rows_of(start + n * (1 - bit), n)], s["MR%d" % step], device))

    def halved(step, start):
        at, device, bit, n = halves[step]
        small(at, s["MR%d" % step], s["MR%d" % step], device).wait_recv()
        mine = rows_of(start + n * bit, n)
        M[mine, :] = M[mine, :] + s["MR%d" % step][...]
        return start + n * bit

    halve(0, 0)
    sY.stage2()
    at = halved(0, 0)
    halve(1, at)
    sD.stage2(0, 2)
    sY.stage3()
    sD.stage2(2, 4)
    at = halved(1, at)
    halve(2, at)
    sV.stage4()
    sH.stage4()
    at = halved(2, at)
    MZ = s["MZ"]
    MZ[z] = M[rows_of(at, 32), :]
    for d in (2, 1, 3):
        launch(lambda d=d: small(2 + d, MZ.at[z], MZ.at[z], zs[d]))
    sD.stage3()
    sY.stage4()
    for d in (1, 3, 2):
        small(2 + d, MZ.at[from_z[d]], MZ.at[from_z[d]], pc).wait_recv()
    total = (MZ[0] + MZ[1]) + (MZ[2] + MZ[3])
    for u in range(ups_n):
        s["MF"][u] = total
        launch(lambda u=u: small(9 + u, s["MF"].at[u], s["MFR"].at[u], ups[u]))
        small(9 + u, s["MFR"].at[u], s["MFR"].at[u], ups[u]).wait_recv()
        total = total + s["MFR"][u]
    MO = s["MO"]
    MO[rows_of(at, 32), :] = total
    for n, device in ((6, p1), (7, p2), (9 + ups_n, p12)):
        launch(lambda at=at, n=n, device=device: small(n, MO.at[rows_of(at, 32)], MO.at[rows_of(at, 32)], device))
    sD.stage4()
    sV.stage6()
    sH.stage6()
    outs = [lg_copy]
    outs.append(sR.stage7(qf.at[1], s["ls"].at[9]))
    sY.stage6()
    for n, slot in ((6, me_1), (7, me_2), (9 + ups_n, me_12)):
        o = 32 * slot
        small(n, MO.at[rows_of(o, 32)], MO.at[rows_of(o, 32)], pc).wait_recv()
    at = 128 * b0
    launch(lambda at=at: small(8, MO.at[rows_of(at, 128)], MO.at[rows_of(at, 128)], pc))
    outs.append(sV.stage7(qf.at[2], s["ls"].at[10]))
    outs.append(sH.stage7(qh, s["ls"].at[11]))
    outs.append(sY.stage7(qy, s["ls"].at[12]))
    o = at + 128 - 256 * b0
    small(8, MO.at[rows_of(o, 128)], MO.at[rows_of(o, 128)], pc).wait_recv()
    c = pltpu.make_async_copy(MO, misc, s["ls"].at[13])
    c.start()
    outs.append(c)
    sD.stage6()
    outs.append(sD.stage7(qf.at[0], s["ls"].at[14]))
    for c in outs:
        c.wait()
    for st in (sD, sR, sV, sY, sH):
        st.release()
    for make in sends:
        make().wait_send()


def step_call(wide, token_count, n_task, lat, actT, ids, steps, tgt, rb, rf, vb, vf, fw, dw, hw, tab, vec):
    n_tok = lat.shape[0]
    ups_n = wide.bit_length() - 4
    V = pltpu.VMEM
    D = pltpu.SemaphoreType.DMA
    scratch = dict(
        WF=V((HID, 3 * HID), bf16), WD=V((HID, LAT), bf16), HT=V((2, 128, HID), bf16),
        SM=V((NZ, 64, 128), bf16), VR=V((40, 128), f32), VEC=V((16, HID), f32), VFULL=V((96, 128), f32),
        X=V((ALL, HID), bf16), XT=V((HID, ALL), bf16), XTp=V((HID, ALL), bf16),
        U=V((ALL, HID), f32), AT=V((HID, ALL), bf16), ATp=V((HID, ALL), bf16),
        DU=V((ALL, LAT), f32),
        PRE=V((ROWS, HID), f32), PRE2=V((ROWS, HID), f32), TT=V((2 * ROWS, HID), f32), ACT=V((ROWS, HID), bf16),
        GP=V((ALL, 3 * HID), bf16), GPp=V((3, ALL, HALF), bf16), GDL=V((ALL, LAT), bf16), GDLp=V((ALL, YHALF), bf16),
        INV=V((ALL, 128), f32), HINV=V((ROWS, 128), f32),
        SIDE=V((3, ROWS, 16), f32), ONES=V((256, 256), bf16),
        VA=V((3, 24, HID), f32), VT=V((24, LAT), f32), GEMB=V((ROWS, BLK), f32),
        ST=V((16, 384), f32), IDR=V((8, 384), i32), PKT=V((128, ROWS), bf16), AC=V((16, 384), f32),
        DWA=V((HID, HALF), f32), DWY=V((HID, YHALF), f32), STG=V((2, SHARD, HALF), f32),
        DWH=V((2, 128, HID), f32), DWHp=V((128, HID), f32),
        MS=V((256, 128), f32), MO=V((256, 128), f32), MZ=V((NZ, 32, 128), f32),
        MR0=V((128, 128), f32), MR1=V((64, 128), f32), MR2=V((32, 128), f32),
        QF=V((3, 8, SENT + 16, 128), i16), QY=V((8, 80, YHALF), i16), QH=V((8, 48, BLK), i16),
    )
    for name, rows, cols in (("", SENT + 16, 128), ("Y", 80, YHALF), ("H", 48, BLK)):
        scratch["E1" + name] = V((4, 2, rows, cols), i16)
        scratch["E2" + name] = V((4, rows, cols), i16)
        scratch["E3" + name] = V((3, rows, cols), i16)
    for name, rows, cols in (("D", SENT + 16, 128), ("R", SENT + 16, 128), ("V", SENT + 16, 128), ("Y", 80, YHALF), ("H", 48, BLK)):
        scratch["R1" + name] = V((4, 2, rows, cols), i16)
        scratch["R2" + name] = V((4, rows, cols), i16)
        scratch["R3" + name] = V((3, rows, cols), i16)
    if ups_n:
        for i, (rows, cols) in enumerate(((SENT + 16, 128),) * 3 + ((80, YHALF), (48, BLK))):
            scratch["FR%d" % i] = V((ups_n, rows, cols), i16)
        scratch["MF"] = V((ups_n, 32, 128), f32)
        scratch["MFR"] = V((ups_n, 32, 128), f32)
    scratch.update(
        ls=D((16,)), gs=D((5, 3, 6)), gr=D((5, 3, 6)), ms=D((4,)), mr=D((4,)),
        xs=D((11,)), xr=D((11,)), ss=D((5, 16 + ups_n)), sr=D((5, 16 + ups_n)), vs=D((10 + ups_n,)), vr=D((10 + ups_n,)),
    )
    vm, hb = pl.BlockSpec(memory_space=pltpu.VMEM), pl.BlockSpec(memory_space=pl.ANY)
    return pl.pallas_call(
        functools.partial(step_kernel, wide, token_count, n_tok, n_task),
        out_shape=(
            jax.ShapeDtypeStruct((n_tok, LAT), f32),
            jax.ShapeDtypeStruct((3, 8, SENT + 16, 128), i16),
            jax.ShapeDtypeStruct((8, 80, YHALF), i16),
            jax.ShapeDtypeStruct((8, 48, BLK), i16),
            jax.ShapeDtypeStruct((256, 128), f32),
        ),
        in_specs=[hb, vm, vm, vm, hb, vm, vm, vm, vm, hb, hb, vm, vm, vm],
        out_specs=[hb] * 5,
        scratch_shapes=scratch,
        compiler_params=pltpu.CompilerParams(
            collective_id=0, has_side_effects=True, vmem_limit_bytes=64 * 2**20),
    )(lat, actT, ids, steps, tgt, rb, rf, vb, vf, fw, dw, hw, tab, vec)


def adam(master, moment, second, gradient, rate):
    moment_new = moment_decay * moment + (1.0 - moment_decay) * gradient
    second_new = moment_decay * second + (1.0 - moment_decay) * gradient * gradient
    correct = 1.0 - moment_decay**STEP
    normed = moment_new / correct / (jnp.sqrt(second_new / correct) + adam_eps)
    return master - rate * (normed + weight_decay * master), moment_new, second_new


def adam_kernel(n_task, lg, qf, qy, qh, misc, *refs):
    arrays, refs = refs[:15], refs[15:]
    outs, (lg_out, fi, fo, di, do, hi, ho, sf, sy, sh, sl, gh, vr, sem) = refs[:15], refs[15:]
    first, dyn, heads, table, vecs = (arrays[3 * k : 3 * k + 3] for k in range(5))
    first_out, dyn_out, heads_out, table_out, vecs_out = (outs[3 * k : 3 * k + 3] for k in range(5))
    z = lax.axis_index("narrow")

    def part(i):
        return pl.ds(pl.multiple_of(HALF * i, HALF), HALF)

    def load_first(k, i):
        return pltpu.make_async_copy(first[k], fi.at[k], sem.at[k, 0])

    def save_first(k, i):
        return pltpu.make_async_copy(fo.at[k, :, part(i)], first_out[k].at[:, part(i)], sem.at[3 + k, i])

    whole = [pltpu.make_async_copy(*c, sem.at[6, i]) for i, c in enumerate(((qf, sf), (qy, sy), (qh, sh), (lg, sl)))]
    others = [
        pltpu.make_async_copy(src[k], dst.at[k], sem.at[7 + j, k])
        for j, (src, dst) in enumerate(((dyn, di), (heads, hi))) for k in range(3)
    ]
    saves = [
        pltpu.make_async_copy(src.at[k], dst[k], sem.at[7 + j, 3 + k])
        for j, (dst, src) in enumerate(((dyn_out, do), (heads_out, ho))) for k in range(3)
    ]
    whole[0].start()
    for k in range(3):
        load_first(k, 0).start()
    whole[1].start()
    whole[2].start()
    for c in others:
        c.start()
    whole[3].start()
    whole[0].wait()
    for k in range(3):
        load_first(k, 0).wait()

    def first_part(i, c):
        for j in range(4):
            cols = pl.ds(pl.multiple_of(HALF * i + 128 * j, 128), 128)
            g = decode(sf.at[lax.div(i, 2), 4 * lax.rem(i, 2) + j])[0:SHARD, :]
            new = adam(fi[0, :, cols], fi[1, :, cols], fi[2, :, cols], g, matrix_rate)
            for k in range(3):
                fo[k, :, cols] = new[k]
        for k in range(3):
            save_first(k, i).start()
        return c
    lax.fori_loop(0, 2, first_part, 0)

    whole[1].wait()
    for c in others[0:3]:
        c.wait()

    def dyn_part(i, c):
        cols = pl.ds(pl.multiple_of(YHALF * lax.div(i, 4), 128), YHALF)
        rows = pl.ds(pl.multiple_of(64 * lax.rem(i, 4), 64), 64)
        new = adam(di[0, rows, cols], di[1, rows, cols], di[2, rows, cols], decode(sy.at[i]), matrix_rate)
        for k in range(3):
            do[k, rows, cols] = new[k]
        return c
    lax.fori_loop(0, 8, dyn_part, 0)
    for c in saves[0:3]:
        c.start()

    whole[2].wait()
    for c in others[3:6]:
        c.wait()
    for k in range(2):
        for j in range(4):
            gh[32 * j : 32 * j + 32, :] = decode(sh.at[4 * k + j])
        new = adam(hi[0, :, k, :], hi[1, :, k, :], hi[2, :, k, :], gh[0:BINS, :], matrix_rate)
        for i in range(3):
            ho[i, :, k, :] = new[i]
    for c in saves[3:6]:
        c.start()
    whole[3].wait()
    lg_save = pltpu.make_async_copy(sl, lg_out, sem.at[6, 4])
    lg_save.start()
    lax.fori_loop(2, 6, first_part, 0)

    g = misc[pl.ds(pl.multiple_of(128 + 32 * z, 32), 32), :]
    new = adam(*(r[...] for r in table), g[0:n_task, 0:TEMB], vector_rate)
    for k in range(3):
        table_out[k][...] = new[k]

    n_vec = vecs[0].shape[0]
    full = n_vec // 128
    left = n_vec - 128 * full
    g = sum(jnp.where(z == q, misc[at : at + 25, :], 0.0) for q, at in enumerate((0, 22, 45, 67)))
    turned = pltpu.roll(g, 64, 1)
    g = jnp.where(lax.rem(z, 2) == 1, jnp.where(lanes(128) < 64, turned[0:24, :], turned[1:25, :]), g[0:24, :])
    vr[...] = jnp.zeros_like(vr)
    for k in range(3):
        for r in range(full):
            vr[k, r : r + 1, :] = vecs[k][pl.ds(128 * r, 128)].reshape(1, 128)
        vr[k, full : full + 1, 0:left] = vecs[k][pl.ds(128 * full, left)].reshape(1, left)
    new = adam(vr[0], vr[1], vr[2], g, vector_rate)
    for k in range(3):
        for r in range(full):
            vecs_out[k][pl.ds(128 * r, 128)] = new[k][r : r + 1, :].reshape(128)
        vecs_out[k][pl.ds(128 * full, left)] = new[k][full : full + 1, 0:left].reshape(left)

    def first_saved(i, c):
        for k in range(3):
            save_first(k, i).wait()
        return c
    lax.fori_loop(0, 6, first_saved, 0)
    for c in saves:
        c.wait()
    lg_save.wait()


def adam_call(lg, qf, qy, qh, misc, arrays):
    V = pltpu.VMEM
    vm, hb = pl.BlockSpec(memory_space=pltpu.VMEM), pl.BlockSpec(memory_space=pl.ANY)
    first, dyn, heads = (arrays[k].shape for k in (0, 3, 6))
    out = [jax.ShapeDtypeStruct(a.shape, f32) for a in arrays] + [jax.ShapeDtypeStruct(lg.shape, f32)]
    return pl.pallas_call(
        functools.partial(adam_kernel, arrays[9].shape[0]),
        out_shape=out,
        in_specs=[hb] * 4 + [vm] + [hb] * 9 + [vm] * 6,
        out_specs=[hb] * 9 + [vm] * 6 + [hb],
        scratch_shapes=[
            V((3, *first), f32), V((3, *first), f32), V((3, *dyn), f32), V((3, *dyn), f32),
            V((3, *heads), f32), V((3, *heads), f32),
            V(qf.shape, i16), V(qy.shape, i16), V(qh.shape, i16), V(lg.shape, f32), V((128, BLK), f32), V((3, 24, 128), f32),
            pltpu.SemaphoreType.DMA((9, 6)),
        ],
        compiler_params=pltpu.CompilerParams(vmem_limit_bytes=64 * 2**20),
    )(lg, qf, qy, qh, misc, *arrays)


def per_device(
    latents, actions, task_ids, steps_left, target_latents, reward_bins, reward_frac, value_bins, value_frac,
    first_weight, first_moment, first_second, dynamics_weight, dynamics_moment, dynamics_second,
    heads_weight, heads_moment, heads_second, task_table, table_moment, table_second,
    vector_params, vector_moment, vector_second,
):
    n_tok = latents.shape[0]
    wide = lax.axis_size("wide")
    token_count = float(HORIZON * n_tok * wide * lax.axis_size("narrow"))
    n_task = task_table.shape[0]
    to_class = lambda a: a.transpose(2, 0, 1)
    lg, qf, qy, qh, misc = step_call(
        wide, token_count, n_task, latents, actions.transpose(1, 2, 0), task_ids,
        steps_left, target_latents.transpose(1, 0, 2),
        reward_bins.T, reward_frac.T, value_bins.T, value_frac.T,
        first_weight, dynamics_weight, to_class(heads_weight), task_table, vector_params)
    heads = [to_class(a) for a in (heads_weight, heads_moment, heads_second)]
    new = adam_call(lg, qf, qy, qh, misc, [
        first_weight, first_moment, first_second, dynamics_weight, dynamics_moment, dynamics_second, *heads,
        task_table, table_moment, table_second, vector_params, vector_moment, vector_second])
    return (new[15], *new[0:6], *(a.transpose(1, 2, 0) for a in new[6:9]), *new[9:15])


def solution(mesh):
    tokens = ("wide", "narrow")
    in_specs = (
        P(tokens, None), P(tokens, None, None), P(tokens), P(tokens), P(tokens, None, None),
        P(tokens, None), P(tokens, None), P(tokens, None), P(tokens, None),
        *(P("narrow", None),) * 6, *(P(None, "narrow", None),) * 3, *(P("narrow", None),) * 3, *(P("narrow"),) * 3,
    )
    out_specs = (
        P(tokens, None), *(P("narrow", None),) * 6, *(P(None, "narrow", None),) * 3,
        *(P("narrow", None),) * 3, *(P("narrow"),) * 3,
    )
    return jax.shard_map(per_device, mesh=mesh, in_specs=in_specs, out_specs=out_specs, check_vma=False)
```
